128 devices in a mesh: lang: 8 (over y, core), pair: 16 (over x, z).
Axes of the slice: x: 4, y: 4, z: 4, core: 2. Of those that a mesh axis runs over, the one named last changes fastest.
Arguments:
- sentences: bfloat16 [512, 128, 1024], P(('lang', 'pair')), may hold values from -16 to 16
- cotangent: bfloat16 [512, 128, 1024], P(('lang', 'pair')), may hold values from -6 to 6
- w_query: bfloat16 [1024, 1024], replicated, may hold values from -0.1875 to 0.1875
- w_key: bfloat16 [1024, 1024], replicated, may hold values from -0.1875 to 0.1875
- w_value: bfloat16 [1024, 1024], replicated, may hold values from -0.1875 to 0.1875
- send_rows: int32 [128, 8, 1], P(('lang', 'pair')), may hold values from 0 to 3
- pair_src: int32 [128, 16], P(('lang', 'pair')), may hold values from 0 to 3
- pair_slot: int32 [128, 16], P(('lang', 'pair')), may hold values from 0 to 7
- pair_valid: int32 [128, 16], P(('lang', 'pair')), may hold values 0 or 1
Outputs:
- attended: bfloat16 [512, 128, 1024], P(('lang', 'pair'))
- grad_sentences: bfloat16 [512, 128, 1024], P(('lang', 'pair'))
- grad_wq: bfloat16 [1024, 1024], replicated
- grad_wk: bfloat16 [1024, 1024], replicated
- grad_wv: bfloat16 [1024, 1024], replicated
The draws below stay inside these ranges and needn't reach their ends.
All inputs are finite; a program needn't handle non-finite values. No bound on the sum of `pair_valid` on one device may be relied on, other than what follows from the above.
Results may differ from the reference program's by a relative error of at most 0.015.
The reference program's roundings to bfloat16 on the way (of `prob_b` and `dscore`) count: a program that leaves them out, or rounds other values in their place, can miss the bound.
Values may be sent and summed in bfloat16 or wider, within the bound.
No kernel may reach another device: no remote copies, remote signals or barrier semaphores. Data moves between devices by JAX's collectives and lax.ppermute only.
A program may use at most 128 MiB of HBM per device.

```python
import jax
import jax.numpy as jnp
from jax import lax

D = 1024
HEADS = 16
L = 128
SENT_DEV = 4
PAIRS_DEV = 16
CAP = 1
SENTENCES = 512
N_LANG = 8
DEVICES = 128


def draw_sentences(key, part):
    key = jax.random.fold_in(key, 7)
    base = jax.random.normal(key, (SENTENCES, L, D), jnp.float32)
    base = jnp.clip(base, -6.0, 6.0)
    return base.astype(jnp.bfloat16)


def with_ends(result, own_key, smallest, largest):
    spot = [jax.random.randint(jax.random.fold_in(own_key, axis), (), 0, length) for axis, length in enumerate(result.shape)]
    widest = result.shape.index(max(result.shape))
    beside = spot[:widest] + [(spot[widest] + 1) % result.shape[widest]] + spot[widest + 1:]
    return result.at[tuple(spot)].set(smallest).at[tuple(beside)].set(largest)


def block_scale(rng, dims, pieces, least, high):
    factor_of = 1.0
    for axis_at, blocks in pieces:
        heights = jax.random.uniform(jax.random.fold_in(jax.random.fold_in(rng, 6), axis_at), (blocks,), jnp.float32, least / len(pieces), high / len(pieces))
        factor_of = factor_of * jnp.repeat(jnp.exp(heights), dims[axis_at] // blocks).reshape((-1,) + (1,) * (len(dims) - 1 - axis_at))
    return factor_of


def noise(own_key, extent, scale, reach, cuts=(), held_as=jnp.bfloat16):
    level = block_scale(own_key, extent, cuts, -0.22, 0.18) if cuts else 1.0
    drawn = jax.random.normal(own_key, extent, jnp.float32) * scale * level
    return jnp.minimum(jnp.maximum(drawn, -reach), reach).astype(held_as)


def setup_inputs(seed: int = 0) -> dict:
    streams_of = jax.random.split(jax.random.key(seed), 10)
    return {
        "sentences": draw_sentences(jax.random.fold_in(streams_of[9], 71), 0),
        "cotangent": noise(streams_of[1], (SENTENCES, L, D), 1.0, 6.0, ((0, 128),)),
        "w_query": noise(streams_of[2], (D, D), D ** -0.5, 0.1875),
        "w_key": noise(streams_of[3], (D, D), D ** -0.5, 0.1875),
        "w_value": noise(streams_of[4], (D, D), D ** -0.5, 0.1875),
        "send_rows": with_ends(jax.random.randint(streams_of[5], (DEVICES, N_LANG, CAP), 0, SENT_DEV), jax.random.fold_in(streams_of[5], 1), 0, SENT_DEV - 1).astype(jnp.int32),
        "pair_src": with_ends(jax.random.randint(streams_of[6], (DEVICES, PAIRS_DEV), 0, SENT_DEV), jax.random.fold_in(streams_of[6], 1), 0, SENT_DEV - 1).astype(jnp.int32),
        "pair_slot": with_ends(jax.random.randint(streams_of[7], (DEVICES, PAIRS_DEV), 0, N_LANG * CAP), jax.random.fold_in(streams_of[7], 1), 0, (N_LANG * CAP) - 1).astype(jnp.int32),
        "pair_valid": with_ends((jax.random.randint(streams_of[8], (DEVICES, PAIRS_DEV), 0, 4) < 3).astype(jnp.int32), jax.random.fold_in(streams_of[8], 1), 0, 1),
    }


def attend_block(q_rows, k_rows, v_rows, g_rows, valid, heads):
    count, length, width = q_rows.shape
    size = width // heads
    scale = size ** -0.5
    qh = q_rows.reshape(count, length, heads, size).astype(jnp.float32)
    kh = k_rows.reshape(count, length, heads, size).astype(jnp.float32)
    vh = v_rows.reshape(count, length, heads, size).astype(jnp.float32)
    mult = valid.astype(jnp.float32)[:, None, None, None]
    gh = g_rows.reshape(count, length, heads, size).astype(jnp.float32) * mult
    scores = jnp.einsum('bqhd,bkhd->bhqk', qh, kh) * scale
    scores = scores - jnp.max(scores, axis=-1, keepdims=True)
    prob = jnp.exp(scores)
    prob = prob / jnp.sum(prob, axis=-1, keepdims=True)
    prob_b = prob.astype(jnp.bfloat16).astype(jnp.float32)
    outp = jnp.einsum('bhqk,bkhd->bqhd', prob_b, vh) * mult
    dvalue = jnp.einsum('bhqk,bqhd->bkhd', prob_b, gh)
    dprob = jnp.einsum('bqhd,bkhd->bhqk', gh, vh)
    dscore = prob * (dprob - jnp.sum(prob * dprob, axis=-1, keepdims=True)) * scale
    dscore = dscore.astype(jnp.bfloat16).astype(jnp.float32)
    dquery = jnp.einsum('bhqk,bkhd->bqhd', dscore, kh)
    dkey = jnp.einsum('bhqk,bqhd->bkhd', dscore, qh)
    shape = (count, length, width)
    return outp.reshape(shape), dquery.reshape(shape), dkey.reshape(shape), dvalue.reshape(shape)


def reference(sentences, cotangent, w_query, w_key, w_value, send_rows, pair_src, pair_slot, pair_valid):
    n_lang = send_rows.shape[1]
    n_dev = send_rows.shape[0]
    n_pair = n_dev // n_lang
    flat = sentences.reshape(-1, D)
    queries = jnp.dot(flat, w_query, preferred_element_type=jnp.float32).astype(jnp.bfloat16).reshape(SENTENCES, L, D)
    keys = jnp.dot(flat, w_key, preferred_element_type=jnp.float32).astype(jnp.bfloat16).reshape(SENTENCES, L, D)
    values = jnp.dot(flat, w_value, preferred_element_type=jnp.float32).astype(jnp.bfloat16).reshape(SENTENCES, L, D)
    dev_ids = jnp.arange(n_dev, dtype=jnp.int32)
    group = dev_ids // n_pair
    place = dev_ids % n_pair
    slot_ids = jnp.arange(n_lang * CAP, dtype=jnp.int32)
    sender = (slot_ids // CAP)[None, :] * n_pair + place[:, None]
    entry = send_rows[sender, group[:, None], (slot_ids % CAP)[None, :]]
    targets = (sender * SENT_DEV + entry).astype(jnp.int32)
    block = 4
    slots = n_lang * CAP

    def one_device(carry, dev):
        grad_t, gwq, gwk, gwv = carry
        local_src = pair_src[dev]
        src_g = dev * SENT_DEV + local_src
        tgt_slots = targets[dev]
        pslot = pair_slot[dev]
        valid = pair_valid[dev]
        zeros_s = jnp.zeros((SENT_DEV, L, D), jnp.float32)
        zeros_t = jnp.zeros((slots, L, D), jnp.float32)

        def step(i, acc):
            out_acc, dq_acc, dk_acc, dv_acc = acc
            lo = i * block
            srcs = lax.dynamic_slice_in_dim(src_g, lo, block)
            locs = lax.dynamic_slice_in_dim(local_src, lo, block)
            sl = lax.dynamic_slice_in_dim(pslot, lo, block)
            vl = lax.dynamic_slice_in_dim(valid, lo, block)
            tg = tgt_slots[sl]
            outp, dquery, dkey, dvalue = attend_block(queries[srcs], keys[tg], values[tg], cotangent[srcs], vl, HEADS)
            return (out_acc.at[locs].add(outp), dq_acc.at[locs].add(dquery), dk_acc.at[sl].add(dkey), dv_acc.at[sl].add(dvalue))

        out_acc, dq_acc, dk_acc, dv_acc = lax.fori_loop(0, PAIRS_DEV // block, step, (zeros_s, zeros_s, zeros_t, zeros_t))
        dq_b = dq_acc.astype(jnp.bfloat16).reshape(-1, D)
        dk_b = dk_acc.astype(jnp.bfloat16).reshape(-1, D)
        dv_b = dv_acc.astype(jnp.bfloat16).reshape(-1, D)
        own = lax.dynamic_slice_in_dim(sentences, dev * SENT_DEV, SENT_DEV).reshape(-1, D)
        grad_src = jnp.dot(dq_b, w_query.T, preferred_element_type=jnp.float32)
        rows_t = sentences[tgt_slots].reshape(-1, D)
        dxt = jnp.dot(dk_b, w_key.T, preferred_element_type=jnp.float32) + jnp.dot(dv_b, w_value.T, preferred_element_type=jnp.float32)
        grad_t = grad_t.at[tgt_slots].add(dxt.reshape(slots, L, D))
        gwq = gwq + jnp.dot(own.T, dq_b, preferred_element_type=jnp.float32)
        gwk = gwk + jnp.dot(rows_t.T, dk_b, preferred_element_type=jnp.float32)
        gwv = gwv + jnp.dot(rows_t.T, dv_b, preferred_element_type=jnp.float32)
        return (grad_t, gwq, gwk, gwv), (out_acc.astype(jnp.bfloat16), grad_src.reshape(SENT_DEV, L, D))

    square = jnp.zeros((D, D), jnp.float32)
    start = (jnp.zeros((SENTENCES, L, D), jnp.float32), square, square, square)
    (grad_t, gwq, gwk, gwv), (attended, grad_src) = lax.scan(one_device, start, dev_ids)
    attended = attended.reshape(SENTENCES, L, D)
    grad_sentences = (grad_src.reshape(SENTENCES, L, D) + grad_t).astype(jnp.bfloat16)
    factor = 1.0 / (SENTENCES * L) ** 0.5
    return attended, grad_sentences, (gwq * factor).astype(jnp.bfloat16), (gwk * factor).astype(jnp.bfloat16), (gwv * factor).astype(jnp.bfloat16)
```

```python
import functools
import jax
import jax.numpy as jnp
from jax import lax
from jax.experimental import pallas as pl
from jax.experimental.pallas import tpu as pltpu
from jax.sharding import PartitionSpec as P

SIZE = 64
BF, F32 = jnp.bfloat16, jnp.float32
NT = (((1,), (1,)), ((), ()))


def mm(a, b):
    return jnp.dot(a, b, preferred_element_type=F32)


def mm_nt(a, b):
    return lax.dot_general(a, b, NT, preferred_element_type=F32)


def attend_kernel(src_ref, slot_ref, valid_ref, x_ref, r_ref, c_ref, wq_ref, wk_ref, wv_ref,
                  att_ref, dq_ref, dk_ref, dv_ref,
                  mult, q2, g2, k_s, v_s, kt, vt, ot, dqt, dk_acc, dv_acc, *, n_src, n_slot, length, width, unroll):
    heads = width // 128
    n_pairs = src_ref.shape[-1]
    for i in range(n_src * n_slot):
        mult[i] = 0
    for j in range(n_pairs):
        at = slot_ref[0, j] * n_src + src_ref[0, j]
        mult[at] = mult[at] + valid_ref[0, j]
    low = lax.broadcasted_iota(jnp.int32, (length, 128), 1) < SIZE
    zero = jnp.zeros((length, 128), BF)

    for s in range(n_src):
        rows = pl.ds(s * length, length)
        q = (mm(x_ref[rows, :], wq_ref[...]).astype(BF) * BF(0.125)).astype(BF)
        for h in range(heads):
            cols = slice(h * 128, (h + 1) * 128)
            qh = q[:, cols]
            gh = c_ref[rows, cols]
            q2[s, h, :length, :] = jnp.where(low, qh, zero)
            q2[s, h, length:, :] = jnp.where(low, zero, qh)
            g2[s, h, :length, :] = jnp.where(low, gh, zero)
            g2[s, h, length:, :] = jnp.where(low, zero, gh)

    def project(t, _):
        rows = pl.ds(pl.multiple_of(t * length, length), length)
        k = mm(r_ref[rows, :], wk_ref[...]).astype(BF)
        v = mm(r_ref[rows, :], wv_ref[...]).astype(BF)
        k_s[t] = k
        v_s[t] = v
        kt[t] = k.T
        vt[t] = v.T
        return 0

    lax.fori_loop(0, n_slot, project, 0)
    ot[...] = jnp.zeros_like(ot)
    dqt[...] = jnp.zeros_like(dqt)
    dk_acc[...] = jnp.zeros_like(dk_acc)
    dv_acc[...] = jnp.zeros_like(dv_acc)

    def combo(i, _):
        count = mult[i]

        @pl.when(count > 0)
        def _():
            t = i // n_src
            s = i % n_src
            m = count.astype(F32)

            def one(h):
                off = h * 128 if isinstance(h, int) else pl.multiple_of(h * 128, 128)
                cols = pl.ds(off, 128)
                kh = k_s[t, :, cols]
                vh = v_s[t, :, cols]
                qd = q2[s, h]
                gd = g2[s, h]
                st = mm_nt(kh, qd)
                dp = mm_nt(vh, gd)
                e = jnp.exp(st - jnp.max(st, axis=0, keepdims=True))
                inv = 1.0 / jnp.sum(e, axis=0, keepdims=True)
                delta = jnp.sum(e * dp, axis=0, keepdims=True) * inv
                p = e * (inv * m)
                pb = p.astype(BF)
                ds = (p * (dp - delta)).astype(BF)
                dv_acc[t, :, cols] += mm(pb, gd)
                dk_acc[t, :, cols] += mm(ds, qd)
                for half in range(2):
                    rows = pl.ds(off + half * SIZE, SIZE)
                    part = slice(half * length, (half + 1) * length)
                    ot[s, rows, :] += mm(vt[t, rows, :], pb[:, part])
                    dqt[s, rows, :] += mm(kt[t, rows, :], ds[:, part])

            if unroll >= heads:
                for h in range(heads):
                    one(h)
            else:
                def group(b, _):
                    for u in range(unroll):
                        one(b * unroll + u)
                    return 0
                lax.fori_loop(0, heads // unroll, group, 0)
        return 0

    lax.fori_loop(0, n_src * n_slot, combo, 0)
    for s in range(n_src):
        rows = slice(s * length, (s + 1) * length)
        att_ref[rows, :] = ot[s].T.astype(BF)
        dq_ref[rows, :] = (dqt[s].T * 0.125).astype(BF)
    for t in range(n_slot):
        rows = slice(t * length, (t + 1) * length)
        dk_ref[rows, :] = dk_acc[t].astype(BF)
        dv_ref[rows, :] = dv_acc[t].astype(BF)


def attend(src, slot, valid, x, r, c, wq, wk, wv, *, width, at=0, length=128, unroll=4):
    n_src, n_slot = x.shape[0] // length, r.shape[0] // length
    heads = width // 128
    smem = pl.BlockSpec(memory_space=pltpu.SMEM)
    whole = lambda a: pl.BlockSpec(a.shape, lambda i: (0, 0))
    cols = lambda a: pl.BlockSpec((a.shape[0], width), lambda i: (0, at))
    out = lambda n: jax.ShapeDtypeStruct((n * length, width), BF)
    outb = lambda n: pl.BlockSpec((n * length, width), lambda i: (0, 0))
    d = x.shape[1]
    macs = (n_src + 2 * n_slot) * length * d * width + 12 * 6 * length * length * width
    return pl.pallas_call(
        functools.partial(attend_kernel, n_src=n_src, n_slot=n_slot, length=length, width=width, unroll=unroll),
        grid=(1,),
        in_specs=[smem, smem, smem, whole(x), whole(r), cols(c), cols(wq), cols(wk), cols(wv)],
        out_specs=[outb(n_src), outb(n_src), outb(n_slot), outb(n_slot)],
        out_shape=[out(n_src), out(n_src), out(n_slot), out(n_slot)],
        scratch_shapes=[
            pltpu.SMEM((n_src * n_slot,), jnp.int32),
            pltpu.VMEM((n_src, heads, 2 * length, 128), BF),
            pltpu.VMEM((n_src, heads, 2 * length, 128), BF),
            pltpu.VMEM((n_slot, length, width), BF),
            pltpu.VMEM((n_slot, length, width), BF),
            pltpu.VMEM((n_slot, width, length), BF),
            pltpu.VMEM((n_slot, width, length), BF),
            pltpu.VMEM((n_src, width, length), F32),
            pltpu.VMEM((n_src, width, length), F32),
            pltpu.VMEM((n_slot, length, width), F32),
            pltpu.VMEM((n_slot, length, width), F32),
        ],
        compiler_params=pltpu.CompilerParams(vmem_limit_bytes=56 * 2**20),
        cost_estimate=pl.CostEstimate(flops=2 * macs * 4, bytes_accessed=8 * 2**20, transcendentals=0),
        name="attend",
    )(src, slot, valid, x, r, c, wq, wk, wv)


def body(sentences, cotangent, w_query, w_key, w_value, send_rows, pair_src, pair_slot, pair_valid):
    sent_dev, length, width = sentences.shape
    n_lang = lax.axis_size("lang")
    n_pair = lax.axis_size("pair")
    slots = n_lang * send_rows.shape[2]
    listed = send_rows[0].reshape(-1)
    outgoing = jnp.take(sentences, listed, axis=0)
    received = lax.all_to_all(outgoing, "lang", split_axis=0, concat_axis=0, tiled=True)
    x = sentences.reshape(-1, width)
    r = received.reshape(-1, width)
    c = cotangent.reshape(-1, width)
    attended, dq_b, dk_b, dv_b = attend(
        pair_src, pair_slot, pair_valid, x, r, c, w_query, w_key, w_value, width=width, length=length
    )
    grad_src = jnp.dot(dq_b, w_query.T, preferred_element_type=F32).reshape(sent_dev, length, width)
    dxt = jnp.dot(dk_b, w_key.T, preferred_element_type=F32) + jnp.dot(dv_b, w_value.T, preferred_element_type=F32)
    returned = lax.all_to_all(
        dxt.astype(BF).reshape(slots, length, width), "lang", split_axis=0, concat_axis=0, tiled=True
    )
    grad_total = grad_src.at[listed].add(returned.astype(F32))
    contract = (((0,), (0,)), ((), ()))
    gwq = lax.dot_general(x, dq_b, contract, preferred_element_type=F32)
    gwk = lax.dot_general(r, dk_b, contract, preferred_element_type=F32)
    gwv = lax.dot_general(r, dv_b, contract, preferred_element_type=F32)
    factor = 1.0 / (sent_dev * n_lang * n_pair * length) ** 0.5
    grads = lax.psum((gwq, gwk, gwv), ("lang", "pair"))
    grads = tuple((g * factor).astype(BF) for g in grads)
    return (attended.reshape(sentences.shape), grad_total.astype(BF)) + grads


def solution(mesh):
    split3, split2 = P(("lang", "pair"), None, None), P(("lang", "pair"), None)
    in_specs = (split3, split3, P(), P(), P(), split3, split2, split2, split2)
    out_specs = (split3, split3, P(), P(), P())
    return jax.shard_map(body, mesh=mesh, in_specs=in_specs, out_specs=out_specs, check_vma=False)
```

```python
import functools
import jax
import jax.numpy as jnp
from jax import lax
from jax.experimental import pallas as pl
from jax.experimental.pallas import tpu as pltpu
from jax.sharding import PartitionSpec as P

SIZE = 64
BF, F32 = jnp.bfloat16, jnp.float32
NT = (((1,), (1,)), ((), ()))


def mm(a, b):
    return jnp.dot(a, b, preferred_element_type=F32)


def mm_nt(a, b):
    return lax.dot_general(a, b, NT, preferred_element_type=F32)


def attend_kernel(src_ref, slot_ref, valid_ref, x_ref, r_ref, c_ref, wq_ref, wk_ref, wv_ref,
                  att_ref, dq_ref, dk_ref, dv_ref, gw_ref,
                  mult, xt, rt, q2, g2, k_s, v_s, kt, vt, ot, dqt, dk_acc, dv_acc,
                  *, n_src, n_slot, length, width):
    heads = width // 128
    n_pairs = src_ref.shape[-1]
    first = pl.program_id(0) == 0

    @pl.when(first)
    def _():
        for i in range(n_src * n_slot):
            mult[i] = 0
        for j in range(n_pairs):
            at = slot_ref[0, j] * n_src + src_ref[0, j]
            mult[at] = mult[at] + valid_ref[0, j]
        for s in range(n_src):
            xt[:, s * length:(s + 1) * length] = x_ref[s * length:(s + 1) * length, :].T
        for t in range(n_slot):
            rt[:, t * length:(t + 1) * length] = r_ref[t * length:(t + 1) * length, :].T

    low = lax.broadcasted_iota(jnp.int32, (n_src * length, 128), 1) < SIZE
    zero = jnp.zeros((n_src * length, 128), BF)
    block = min(256, width)

    for n in range(0, width, block):
        q = mm(x_ref[...], wq_ref[:, n:n + block]).astype(BF) * BF(0.125)
        for h in range(n // 128, (n + block) // 128):
            qh = q[:, h * 128 - n:(h + 1) * 128 - n]
            gh = c_ref[:, h * 128:(h + 1) * 128]
            for ref, rows in ((q2, qh), (g2, gh)):
                top = jnp.where(low, rows, zero)
                bot = jnp.where(low, zero, rows)
                for s in range(n_src):
                    ref[s, h, :length, :] = top[s * length:(s + 1) * length]
                    ref[s, h, length:, :] = bot[s * length:(s + 1) * length]

    half = n_slot // 2
    for n in range(0, width, block):
        cols = slice(n, n + block)
        for w_ref, nat, tra in ((wk_ref, k_s, kt), (wv_ref, v_s, vt)):
            for lo in range(0, n_slot, half):
                k = mm(r_ref[lo * length:(lo + half) * length, :], w_ref[:, cols]).astype(BF)
                for t in range(half):
                    rows = k[t * length:(t + 1) * length]
                    nat[lo + t, :, cols] = rows
                    tra[lo + t, cols, :] = rows.T
    ot[...] = jnp.zeros_like(ot)
    dqt[...] = jnp.zeros_like(dqt)
    dk_acc[...] = jnp.zeros_like(dk_acc)
    dv_acc[...] = jnp.zeros_like(dv_acc)

    def combo(i, _):
        count = mult[i]

        @pl.when(count > 0)
        def _():
            t = i // n_src
            s = i % n_src
            m = count.astype(F32)

            def scores(h):
                cols = slice(h * 128, (h + 1) * 128)
                return mm_nt(k_s[t, :, cols], q2[s, h]), mm_nt(v_s[t, :, cols], g2[s, h])

            def soft(st, dp):
                e = jnp.exp(st - jnp.max(st, axis=0, keepdims=True))
                inv = 1.0 / jnp.sum(e, axis=0, keepdims=True)
                delta = jnp.sum(e * dp, axis=0, keepdims=True) * inv
                p = e * (inv * m)
                return p.astype(BF), (p * (dp - delta)).astype(BF)

            def grads(h, pb, ds):
                cols = slice(h * 128, (h + 1) * 128)
                dv = mm(pb, g2[s, h])
                dk = mm(ds, q2[s, h])
                o = mm(vt[t, cols, :], pb)
                dq = mm(kt[t, cols, :], ds)
                dv_acc[t, :, cols] += dv
                dk_acc[t, :, cols] += dk
                for half in range(2):
                    rows = slice(h * 128 + half * SIZE, h * 128 + (half + 1) * SIZE)
                    own = slice(half * SIZE, (half + 1) * SIZE)
                    part = slice(half * length, (half + 1) * length)
                    ot[s, rows, :] += o[own, part]
                    dqt[s, rows, :] += dq[own, part]

            ready = [scores(h) for h in range(min(2, heads))]
            waiting = []
            for h in range(heads):
                if h + 2 < heads:
                    ready.append(scores(h + 2))
                waiting.append((h,) + soft(*ready.pop(0)))
                if h > 0:
                    grads(*waiting.pop(0))
            grads(*waiting.pop(0))
        return 0

    lax.fori_loop(0, n_src * n_slot, combo, 0)
    for s in range(n_src):
        rows = slice(s * length, (s + 1) * length)
        att_ref[rows, :] = ot[s].T.astype(BF)
        dq_ref[rows, :] = (dqt[s].T * 0.125).astype(BF)
    for t in range(n_slot):
        rows = slice(t * length, (t + 1) * length)
        dk_ref[rows, :] = dk_acc[t].astype(BF)
        dv_ref[rows, :] = dv_acc[t].astype(BF)
    groups, _, each, _ = gw_ref.shape
    for n in range(0, width, block):
        cols = slice(n, n + block)
        for i, (lhs, rhs) in enumerate(((xt, dq_ref), (rt, dk_ref), (rt, dv_ref))):
            for lo in range(0, groups, groups // 2):
                g = mm(lhs[lo * each:(lo + groups // 2) * each, :], rhs[:, cols]).astype(BF)
                gw_ref[lo:lo + groups // 2, i, :, cols] = g.reshape(groups // 2, each, block)


def attend(src, slot, valid, x, r, c, wq, wk, wv, *, groups, width, at=0, steps=1, length=128):
    n_src, n_slot = x.shape[0] // length, r.shape[0] // length
    heads = width // 128
    smem = pl.BlockSpec(memory_space=pltpu.SMEM)
    whole = lambda a: pl.BlockSpec(a.shape, lambda i: (0, 0))
    cols = lambda a: pl.BlockSpec((a.shape[0], width), lambda i: (0, at + i))
    out = lambda n: jax.ShapeDtypeStruct((n * length, width * steps), BF)
    outb = lambda n: pl.BlockSpec((n * length, width), lambda i: (0, i))
    d = x.shape[1]
    each = d // groups
    macs = steps * (2 * (n_src + 2 * n_slot) * length * d * width + 12 * 6 * length * length * width)
    return pl.pallas_call(
        functools.partial(attend_kernel, n_src=n_src, n_slot=n_slot, length=length, width=width),
        grid=(steps,),
        in_specs=[smem, smem, smem, whole(x), whole(r), cols(c), cols(wq), cols(wk), cols(wv)],
        out_specs=[outb(n_src), outb(n_src), outb(n_slot), outb(n_slot),
                   pl.BlockSpec((groups, 3, each, width), lambda i: (0, 0, 0, i))],
        out_shape=[out(n_src), out(n_src), out(n_slot), out(n_slot),
                   jax.ShapeDtypeStruct((groups, 3, each, width * steps), BF)],
        scratch_shapes=[
            pltpu.SMEM((n_src * n_slot,), jnp.int32),
            pltpu.VMEM((d, n_src * length), BF),
            pltpu.VMEM((d, n_slot * length), BF),
            pltpu.VMEM((n_src, heads, 2 * length, 128), BF),
            pltpu.VMEM((n_src, heads, 2 * length, 128), BF),
            pltpu.VMEM((n_slot, length, width), BF),
            pltpu.VMEM((n_slot, length, width), BF),
            pltpu.VMEM((n_slot, width, length), BF),
            pltpu.VMEM((n_slot, width, length), BF),
            pltpu.VMEM((n_src, width, length), F32),
            pltpu.VMEM((n_src, width, length), F32),
            pltpu.VMEM((n_slot, length, width), F32),
            pltpu.VMEM((n_slot, length, width), F32),
        ],
        compiler_params=pltpu.CompilerParams(vmem_limit_bytes=56 * 2**20),
        cost_estimate=pl.CostEstimate(flops=2 * macs * 4, bytes_accessed=8 * 2**20, transcendentals=0),
        name="attend",
    )(src, slot, valid, x, r, c, wq, wk, wv)


def body(sentences, cotangent, w_query, w_key, w_value, send_rows, pair_src, pair_slot, pair_valid):
    sent_dev, length, width = sentences.shape
    n_lang = lax.axis_size("lang")
    n_pair = lax.axis_size("pair")
    slots = n_lang * send_rows.shape[2]
    listed = send_rows[0].reshape(-1)
    outgoing = jnp.take(sentences, listed, axis=0, mode="clip")
    received = lax.all_to_all(outgoing, "lang", split_axis=0, concat_axis=0, tiled=True)
    x = sentences.reshape(-1, width)
    r = received.reshape(-1, width)
    c = cotangent.reshape(-1, width)
    attended, dq_b, dk_b, dv_b, grads = attend(
        pair_src, pair_slot, pair_valid, x, r, c, w_query, w_key, w_value,
        groups=n_lang, width=width, length=length,
    )
    part = lax.psum_scatter(grads.reshape(-1, width), "lang", scatter_dimension=0, tiled=True)
    grad_src = jnp.dot(dq_b, w_query.T, preferred_element_type=F32).reshape(sent_dev, length, width)
    dxt = jnp.dot(dk_b, w_key.T, preferred_element_type=F32) + jnp.dot(dv_b, w_value.T, preferred_element_type=F32)
    returned = lax.all_to_all(
        dxt.astype(BF).reshape(slots, length, width), "lang", split_axis=0, concat_axis=0, tiled=True
    )
    part, returned = lax.optimization_barrier((part, returned))
    grad_total = grad_src.at[listed].add(returned.astype(F32))
    factor = 1.0 / (sent_dev * n_lang * n_pair * length) ** 0.5
    rows = width // n_lang // n_pair
    pieces = part.reshape(3, n_pair, rows, width).transpose(1, 0, 2, 3)
    pieces = lax.all_to_all(pieces, "pair", split_axis=0, concat_axis=0, tiled=True)
    mine = (jnp.sum(pieces.astype(F32), axis=0) * factor).astype(BF)
    copies = jnp.broadcast_to(mine[None], (n_pair, 3, rows, width))
    group = lax.all_to_all(copies, "pair", split_axis=0, concat_axis=0, tiled=True)
    group = group.transpose(1, 0, 2, 3).reshape(3 * n_pair * rows, width)
    grads = lax.all_gather(group, "lang", axis=0, tiled=True).reshape(n_lang, 3, n_pair * rows, width)
    grads = tuple(grads[:, i].reshape(width, width) for i in range(3))
    return (attended.reshape(sentences.shape), grad_total.astype(BF)) + grads


def solution(mesh):
    split3, split2 = P(("lang", "pair"), None, None), P(("lang", "pair"), None)
    in_specs = (split3, split3, P(), P(), P(), split3, split2, split2, split2)
    out_specs = (split3, split3, P(), P(), P())
    return jax.shard_map(body, mesh=mesh, in_specs=in_specs, out_specs=out_specs, check_vma=False)
```

```python
import functools

import jax
import jax.numpy as jnp
from jax import lax
from jax.experimental import pallas as pl
from jax.experimental.pallas import tpu as pltpu
from jax.sharding import PartitionSpec as P

SIZE = 64
LANES = 128
BF, F32 = jnp.bfloat16, jnp.float32
NT = (((1,), (1,)), ((), ()))


def mm(a, b):
    return jnp.dot(a, b, preferred_element_type=F32)


def mm_nt(a, b):
    return lax.dot_general(a, b, NT, preferred_element_type=F32)


def attend_kernel(me_ref, src_ref, slot_ref, valid_ref, x_hbm, r_hbm, c_hbm, wq_hbm, wk_hbm, wv_hbm,
                  *rest, n_src, n_slot, length):
    outs, scratch = rest[:4 + n_slot], rest[4 + n_slot:]
    att_hbm, dq_hbm, keep_hbm, send_hbm = outs[:4]
    dx_hbm = outs[4:]
    (mult, x_ref, r_ref, c_ref, wq_ref, wk_ref, wv_ref, att_v, dq_v, gw_v, dx_v,
     xt, rt, q2, g2, k_s, v_s, kt, vt, ot, dqt, dk_acc, dv_acc, sem_in, sem_r, sem_out) = scratch
    width = x_ref.shape[1]
    heads = width // LANES
    n_pairs = src_ref.shape[-1]
    me = me_ref[0]
    block = 256

    copies = [pltpu.make_async_copy(a, b, sem_in.at[i]) for i, (a, b) in enumerate(
        ((x_hbm, x_ref), (wq_hbm, wq_ref), (c_hbm, c_ref), (wk_hbm, wk_ref), (wv_hbm, wv_ref)))]
    slots = [pltpu.make_async_copy(r_hbm.at[lax.rem(me + p, n_slot)], r_ref.at[pl.ds(p * length, length), :],
                                   sem_r.at[p]) for p in range(n_slot)]
    for c in copies[:4] + slots + copies[4:]:
        c.start()

    for i in range(n_src * n_slot):
        mult[i] = 0
    for j in range(n_pairs):
        at = lax.rem(slot_ref[0, j] + n_slot - me, n_slot) * n_src + src_ref[0, j]
        mult[at] = mult[at] + valid_ref[0, j]
    ot[...] = jnp.zeros_like(ot)
    dqt[...] = jnp.zeros_like(dqt)
    dk_acc[...] = jnp.zeros_like(dk_acc)
    dv_acc[...] = jnp.zeros_like(dv_acc)

    for c in copies[:3]:
        c.wait()
    low = lax.broadcasted_iota(jnp.int32, (n_src * length, LANES), 1) < SIZE
    zero = jnp.zeros((n_src * length, LANES), BF)
    for n in range(0, width, block):
        q = mm(x_ref[...], wq_ref[:, n:n + block]).astype(BF) * BF(0.125)
        for h in range(n // LANES, (n + block) // LANES):
            qh = q[:, h * LANES - n:(h + 1) * LANES - n]
            gh = c_ref[:, h * LANES:(h + 1) * LANES]
            for ref, rows in ((q2, qh), (g2, gh)):
                top = jnp.where(low, rows, zero)
                bot = jnp.where(low, zero, rows)
                for s in range(n_src):
                    ref[s, h, :length, :] = top[s * length:(s + 1) * length]
                    ref[s, h, length:, :] = bot[s * length:(s + 1) * length]
    for s in range(n_src):
        xt[:, s * length:(s + 1) * length] = x_ref[s * length:(s + 1) * length, :].T

    copies[3].wait()
    for c in slots:
        c.wait()
    half = n_slot // 2
    for w_ref, nat, tra in ((wk_ref, k_s, kt), (wv_ref, v_s, vt)):
        if w_ref is wv_ref:
            copies[4].wait()
        for n in range(0, width, block):
            cols = slice(n, n + block)
            for lo in range(0, n_slot, half):
                k = mm(r_ref[lo * length:(lo + half) * length, :], w_ref[:, cols]).astype(BF)
                for t in range(half):
                    rows = k[t * length:(t + 1) * length]
                    nat[lo + t, :, cols] = rows
                    tra[lo + t, cols, :] = rows.T
    for t in range(n_slot):
        rt[:, t * length:(t + 1) * length] = r_ref[t * length:(t + 1) * length, :].T

    def combo(i, _):
        count = mult[i]

        @pl.when(count > 0)
        def _():
            t = i // n_src
            s = i % n_src
            m = count.astype(F32)

            def scores(h):
                cols = slice(h * LANES, (h + 1) * LANES)
                return mm_nt(k_s[t, :, cols], q2[s, h]), mm_nt(v_s[t, :, cols], g2[s, h])

            def soft(st, dp):
                e = jnp.exp(st - jnp.max(st, axis=0, keepdims=True))
                inv = 1.0 / jnp.sum(e, axis=0, keepdims=True)
                delta = jnp.sum(e * dp, axis=0, keepdims=True) * inv
                p = e * (inv * m)
                return p.astype(BF), (p * (dp - delta)).astype(BF)

            def grads(h, pb, ds):
                cols = slice(h * LANES, (h + 1) * LANES)
                dv = mm(pb, g2[s, h])
                dk = mm(ds, q2[s, h])
                o = mm(vt[t, cols, :], pb)
                dq = mm(kt[t, cols, :], ds)
                dv_acc[t, :, cols] += dv
                dk_acc[t, :, cols] += dk
                for part in range(2):
                    rows = slice(h * LANES + part * SIZE, h * LANES + (part + 1) * SIZE)
                    own = slice(part * SIZE, (part + 1) * SIZE)
                    keys = slice(part * length, (part + 1) * length)
                    ot[s, rows, :] += o[own, keys]
                    dqt[s, rows, :] += dq[own, keys]

            ready = [scores(h) for h in range(min(2, heads))]
            waiting = []
            for h in range(heads):
                if h + 2 < heads:
                    ready.append(scores(h + 2))
                waiting.append((h,) + soft(*ready.pop(0)))
                if h > 0:
                    grads(*waiting.pop(0))
            grads(*waiting.pop(0))
        return 0

    lax.fori_loop(0, n_src * n_slot, combo, 0)

    for t in range(n_slot):
        k_s[t] = dk_acc[t].astype(BF)
        v_s[t] = dv_acc[t].astype(BF)
    for s in range(n_src):
        dq_v[s * length:(s + 1) * length, :] = (dqt[s].T * 0.125).astype(BF)
    dk = k_s[...].reshape(n_slot * length, width)
    dv = v_s[...].reshape(n_slot * length, width)

    done = []

    def out(src, dst):
        c = pltpu.make_async_copy(src, dst, sem_out.at[len(done)])
        c.start()
        done.append(c)

    _, pieces, _, each, _ = gw_v.shape
    core = lax.rem(me, 2)
    for k, dst in enumerate((send_hbm, keep_hbm)):
        base = pl.multiple_of((core if k else 1 - core) * (pieces * each), LANES)
        rows = pl.ds(base, pieces * each)
        for n in range(0, width, block):
            cols = slice(n, n + block)
            for i, (lhs, rhs) in enumerate(((xt, dq_v[:, cols]), (rt, dk[:, cols]), (rt, dv[:, cols]))):
                gw_v[k, :, i, :, cols] = mm(lhs[rows, :], rhs).astype(BF).reshape(pieces, each, block)
        out(gw_v.at[k], dst)
        if k == 0:
            out(dq_v, dq_hbm)
    for s in range(n_src):
        att_v[s * length:(s + 1) * length, :] = ot[s].T.astype(BF)
    out(att_v, att_hbm)
    for lo in range(0, n_slot, half):
        rows = slice(lo * length, (lo + half) * length)
        for n in range(0, width, block):
            cols = slice(n, n + block)
            dx_v[rows, cols] = (mm_nt(dk[rows], wk_ref[cols, :]) + mm_nt(dv[rows], wv_ref[cols, :])).astype(BF)
        for t in range(lo, lo + half):
            out(dx_v.at[pl.ds(t * length, length), :], dx_hbm[t])
    for c in done:
        c.wait()


def attend(me, src, slot, valid, x, r, c, wq, wk, wv, *, pieces):
    n_slot, length, width = r.shape
    rows = x.shape[0]
    n_src = rows // length
    each = width // 2 // pieces
    heads = width // LANES
    smem = pl.BlockSpec(memory_space=pltpu.SMEM)
    hbm = pl.BlockSpec(memory_space=pl.ANY)
    shape = jax.ShapeDtypeStruct
    vm = pltpu.VMEM
    macs = 2 * (n_src + 3 * n_slot) * length * width * width + 12 * 6 * length * length * width
    return pl.pallas_call(
        functools.partial(attend_kernel, n_src=n_src, n_slot=n_slot, length=length),
        in_specs=[smem] * 4 + [hbm] * 6,
        out_specs=[hbm] * (4 + n_slot),
        out_shape=[shape((rows, width), BF), shape((rows, width), BF),
                   shape((pieces, 3, each, width), BF), shape((pieces, 3, each, width), BF)]
        + [shape((length, width), BF)] * n_slot,
        scratch_shapes=[
            pltpu.SMEM((n_src * n_slot,), jnp.int32),
            vm((rows, width), BF), vm((n_slot * length, width), BF), vm((rows, width), BF),
            vm((width, width), BF), vm((width, width), BF), vm((width, width), BF),
            vm((rows, width), BF), vm((rows, width), BF),
            vm((2, pieces, 3, each, width), BF), vm((n_slot * length, width), BF),
            vm((width, rows), BF), vm((width, n_slot * length), BF),
            vm((n_src, heads, 2 * length, LANES), BF), vm((n_src, heads, 2 * length, LANES), BF),
            vm((n_slot, length, width), BF), vm((n_slot, length, width), BF),
            vm((n_slot, width, length), BF), vm((n_slot, width, length), BF),
            vm((n_src, width, length), F32), vm((n_src, width, length), F32),
            vm((n_slot, length, width), F32), vm((n_slot, length, width), F32),
            pltpu.SemaphoreType.DMA((5,)), pltpu.SemaphoreType.DMA((n_slot,)),
            pltpu.SemaphoreType.DMA((4 + n_slot,)),
        ],
        compiler_params=pltpu.CompilerParams(vmem_limit_bytes=60 * 2**20),
        cost_estimate=pl.CostEstimate(flops=4 * macs, bytes_accessed=20 * 2**20, transcendentals=0),
        name="attend",
    )(me, src, slot, valid, x, r, c, wq, wk, wv)


def combine_kernel(me_ref, listed_ref, dq_ref, wq_ref, *rest):
    parts, (out_ref, acc) = rest[:-2], rest[-2:]
    n_slot = len(parts)
    length = parts[0].shape[0]
    me = me_ref[0]
    block = 256
    for n in range(0, acc.shape[2], block):
        cols = slice(n, n + block)
        acc[:, :, cols] = mm_nt(dq_ref[...], wq_ref[cols, :]).reshape(acc.shape[0], length, block)
    for s, part in enumerate(parts):
        at = listed_ref[lax.rem(me + n_slot - s, n_slot)]
        acc[at] += part[...].astype(F32)
    out_ref[...] = acc[...].astype(BF)


def combine(me, listed, dq, wq, parts):
    length, width = parts[0].shape
    n_src = dq.shape[0] // length
    smem = pl.BlockSpec(memory_space=pltpu.SMEM)
    vmem = pl.BlockSpec(memory_space=pltpu.VMEM)
    return pl.pallas_call(
        combine_kernel,
        in_specs=[smem, smem] + [vmem] * (2 + len(parts)),
        out_specs=vmem,
        out_shape=jax.ShapeDtypeStruct((n_src, length, width), BF),
        scratch_shapes=[pltpu.VMEM((n_src, length, width), F32)],
        compiler_params=pltpu.CompilerParams(vmem_limit_bytes=24 * 2**20),
        cost_estimate=pl.CostEstimate(flops=2 * dq.size * width, bytes_accessed=6 * 2**20, transcendentals=0),
        name="combine",
    )(me, listed, dq, wq, *parts)


def spread_kernel(parts_ref, out_ref, *, factor):
    total = jnp.sum(parts_ref[...].astype(F32), axis=0)
    out_ref[...] = jnp.broadcast_to((total * factor).astype(BF)[None], out_ref.shape)


def spread(parts, copies, factor):
    shape = parts.shape[1:]
    grid = shape[0]
    return pl.pallas_call(
        functools.partial(spread_kernel, factor=factor),
        grid=(grid,),
        in_specs=[pl.BlockSpec((parts.shape[0], 1) + shape[1:], lambda i: (0, i, 0, 0))],
        out_specs=pl.BlockSpec((copies, 1) + shape[1:], lambda i: (0, i, 0, 0)),
        out_shape=jax.ShapeDtypeStruct((copies,) + shape, BF),
        compiler_params=pltpu.CompilerParams(vmem_limit_bytes=16 * 2**20),
        cost_estimate=pl.CostEstimate(flops=parts.size, bytes_accessed=4 * parts.size, transcendentals=0),
        name="spread",
    )(parts)


def place_kernel(half_ref, rows_hbm, *rest):
    sem = rest[-1]
    outs = rest[-4:-1]
    copies = [pltpu.make_async_copy(rows_hbm.at[:, i], out.at[half_ref[0]], sem.at[i]) for i, out in enumerate(outs)]
    for c in copies:
        c.start()
    for c in copies:
        c.wait()


def place(half, rows, into=()):
    pieces, n, each, width = rows.shape
    hbm = pl.BlockSpec(memory_space=pl.ANY)
    return pl.pallas_call(
        place_kernel,
        in_specs=[pl.BlockSpec(memory_space=pltpu.SMEM), hbm] + [hbm] * len(into),
        out_specs=[hbm] * n,
        out_shape=[jax.ShapeDtypeStruct((2, pieces, each, width), BF)] * n,
        input_output_aliases={2 + i: i for i in range(len(into))},
        scratch_shapes=[pltpu.SemaphoreType.DMA((n,))],
        cost_estimate=pl.CostEstimate(flops=0, bytes_accessed=4 * rows.size, transcendentals=0),
        name="place",
    )(half, rows, *into)


def body(sentences, cotangent, w_query, w_key, w_value, send_rows, pair_src, pair_slot, pair_valid):
    sent_dev, length, width = sentences.shape
    n_lang = lax.axis_size("lang")
    n_pair = lax.axis_size("pair")
    me = lax.axis_index("lang")
    listed = send_rows[0].reshape(-1)
    outgoing = jnp.take(sentences, listed, axis=0, mode="clip")
    received = lax.all_to_all(outgoing, "lang", split_axis=0, concat_axis=0, tiled=True)
    x = sentences.reshape(-1, width)
    c = cotangent.reshape(-1, width)
    where = me.reshape(1).astype(jnp.int32)
    attended, dq, keep, send, *dx = attend(
        where, pair_src, pair_slot, pair_valid, x, received, c, w_query, w_key, w_value, pieces=n_pair
    )
    other_core = [(i, i ^ 1) for i in range(n_lang)]
    other = lax.ppermute(send, "lang", other_core)
    back = [dx[0]]
    for s in range(1, n_lang):
        back.append(lax.ppermute(dx[s], "lang", [(i, (i + s) % n_lang) for i in range(n_lang)]))
    chip = (keep.astype(F32) + other.astype(F32)).astype(BF)
    pieces = lax.all_to_all(chip, "pair", split_axis=0, concat_axis=0, tiled=True)
    pieces, *back[1:6] = lax.optimization_barrier((pieces, *back[1:6]))
    n_y = n_lang // 2
    along_y = [[2 * y + core for y in range(n_y)] for core in range(2)]
    columns = lax.all_to_all(
        spread(pieces, n_y, 1.0), "lang", split_axis=0, concat_axis=0, axis_index_groups=along_y, tiled=True
    )
    factor = 1.0 / (sent_dev * n_lang * n_pair * length) ** 0.5
    near = lax.all_to_all(spread(columns, n_pair, factor), "pair", split_axis=0, concat_axis=0, tiled=True)
    near, *back[6:] = lax.optimization_barrier((near, *back[6:]))
    far = lax.ppermute(near, "lang", other_core)
    grad_sentences = combine(where, listed, dq, w_query, back)
    core = lax.rem(where, 2)
    grads = place(1 - core, far, place(core, near))
    grads = tuple(g.reshape(width, width) for g in grads)
    return (attended.reshape(sentences.shape), grad_sentences) + grads


def solution(mesh):
    split3, split2 = P(("lang", "pair"), None, None), P(("lang", "pair"), None)
    in_specs = (split3, split3, P(), P(), P(), split3, split2, split2, split2)
    out_specs = (split3, split3, P(), P(), P())
    return jax.shard_map(body, mesh=mesh, in_specs=in_specs, out_specs=out_specs, check_vma=False)
```

```python
import functools

import jax
import jax.numpy as jnp
from jax import lax
from jax.experimental import pallas as pl
from jax.experimental.pallas import tpu as pltpu
from jax.sharding import PartitionSpec as P

SIZE = 64
LANES = 128
BF, F32 = jnp.bfloat16, jnp.float32
NT = (((1,), (1,)), ((), ()))


def mm(a, b):
    return jnp.dot(a, b, preferred_element_type=F32)


def mm_nt(a, b):
    return lax.dot_general(a, b, NT, preferred_element_type=F32)


def attend_kernel(me_ref, src_ref, slot_ref, valid_ref, x_hbm, r_hbm, c_hbm, wq_hbm, wk_hbm, wv_hbm,
                  *rest, n_src, n_slot, length):
    outs, scratch = rest[:4 + n_slot], rest[4 + n_slot:]
    att_hbm, dq_hbm, keep_hbm, send_hbm = outs[:4]
    dx_hbm = outs[4:]
    (mult, x_ref, r_ref, c_ref, wq_ref, wk_ref, wv_ref, att_v, dq_v, gw_v, dx_v,
     xt, rt, q2, g2, k_s, v_s, kt, vt, ot, dqt, dk_acc, dv_acc, sem_in, sem_r, sem_out) = scratch
    width = x_ref.shape[1]
    heads = width // LANES
    n_pairs = src_ref.shape[-1]
    me = me_ref[0]
    block = 256

    copies = [pltpu.make_async_copy(a, b, sem_in.at[i]) for i, (a, b) in enumerate(
        ((x_hbm, x_ref), (wq_hbm, wq_ref), (c_hbm, c_ref), (wk_hbm, wk_ref), (wv_hbm, wv_ref)))]
    slots = [pltpu.make_async_copy(r_hbm.at[lax.rem(me + p, n_slot)], r_ref.at[pl.ds(p * length, length), :],
                                   sem_r.at[p]) for p in range(n_slot)]
    for c in copies[:4] + slots + copies[4:]:
        c.start()

    for i in range(n_src * n_slot):
        mult[i] = 0
    for j in range(n_pairs):
        at = lax.rem(slot_ref[0, j] + n_slot - me, n_slot) * n_src + src_ref[0, j]
        mult[at] = mult[at] + valid_ref[0, j]
    ot[...] = jnp.zeros_like(ot)
    dqt[...] = jnp.zeros_like(dqt)
    dk_acc[...] = jnp.zeros_like(dk_acc)
    dv_acc[...] = jnp.zeros_like(dv_acc)

    for c in copies[:3]:
        c.wait()
    low = lax.broadcasted_iota(jnp.int32, (n_src * length, LANES), 1) < SIZE
    zero = jnp.zeros((n_src * length, LANES), BF)
    for n in range(0, width, block):
        q = mm(x_ref[...], wq_ref[:, n:n + block]).astype(BF) * BF(0.125)
        for h in range(n // LANES, (n + block) // LANES):
            qh = q[:, h * LANES - n:(h + 1) * LANES - n]
            gh = c_ref[:, h * LANES:(h + 1) * LANES]
            for ref, rows in ((q2, qh), (g2, gh)):
                top = jnp.where(low, rows, zero)
                bot = jnp.where(low, zero, rows)
                for s in range(n_src):
                    ref[s, h, :length, :] = top[s * length:(s + 1) * length]
                    ref[s, h, length:, :] = bot[s * length:(s + 1) * length]
    for s in range(n_src):
        xt[:, s * length:(s + 1) * length] = x_ref[s * length:(s + 1) * length, :].T

    copies[3].wait()
    for c in slots:
        c.wait()
    half = n_slot // 2
    for w_ref, nat, tra in ((wk_ref, k_s, kt), (wv_ref, v_s, vt)):
        if w_ref is wv_ref:
            copies[4].wait()
        for n in range(0, width, block):
            cols = slice(n, n + block)
            for lo in range(0, n_slot, half):
                k = mm(r_ref[lo * length:(lo + half) * length, :], w_ref[:, cols]).astype(BF)
                for t in range(half):
                    rows = k[t * length:(t + 1) * length]
                    nat[lo + t, :, cols] = rows
                    tra[lo + t, cols, :] = rows.T
    for t in range(n_slot):
        rt[:, t * length:(t + 1) * length] = r_ref[t * length:(t + 1) * length, :].T

    def combo(i, _):
        count = mult[i]

        @pl.when(count > 0)
        def _():
            t = i // n_src
            s = i % n_src
            m = count.astype(F32)

            def scores(h):
                cols = slice(h * LANES, (h + 1) * LANES)
                return mm_nt(k_s[t, :, cols], q2[s, h]), mm_nt(v_s[t, :, cols], g2[s, h])

            def soft(st, dp):
                e = jnp.exp(st - jnp.max(st, axis=0, keepdims=True))
                inv = 1.0 / jnp.sum(e, axis=0, keepdims=True)
                delta = jnp.sum(e * dp, axis=0, keepdims=True) * inv
                p = e * (inv * m)
                return p.astype(BF), (p * (dp - delta)).astype(BF)

            def grads(h, pb, ds):
                cols = slice(h * LANES, (h + 1) * LANES)
                dv = mm(pb, g2[s, h])
                dk = mm(ds, q2[s, h])
                o = mm(vt[t, cols, :], pb)
                dq = mm(kt[t, cols, :], ds)
                dv_acc[t, :, cols] += dv
                dk_acc[t, :, cols] += dk
                for part in range(2):
                    rows = slice(h * LANES + part * SIZE, h * LANES + (part + 1) * SIZE)
                    own = slice(part * SIZE, (part + 1) * SIZE)
                    keys = slice(part * length, (part + 1) * length)
                    ot[s, rows, :] += o[own, keys]
                    dqt[s, rows, :] += dq[own, keys]

            ready = [scores(h) for h in range(min(2, heads))]
            waiting = []
            for h in range(heads):
                if h + 2 < heads:
                    ready.append(scores(h + 2))
                waiting.append((h,) + soft(*ready.pop(0)))
                if h > 0:
                    grads(*waiting.pop(0))
            grads(*waiting.pop(0))
        return 0

    lax.fori_loop(0, n_src * n_slot, combo, 0)

    for t in range(n_slot):
        k_s[t] = dk_acc[t].astype(BF)
        v_s[t] = dv_acc[t].astype(BF)
    for s in range(n_src):
        dq_v[s * length:(s + 1) * length, :] = (dqt[s].T * 0.125).astype(BF)
    dk = k_s[...].reshape(n_slot * length, width)
    dv = v_s[...].reshape(n_slot * length, width)

    done = []

    def out(src, dst):
        c = pltpu.make_async_copy(src, dst, sem_out.at[len(done)])
        c.start()
        done.append(c)

    _, pieces, _, each, _ = gw_v.shape
    core = lax.rem(me, 2)
    for k, dst in enumerate((send_hbm, keep_hbm)):
        base = pl.multiple_of((core if k else 1 - core) * (pieces * each), LANES)
        rows = pl.ds(base, pieces * each)
        for n in range(0, width, block):
            cols = slice(n, n + block)
            for i, (lhs, rhs) in enumerate(((xt, dq_v[:, cols]), (rt, dk[:, cols]), (rt, dv[:, cols]))):
                gw_v[k, :, i, :, cols] = mm(lhs[rows, :], rhs).astype(BF).reshape(pieces, each, block)
        out(gw_v.at[k], dst)
        if k == 0:
            out(dq_v, dq_hbm)
    for s in range(n_src):
        att_v[s * length:(s + 1) * length, :] = ot[s].T.astype(BF)
    out(att_v, att_hbm)
    for lo in range(0, n_slot, half):
        rows = slice(lo * length, (lo + half) * length)
        for n in range(0, width, block):
            cols = slice(n, n + block)
            dx_v[rows, cols] = (mm_nt(dk[rows], wk_ref[cols, :]) + mm_nt(dv[rows], wv_ref[cols, :])).astype(BF)
        for t in range(lo, lo + half):
            out(dx_v.at[pl.ds(t * length, length), :], dx_hbm[t])
    for c in done:
        c.wait()


def attend(me, src, slot, valid, x, r, c, wq, wk, wv, *, pieces):
    n_slot, length, width = r.shape
    rows = x.shape[0]
    n_src = rows // length
    each = width // 2 // pieces
    heads = width // LANES
    smem = pl.BlockSpec(memory_space=pltpu.SMEM)
    hbm = pl.BlockSpec(memory_space=pl.ANY)
    shape = jax.ShapeDtypeStruct
    vm = pltpu.VMEM
    macs = 2 * (n_src + 3 * n_slot) * length * width * width + 12 * 6 * length * length * width
    return pl.pallas_call(
        functools.partial(attend_kernel, n_src=n_src, n_slot=n_slot, length=length),
        in_specs=[smem] * 4 + [hbm] * 6,
        out_specs=[hbm] * (4 + n_slot),
        out_shape=[shape((rows, width), BF), shape((rows, width), BF),
                   shape((pieces, 3, each, width), BF), shape((pieces, 3, each, width), BF)]
        + [shape((length, width), BF)] * n_slot,
        scratch_shapes=[
            pltpu.SMEM((n_src * n_slot,), jnp.int32),
            vm((rows, width), BF), vm((n_slot * length, width), BF), vm((rows, width), BF),
            vm((width, width), BF), vm((width, width), BF), vm((width, width), BF),
            vm((rows, width), BF), vm((rows, width), BF),
            vm((2, pieces, 3, each, width), BF), vm((n_slot * length, width), BF),
            vm((width, rows), BF), vm((width, n_slot * length), BF),
            vm((n_src, heads, 2 * length, LANES), BF), vm((n_src, heads, 2 * length, LANES), BF),
            vm((n_slot, length, width), BF), vm((n_slot, length, width), BF),
            vm((n_slot, width, length), BF), vm((n_slot, width, length), BF),
            vm((n_src, width, length), F32), vm((n_src, width, length), F32),
            vm((n_slot, length, width), F32), vm((n_slot, length, width), F32),
            pltpu.SemaphoreType.DMA((5,)), pltpu.SemaphoreType.DMA((n_slot,)),
            pltpu.SemaphoreType.DMA((4 + n_slot,)),
        ],
        compiler_params=pltpu.CompilerParams(vmem_limit_bytes=60 * 2**20),
        cost_estimate=pl.CostEstimate(flops=4 * macs, bytes_accessed=20 * 2**20, transcendentals=0),
        name="attend",
    )(me, src, slot, valid, x, r, c, wq, wk, wv)


def combine_kernel(me_ref, listed_ref, dq_ref, wq_ref, *rest):
    parts, (out_ref, acc) = rest[:-2], rest[-2:]
    n_slot = len(parts)
    length = parts[0].shape[0]
    me = me_ref[0]
    block = 256
    for n in range(0, acc.shape[2], block):
        cols = slice(n, n + block)
        acc[:, :, cols] = mm_nt(dq_ref[...], wq_ref[cols, :]).reshape(acc.shape[0], length, block)
    for s, part in enumerate(parts):
        at = listed_ref[lax.rem(me + n_slot - s, n_slot)]
        acc[at] += part[...].astype(F32)
    out_ref[...] = acc[...].astype(BF)


def combine(me, listed, dq, wq, parts):
    length, width = parts[0].shape
    n_src = dq.shape[0] // length
    smem = pl.BlockSpec(memory_space=pltpu.SMEM)
    vmem = pl.BlockSpec(memory_space=pltpu.VMEM)
    return pl.pallas_call(
        combine_kernel,
        in_specs=[smem, smem] + [vmem] * (2 + len(parts)),
        out_specs=vmem,
        out_shape=jax.ShapeDtypeStruct((n_src, length, width), BF),
        scratch_shapes=[pltpu.VMEM((n_src, length, width), F32)],
        compiler_params=pltpu.CompilerParams(vmem_limit_bytes=24 * 2**20),
        cost_estimate=pl.CostEstimate(flops=2 * dq.size * width, bytes_accessed=6 * 2**20, transcendentals=0),
        name="combine",
    )(me, listed, dq, wq, *parts)


def spread_kernel(parts_ref, out_ref, *, factor):
    total = jnp.sum(parts_ref[...].astype(F32), axis=0)
    out_ref[...] = jnp.broadcast_to((total * factor).astype(BF)[None], out_ref.shape)


def spread(parts, copies, factor):
    shape = parts.shape[1:]
    grid = shape[0]
    return pl.pallas_call(
        functools.partial(spread_kernel, factor=factor),
        grid=(grid,),
        in_specs=[pl.BlockSpec((parts.shape[0], 1) + shape[1:], lambda i: (0, i, 0, 0))],
        out_specs=pl.BlockSpec((copies, 1) + shape[1:], lambda i: (0, i, 0, 0)),
        out_shape=jax.ShapeDtypeStruct((copies,) + shape, BF),
        compiler_params=pltpu.CompilerParams(vmem_limit_bytes=16 * 2**20),
        cost_estimate=pl.CostEstimate(flops=parts.size, bytes_accessed=4 * parts.size, transcendentals=0),
        name="spread",
    )(parts)


def place_kernel(half_ref, rows_ref, *rest):
    n = rows_ref.shape[1]
    for i, out in enumerate(rest[-n:]):
        out[0] = rows_ref[:, i]


def place(half, rows, into=()):
    pieces, n, each, width = rows.shape
    step = pieces // 4
    hbm = pl.BlockSpec(memory_space=pl.ANY)
    return pl.pallas_call(
        place_kernel,
        grid_spec=pltpu.PrefetchScalarGridSpec(
            num_scalar_prefetch=1,
            grid=(pieces // step,),
            in_specs=[pl.BlockSpec((step, n, each, width), lambda p, half: (p, 0, 0, 0))] + [hbm] * len(into),
            out_specs=[pl.BlockSpec((1, step, each, width), lambda p, half: (half[0], p, 0, 0))] * n,
        ),
        out_shape=[jax.ShapeDtypeStruct((2, pieces, each, width), BF)] * n,
        input_output_aliases={2 + i: i for i in range(len(into))},
        compiler_params=pltpu.CompilerParams(vmem_limit_bytes=16 * 2**20),
        cost_estimate=pl.CostEstimate(flops=0, bytes_accessed=4 * rows.size, transcendentals=0),
        name="place",
    )(half, rows, *into)


def body(sentences, cotangent, w_query, w_key, w_value, send_rows, pair_src, pair_slot, pair_valid):
    sent_dev, length, width = sentences.shape
    n_lang = lax.axis_size("lang")
    n_pair = lax.axis_size("pair")
    me = lax.axis_index("lang")
    listed = send_rows[0].reshape(-1)
    outgoing = jnp.take(sentences, listed, axis=0, mode="clip")
    received = lax.all_to_all(outgoing, "lang", split_axis=0, concat_axis=0, tiled=True)
    x = sentences.reshape(-1, width)
    c = cotangent.reshape(-1, width)
    where = me.reshape(1).astype(jnp.int32)
    attended, dq, keep, send, *dx = attend(
        where, pair_src, pair_slot, pair_valid, x, received, c, w_query, w_key, w_value, pieces=n_pair
    )
    other_core = [(i, i ^ 1) for i in range(n_lang)]
    other = lax.ppermute(send, "lang", other_core)
    back = [dx[0]]
    for s in range(1, n_lang):
        back.append(lax.ppermute(dx[s], "lang", [(i, (i + s) % n_lang) for i in range(n_lang)]))
    chip = (keep.astype(F32) + other.astype(F32)).astype(BF)
    pieces = lax.all_to_all(chip, "pair", split_axis=0, concat_axis=0, tiled=True)
    pieces, *back[1:6] = lax.optimization_barrier((pieces, *back[1:6]))
    n_y = n_lang // 2
    along_y = [[2 * y + core for y in range(n_y)] for core in range(2)]
    columns = lax.all_to_all(
        spread(pieces, n_y, 1.0), "lang", split_axis=0, concat_axis=0, axis_index_groups=along_y, tiled=True
    )
    factor = 1.0 / (sent_dev * n_lang * n_pair * length) ** 0.5
    near = lax.all_to_all(spread(columns, n_pair, factor), "pair", split_axis=0, concat_axis=0, tiled=True)
    near, *back[6:] = lax.optimization_barrier((near, *back[6:]))
    far = lax.ppermute(near, "lang", other_core)
    grad_sentences = combine(where, listed, dq, w_query, back)
    core = lax.rem(where, 2)
    grads = place(1 - core, far, place(core, near))
    grads = tuple(g.reshape(width, width) for g in grads)
    return (attended.reshape(sentences.shape), grad_sentences) + grads


def solution(mesh):
    split3, split2 = P(("lang", "pair"), None, None), P(("lang", "pair"), None)
    in_specs = (split3, split3, P(), P(), P(), split3, split2, split2, split2)
    out_specs = (split3, split3, P(), P(), P())
    return jax.shard_map(body, mesh=mesh, in_specs=in_specs, out_specs=out_specs, check_vma=False)
```

```python
import functools

import jax
import jax.numpy as jnp
from jax import lax
from jax.experimental import pallas as pl
from jax.experimental.pallas import tpu as pltpu
from jax.sharding import PartitionSpec as P

SIZE = 64
LANES = 128
BF, F32 = jnp.bfloat16, jnp.float32
NT = (((1,), (1,)), ((), ()))


def mm(a, b):
    return jnp.dot(a, b, preferred_element_type=F32)


def mm_nt(a, b):
    return lax.dot_general(a, b, NT, preferred_element_type=F32)


def attend_kernel(me_ref, src_ref, slot_ref, valid_ref, x_hbm, r_hbm, c_hbm, wq_hbm, wk_hbm, wv_hbm,
                  *rest, n_src, n_slot, length, lo, earlier):
    if earlier:
        (dk0_hbm, dv0_hbm), att_in, rest = rest[:2], rest[2], rest[3:]
        n_out = 4 + n_slot
    else:
        n_out = 6
    outs, scratch = rest[:n_out], rest[n_out:]
    att_hbm, dq_hbm, keep_hbm, send_hbm = outs[:4]
    (mult, x_ref, r_ref, c_ref, wq_ref, wk_ref, wv_ref, att_v, dq_v, gw_v,
     xt, rt, q2, g2, k_s, v_s, kt, vt, ot, dqt, dk_acc, dv_acc, sem_in, sem_r, sem_out) = scratch[:25]
    depth = x_ref.shape[1]
    width = c_ref.shape[1]
    heads = width // LANES
    n_pairs = src_ref.shape[-1]
    me = me_ref[0]
    block = 256
    mine = pl.ds(lo, width)

    copies = [pltpu.make_async_copy(a, b, sem_in.at[i]) for i, (a, b) in enumerate(
        ((x_hbm, x_ref), (wq_hbm.at[:, mine], wq_ref), (c_hbm.at[:, mine], c_ref),
         (wk_hbm.at[:, mine], wk_ref), (wv_hbm.at[:, mine], wv_ref)))]
    slots = [pltpu.make_async_copy(r_hbm.at[lax.rem(me + p, n_slot)], r_ref.at[pl.ds(p * length, length), :],
                                   sem_r.at[p]) for p in range(n_slot)]
    for c in copies[:4] + slots + copies[4:]:
        c.start()
    before = []
    if earlier:
        dk0, dv0, wk0, wv0, dx_v, sem_b = scratch[25:]
        old = pl.ds(0, lo)
        before = [pltpu.make_async_copy(a, b, sem_b.at[i]) for i, (a, b) in enumerate(
            ((dk0_hbm, dk0), (dv0_hbm, dv0), (wk_hbm.at[:, old], wk0), (wv_hbm.at[:, old], wv0)))]
        for c in before:
            c.start()

    for i in range(n_src * n_slot):
        mult[i] = 0
    for j in range(n_pairs):
        at = lax.rem(slot_ref[0, j] + n_slot - me, n_slot) * n_src + src_ref[0, j]
        mult[at] = mult[at] + valid_ref[0, j]
    ot[...] = jnp.zeros_like(ot)
    dqt[...] = jnp.zeros_like(dqt)
    dk_acc[...] = jnp.zeros_like(dk_acc)
    dv_acc[...] = jnp.zeros_like(dv_acc)

    for c in copies[:3]:
        c.wait()
    low = lax.broadcasted_iota(jnp.int32, (n_src * length, LANES), 1) < SIZE
    zero = jnp.zeros((n_src * length, LANES), BF)
    for n in range(0, width, block):
        q = mm(x_ref[...], wq_ref[:, n:n + block]).astype(BF) * BF(0.125)
        for h in range(n // LANES, (n + block) // LANES):
            qh = q[:, h * LANES - n:(h + 1) * LANES - n]
            gh = c_ref[:, h * LANES:(h + 1) * LANES]
            for ref, rows in ((q2, qh), (g2, gh)):
                top = jnp.where(low, rows, zero)
                bot = jnp.where(low, zero, rows)
                for s in range(n_src):
                    ref[s, h, :length, :] = top[s * length:(s + 1) * length]
                    ref[s, h, length:, :] = bot[s * length:(s + 1) * length]
    for s in range(n_src):
        xt[:, s * length:(s + 1) * length] = x_ref[s * length:(s + 1) * length, :].T

    copies[3].wait()
    for c in slots:
        c.wait()
    half = n_slot // 2
    for w_ref, nat, tra in ((wk_ref, k_s, kt), (wv_ref, v_s, vt)):
        if w_ref is wv_ref:
            copies[4].wait()
        for n in range(0, width, block):
            cols = slice(n, n + block)
            for lo in range(0, n_slot, half):
                k = mm(r_ref[lo * length:(lo + half) * length, :], w_ref[:, cols]).astype(BF)
                for t in range(half):
                    rows = k[t * length:(t + 1) * length]
                    nat[lo + t, :, cols] = rows
                    tra[lo + t, cols, :] = rows.T
    for t in range(n_slot):
        rt[:, t * length:(t + 1) * length] = r_ref[t * length:(t + 1) * length, :].T

    def combo(i, _):
        count = mult[i]

        @pl.when(count > 0)
        def _():
            t = i // n_src
            s = i % n_src
            m = count.astype(F32)

            def scores(h):
                cols = slice(h * LANES, (h + 1) * LANES)
                return mm_nt(k_s[t, :, cols], q2[s, h]), mm_nt(v_s[t, :, cols], g2[s, h])

            def soft(st, dp):
                e = jnp.exp(st - jnp.max(st, axis=0, keepdims=True))
                inv = 1.0 / jnp.sum(e, axis=0, keepdims=True)
                delta = jnp.sum(e * dp, axis=0, keepdims=True) * inv
                p = e * (inv * m)
                return p.astype(BF), (p * (dp - delta)).astype(BF)

            def grads(h, pb, ds):
                cols = slice(h * LANES, (h + 1) * LANES)
                dv = mm(pb, g2[s, h])
                dk = mm(ds, q2[s, h])
                o = mm(vt[t, cols, :], pb)
                dq = mm(kt[t, cols, :], ds)
                dv_acc[t, :, cols] += dv
                dk_acc[t, :, cols] += dk
                for part in range(2):
                    rows = slice(h * LANES + part * SIZE, h * LANES + (part + 1) * SIZE)
                    own = slice(part * SIZE, (part + 1) * SIZE)
                    keys = slice(part * length, (part + 1) * length)
                    ot[s, rows, :] += o[own, keys]
                    dqt[s, rows, :] += dq[own, keys]

            ready = [scores(h) for h in range(min(2, heads))]
            waiting = []
            for h in range(heads):
                if h + 2 < heads:
                    ready.append(scores(h + 2))
                waiting.append((h,) + soft(*ready.pop(0)))
                if h > 0:
                    grads(*waiting.pop(0))
            grads(*waiting.pop(0))
        return 0

    lax.fori_loop(0, n_src * n_slot, combo, 0)

    for t in range(n_slot):
        k_s[t] = dk_acc[t].astype(BF)
        v_s[t] = dv_acc[t].astype(BF)
    for s in range(n_src):
        dq_v[s * length:(s + 1) * length, :] = (dqt[s].T * 0.125).astype(BF)
    dk = k_s[...].reshape(n_slot * length, width)
    dv = v_s[...].reshape(n_slot * length, width)

    done = []

    def out(src, dst):
        c = pltpu.make_async_copy(src, dst, sem_out.at[len(done)])
        c.start()
        done.append(c)

    _, pieces, _, each, _ = gw_v.shape
    core = lax.rem(me, 2)
    for k, dst in enumerate((send_hbm, keep_hbm)):
        base = pl.multiple_of((core if k else 1 - core) * (pieces * each), LANES)
        rows = pl.ds(base, pieces * each)
        for n in range(0, width, block):
            cols = slice(n, n + block)
            for i, (lhs, rhs) in enumerate(((xt, dq_v[:, cols]), (rt, dk[:, cols]), (rt, dv[:, cols]))):
                gw_v[k, :, i, :, cols] = mm(lhs[rows, :], rhs).astype(BF).reshape(pieces, each, block)
        out(gw_v.at[k], dst)
        if k == 0:
            out(dq_v, dq_hbm)
            if not earlier:
                for t in range(n_slot):
                    out(k_s.at[t], outs[4].at[pl.ds(t * length, length), :])
                    out(v_s.at[t], outs[5].at[pl.ds(t * length, length), :])
    for s in range(n_src):
        att_v[s * length:(s + 1) * length, :] = ot[s].T.astype(BF)
    out(att_v, att_hbm.at[:, mine])
    if earlier:
        for c in before:
            c.wait()
        half = n_slot // 2
        for top in range(0, n_slot, half):
            rows = slice(top * length, (top + half) * length)
            for n in range(0, depth, block):
                cols = slice(n, n + block)
                dx = mm_nt(dk[rows], wk_ref[cols, :]) + mm_nt(dv[rows], wv_ref[cols, :])
                dx += mm_nt(dk0[rows, :], wk0[cols, :]) + mm_nt(dv0[rows, :], wv0[cols, :])
                dx_v[rows, cols] = dx.astype(BF)
            for t in range(top, top + half):
                out(dx_v.at[pl.ds(t * length, length), :], outs[4 + t])
    for c in done:
        c.wait()


def attend(me, src, slot, valid, x, r, c, wq, wk, wv, earlier=(), *, lo, width, pieces):
    n_slot, length, depth = r.shape
    rows = x.shape[0]
    n_src = rows // length
    each = depth // 2 // pieces
    heads = width // LANES
    smem = pl.BlockSpec(memory_space=pltpu.SMEM)
    hbm = pl.BlockSpec(memory_space=pltpu.HBM)
    shape = jax.ShapeDtypeStruct
    vm = pltpu.VMEM
    tall = (n_slot * length, width)
    out_shape = [shape((rows, depth), BF), shape((rows, width), BF)]
    out_shape += [shape((pieces, 3, each, width), BF)] * 2
    scratch = [
        pltpu.SMEM((n_src * n_slot,), jnp.int32),
        vm((rows, depth), BF), vm((n_slot * length, depth), BF), vm((rows, width), BF),
        vm((depth, width), BF), vm((depth, width), BF), vm((depth, width), BF),
        vm((rows, width), BF), vm((rows, width), BF), vm((2, pieces, 3, each, width), BF),
        vm((depth, rows), BF), vm((depth, n_slot * length), BF),
        vm((n_src, heads, 2 * length, LANES), BF), vm((n_src, heads, 2 * length, LANES), BF),
        vm((n_slot, length, width), BF), vm((n_slot, length, width), BF),
        vm((n_slot, width, length), BF), vm((n_slot, width, length), BF),
        vm((n_src, width, length), F32), vm((n_src, width, length), F32),
        vm((n_slot, length, width), F32), vm((n_slot, length, width), F32),
        pltpu.SemaphoreType.DMA((5,)), pltpu.SemaphoreType.DMA((n_slot,)),
        pltpu.SemaphoreType.DMA((4 + 2 * n_slot,)),
    ]
    if earlier:
        out_shape += [shape((length, depth), BF)] * n_slot
        scratch += [vm((n_slot * length, lo), BF), vm((n_slot * length, lo), BF), vm((depth, lo), BF),
                    vm((depth, lo), BF), vm((n_slot * length, depth), BF), pltpu.SemaphoreType.DMA((4,))]
    else:
        out_shape += [shape(tall, BF)] * 2
    macs = 2 * (n_src + 2 * n_slot) * length * depth * width + 12 * 6 * length * length * width
    return pl.pallas_call(
        functools.partial(attend_kernel, n_src=n_src, n_slot=n_slot, length=length, lo=lo, earlier=bool(earlier)),
        in_specs=[smem] * 4 + [hbm] * (6 + len(earlier)),
        out_specs=[hbm] * len(out_shape),
        out_shape=out_shape,
        scratch_shapes=scratch,
        input_output_aliases={12: 0} if earlier else {},
        compiler_params=pltpu.CompilerParams(vmem_limit_bytes=56 * 2**20),
        cost_estimate=pl.CostEstimate(flops=8 * macs, bytes_accessed=16 * 2**20, transcendentals=0),
        name="attend",
    )(me, src, slot, valid, x, r, c, wq, wk, wv, *earlier)


def combine_kernel(me_ref, listed_ref, dq0_ref, dq1_ref, wq_ref, *rest):
    parts, (out_ref, acc) = rest[:-2], rest[-2:]
    n_slot = len(parts)
    length = parts[0].shape[0]
    me = me_ref[0]
    block = 256
    lo = dq0_ref.shape[1]
    for n in range(0, acc.shape[2], block):
        cols = slice(n, n + block)
        dx = mm_nt(dq0_ref[...], wq_ref[cols, :lo]) + mm_nt(dq1_ref[...], wq_ref[cols, lo:])
        acc[:, :, cols] = dx.reshape(acc.shape[0], length, block)
    for s, part in enumerate(parts):
        at = listed_ref[lax.rem(me + n_slot - s, n_slot)]
        acc[at] += part[...].astype(F32)
    out_ref[...] = acc[...].astype(BF)


def combine(me, listed, dq, wq, parts):
    length, width = parts[0].shape
    n_src = dq[0].shape[0] // length
    smem = pl.BlockSpec(memory_space=pltpu.SMEM)
    vmem = pl.BlockSpec(memory_space=pltpu.VMEM)
    return pl.pallas_call(
        combine_kernel,
        in_specs=[smem, smem] + [vmem] * (3 + len(parts)),
        out_specs=vmem,
        out_shape=jax.ShapeDtypeStruct((n_src, length, width), BF),
        scratch_shapes=[pltpu.VMEM((n_src, length, width), F32)],
        compiler_params=pltpu.CompilerParams(vmem_limit_bytes=24 * 2**20),
        cost_estimate=pl.CostEstimate(flops=2 * wq.size * n_src * length, bytes_accessed=6 * 2**20, transcendentals=0),
        name="combine",
    )(me, listed, *dq, wq, *parts)


def spread_kernel(*refs, factor):
    out_ref = refs[-1]
    at = 0
    for ref in refs[:-1]:
        cols = slice(at, at + ref.shape[-1])
        total = jnp.sum(ref[...].astype(F32), axis=0)
        out_ref[:, :, :, cols] = jnp.broadcast_to((total * factor).astype(BF)[None], out_ref.shape[:3] + total.shape[-1:])
        at = cols.stop


def spread(parts, copies, factor):
    n, each = parts[0].shape[1:3]
    width = sum(p.shape[-1] for p in parts)
    spec = lambda count, w: pl.BlockSpec((count, 1, each, w), lambda i: (0, i, 0, 0))
    size = sum(p.size for p in parts)
    return pl.pallas_call(
        functools.partial(spread_kernel, factor=factor),
        grid=(n,),
        in_specs=[spec(p.shape[0], p.shape[-1]) for p in parts],
        out_specs=spec(copies, width),
        out_shape=jax.ShapeDtypeStruct((copies, n, each, width), BF),
        compiler_params=pltpu.CompilerParams(vmem_limit_bytes=16 * 2**20),
        cost_estimate=pl.CostEstimate(flops=size, bytes_accessed=4 * size, transcendentals=0),
        name="spread",
    )(*parts)


def place_kernel(half_ref, rows_ref, *rest):
    n = rows_ref.shape[1]
    for i, out in enumerate(rest[-n:]):
        out[0] = rows_ref[:, i]


def place(half, rows, into=()):
    pieces, n, each, width = rows.shape
    step = pieces // 4
    hbm = pl.BlockSpec(memory_space=pltpu.HBM)
    return pl.pallas_call(
        place_kernel,
        grid_spec=pltpu.PrefetchScalarGridSpec(
            num_scalar_prefetch=1,
            grid=(pieces // step,),
            in_specs=[pl.BlockSpec((step, n, each, width), lambda p, half: (p, 0, 0, 0))] + [hbm] * len(into),
            out_specs=[pl.BlockSpec((1, step, each, width), lambda p, half: (half[0], p, 0, 0))] * n,
        ),
        out_shape=[jax.ShapeDtypeStruct((2, pieces, each, width), BF)] * n,
        input_output_aliases={2 + i: i for i in range(len(into))},
        compiler_params=pltpu.CompilerParams(vmem_limit_bytes=16 * 2**20),
        cost_estimate=pl.CostEstimate(flops=0, bytes_accessed=4 * rows.size, transcendentals=0),
        name="place",
    )(half, rows, *into)


def body(sentences, cotangent, w_query, w_key, w_value, send_rows, pair_src, pair_slot, pair_valid):
    sent_dev, length, width = sentences.shape
    n_lang = lax.axis_size("lang")
    n_pair = lax.axis_size("pair")
    me = lax.axis_index("lang")
    listed = send_rows[0].reshape(-1)
    outgoing = jnp.take(sentences, listed, axis=0, mode="clip")
    received = lax.all_to_all(outgoing, "lang", split_axis=0, concat_axis=0, tiled=True)
    x = sentences.reshape(-1, width)
    c = cotangent.reshape(-1, width)
    where = me.reshape(1).astype(jnp.int32)
    other_core = [(i, i ^ 1) for i in range(n_lang)]

    def chip_sum(keep, send):
        other = lax.ppermute(send, "lang", other_core)
        return (keep.astype(F32) + other.astype(F32)).astype(BF)

    def over_pair(a):
        return lax.all_to_all(a, "pair", split_axis=0, concat_axis=0, tiled=True)

    half = width // 2
    pairs = (where, pair_src, pair_slot, pair_valid)
    attended, dq0, keep, send, dk0, dv0 = attend(
        *pairs, x, received, c, w_query, w_key, w_value, lo=0, width=half, pieces=n_pair
    )
    chip, x = lax.optimization_barrier((chip_sum(keep, send), x))
    pieces0 = over_pair(chip)
    attended, dq1, keep, send, *dx = attend(
        *pairs, x, received, c, w_query, w_key, w_value, (dk0, dv0, attended), lo=half, width=half, pieces=n_pair
    )
    pieces0, dq1, keep, send, *dx = lax.optimization_barrier((pieces0, dq1, keep, send, *dx))
    back = [dx[0]]
    for s in range(1, n_lang):
        back.append(lax.ppermute(dx[s], "lang", [(i, (i + s) % n_lang) for i in range(n_lang)]))
    pieces1 = over_pair(chip_sum(keep, send))
    pieces1, *back[1:6] = lax.optimization_barrier((pieces1, *back[1:6]))
    n_y = n_lang // 2
    along_y = [[2 * y + core for y in range(n_y)] for core in range(2)]
    columns = lax.all_to_all(
        spread((pieces0, pieces1), n_y, 1.0), "lang", split_axis=0, concat_axis=0, axis_index_groups=along_y, tiled=True
    )
    factor = 1.0 / (sent_dev * n_lang * n_pair * length) ** 0.5
    near = over_pair(spread((columns,), n_pair, factor))
    grad_sentences = combine(where, listed, (dq0, dq1), w_query, back)
    near, grad_sentences = lax.optimization_barrier((near, grad_sentences))
    far = lax.ppermute(near, "lang", other_core)
    core = lax.rem(where, 2)
    grads = place(1 - core, far, place(core, near))
    grads = tuple(g.reshape(width, width) for g in grads)
    return (attended.reshape(sentences.shape), grad_sentences) + grads


def solution(mesh):
    split3, split2 = P(("lang", "pair"), None, None), P(("lang", "pair"), None)
    in_specs = (split3, split3, P(), P(), P(), split3, split2, split2, split2)
    out_specs = (split3, split3, P(), P(), P())
    return jax.shard_map(body, mesh=mesh, in_specs=in_specs, out_specs=out_specs, check_vma=False)
```

```python
import functools

import jax
import jax.numpy as jnp
from jax import lax
from jax.experimental import pallas as pl
from jax.experimental.pallas import tpu as pltpu
from jax.sharding import PartitionSpec as P

SIZE = 64
LANES = 128
BF, F32 = jnp.bfloat16, jnp.float32
NT = (((1,), (1,)), ((), ()))


def mm(a, b):
    return jnp.dot(a, b, preferred_element_type=F32)


def mm_nt(a, b):
    return lax.dot_general(a, b, NT, preferred_element_type=F32)


def attend_kernel(me_ref, src_ref, slot_ref, valid_ref, x_hbm, r_hbm, c_hbm, wq_hbm, wk_hbm, wv_hbm,
                  *rest, n_src, n_slot, length):
    outs, scratch = rest[:4 + n_slot], rest[4 + n_slot:]
    att_hbm, dq_hbm, keep_hbm, send_hbm = outs[:4]
    dx_hbm = outs[4:]
    (mult, x_ref, r_ref, c_ref, wq_ref, wk_ref, wv_ref, att_v, dq_v, gw_v, dx_v,
     xt, rt, q2, g2, k_s, v_s, kt, vt, ot, dqt, dk_acc, dv_acc, sem_in, sem_r, sem_out) = scratch
    width = x_ref.shape[1]
    heads = width // LANES
    n_pairs = src_ref.shape[-1]
    me = me_ref[0]
    block = 256

    copies = [pltpu.make_async_copy(a, b, sem_in.at[i]) for i, (a, b) in enumerate(
        ((x_hbm, x_ref), (wq_hbm, wq_ref), (c_hbm, c_ref), (wk_hbm, wk_ref), (wv_hbm, wv_ref)))]
    slots = [pltpu.make_async_copy(r_hbm.at[lax.rem(me + p, n_slot)], r_ref.at[pl.ds(p * length, length), :],
                                   sem_r.at[p]) for p in range(n_slot)]
    for c in copies[:4] + slots + copies[4:]:
        c.start()

    for i in range(n_src * n_slot):
        mult[i] = 0
    for j in range(n_pairs):
        at = lax.rem(slot_ref[0, j] + n_slot - me, n_slot) * n_src + src_ref[0, j]
        mult[at] = mult[at] + valid_ref[0, j]
    ot[...] = jnp.zeros_like(ot)
    dqt[...] = jnp.zeros_like(dqt)
    dk_acc[...] = jnp.zeros_like(dk_acc)
    dv_acc[...] = jnp.zeros_like(dv_acc)

    for c in copies[:3]:
        c.wait()
    low = lax.broadcasted_iota(jnp.int32, (n_src * length, LANES), 1) < SIZE
    zero = jnp.zeros((n_src * length, LANES), BF)
    for n in range(0, width, block):
        q = mm(x_ref[...], wq_ref[:, n:n + block]).astype(BF) * BF(0.125)
        for h in range(n // LANES, (n + block) // LANES):
            qh = q[:, h * LANES - n:(h + 1) * LANES - n]
            gh = c_ref[:, h * LANES:(h + 1) * LANES]
            for ref, rows in ((q2, qh), (g2, gh)):
                top = jnp.where(low, rows, zero)
                bot = jnp.where(low, zero, rows)
                for s in range(n_src):
                    ref[s, h, :length, :] = top[s * length:(s + 1) * length]
                    ref[s, h, length:, :] = bot[s * length:(s + 1) * length]
    for s in range(n_src):
        xt[:, s * length:(s + 1) * length] = x_ref[s * length:(s + 1) * length, :].T

    copies[3].wait()
    for c in slots:
        c.wait()
    half = n_slot // 2
    for w_ref, nat, tra in ((wk_ref, k_s, kt), (wv_ref, v_s, vt)):
        if w_ref is wv_ref:
            copies[4].wait()
        for n in range(0, width, block):
            cols = slice(n, n + block)
            for lo in range(0, n_slot, half):
                k = mm(r_ref[lo * length:(lo + half) * length, :], w_ref[:, cols]).astype(BF)
                for t in range(half):
                    rows = k[t * length:(t + 1) * length]
                    nat[lo + t, :, cols] = rows
                    tra[lo + t, cols, :] = rows.T
    for t in range(n_slot):
        rt[:, t * length:(t + 1) * length] = r_ref[t * length:(t + 1) * length, :].T

    def combo(i, _):
        count = mult[i]

        @pl.when(count > 0)
        def _():
            t = i // n_src
            s = i % n_src
            m = count.astype(F32)

            def scores(h):
                cols = slice(h * LANES, (h + 1) * LANES)
                return mm_nt(k_s[t, :, cols], q2[s, h]), mm_nt(v_s[t, :, cols], g2[s, h])

            def soft(st, dp):
                e = jnp.exp(st - jnp.max(st, axis=0, keepdims=True))
                inv = 1.0 / jnp.sum(e, axis=0, keepdims=True)
                delta = jnp.sum(e * dp, axis=0, keepdims=True) * inv
                p = e * (inv * m)
                return p.astype(BF), (p * (dp - delta)).astype(BF)

            def grads(h, pb, ds):
                cols = slice(h * LANES, (h + 1) * LANES)
                dv = mm(pb, g2[s, h])
                dk = mm(ds, q2[s, h])
                o = mm(vt[t, cols, :], pb)
                dq = mm(kt[t, cols, :], ds)
                dv_acc[t, :, cols] += dv
                dk_acc[t, :, cols] += dk
                for part in range(2):
                    rows = slice(h * LANES + part * SIZE, h * LANES + (part + 1) * SIZE)
                    own = slice(part * SIZE, (part + 1) * SIZE)
                    keys = slice(part * length, (part + 1) * length)
                    ot[s, rows, :] += o[own, keys]
                    dqt[s, rows, :] += dq[own, keys]

            ready = [scores(h) for h in range(min(2, heads))]
            waiting = []
            for h in range(heads):
                if h + 2 < heads:
                    ready.append(scores(h + 2))
                waiting.append((h,) + soft(*ready.pop(0)))
                if h > 0:
                    grads(*waiting.pop(0))
            grads(*waiting.pop(0))
        return 0

    lax.fori_loop(0, n_src * n_slot, combo, 0)

    for t in range(n_slot):
        k_s[t] = dk_acc[t].astype(BF)
        v_s[t] = dv_acc[t].astype(BF)
    for s in range(n_src):
        dq_v[s * length:(s + 1) * length, :] = (dqt[s].T * 0.125).astype(BF)
    dk = k_s[...].reshape(n_slot * length, width)
    dv = v_s[...].reshape(n_slot * length, width)

    done = []

    def out(src, dst):
        c = pltpu.make_async_copy(src, dst, sem_out.at[len(done)])
        c.start()
        done.append(c)

    _, pieces, _, each, _ = gw_v.shape
    core = lax.rem(me, 2)
    for k, dst in enumerate((send_hbm, keep_hbm)):
        base = pl.multiple_of((core if k else 1 - core) * (pieces * each), LANES)
        rows = pl.ds(base, pieces * each)
        for n in range(0, width, block):
            cols = slice(n, n + block)
            for i, (lhs, rhs) in enumerate(((xt, dq_v[:, cols]), (rt, dk[:, cols]), (rt, dv[:, cols]))):
                gw_v[k, :, i, :, cols] = mm(lhs[rows, :], rhs).astype(BF).reshape(pieces, each, block)
        out(gw_v.at[k], dst)
        if k == 0:
            out(dq_v, dq_hbm)
    for s in range(n_src):
        att_v[s * length:(s + 1) * length, :] = ot[s].T.astype(BF)
    out(att_v, att_hbm)
    for lo in range(0, n_slot, half):
        rows = slice(lo * length, (lo + half) * length)
        for n in range(0, width, block):
            cols = slice(n, n + block)
            dx_v[rows, cols] = (mm_nt(dk[rows], wk_ref[cols, :]) + mm_nt(dv[rows], wv_ref[cols, :])).astype(BF)
        for t in range(lo, lo + half):
            out(dx_v.at[pl.ds(t * length, length), :], dx_hbm[t])
    for c in done:
        c.wait()


def attend(me, src, slot, valid, x, r, c, wq, wk, wv, *, pieces):
    n_slot, length, width = r.shape
    rows = x.shape[0]
    n_src = rows // length
    each = width // 2 // pieces
    heads = width // LANES
    smem = pl.BlockSpec(memory_space=pltpu.SMEM)
    hbm = pl.BlockSpec(memory_space=pltpu.HBM)
    shape = jax.ShapeDtypeStruct
    vm = pltpu.VMEM
    macs = 2 * (n_src + 3 * n_slot) * length * width * width + 12 * 6 * length * length * width
    return pl.pallas_call(
        functools.partial(attend_kernel, n_src=n_src, n_slot=n_slot, length=length),
        in_specs=[smem] * 4 + [hbm] * 6,
        out_specs=[hbm] * (4 + n_slot),
        out_shape=[shape((rows, width), BF), shape((rows, width), BF),
                   shape((pieces, 3, each, width), BF), shape((pieces, 3, each, width), BF)]
        + [shape((length, width), BF)] * n_slot,
        scratch_shapes=[
            pltpu.SMEM((n_src * n_slot,), jnp.int32),
            vm((rows, width), BF), vm((n_slot * length, width), BF), vm((rows, width), BF),
            vm((width, width), BF), vm((width, width), BF), vm((width, width), BF),
            vm((rows, width), BF), vm((rows, width), BF),
            vm((2, pieces, 3, each, width), BF), vm((n_slot * length, width), BF),
            vm((width, rows), BF), vm((width, n_slot * length), BF),
            vm((n_src, heads, 2 * length, LANES), BF), vm((n_src, heads, 2 * length, LANES), BF),
            vm((n_slot, length, width), BF), vm((n_slot, length, width), BF),
            vm((n_slot, width, length), BF), vm((n_slot, width, length), BF),
            vm((n_src, width, length), F32), vm((n_src, width, length), F32),
            vm((n_slot, length, width), F32), vm((n_slot, length, width), F32),
            pltpu.SemaphoreType.DMA((5,)), pltpu.SemaphoreType.DMA((n_slot,)),
            pltpu.SemaphoreType.DMA((4 + n_slot,)),
        ],
        compiler_params=pltpu.CompilerParams(vmem_limit_bytes=60 * 2**20),
        cost_estimate=pl.CostEstimate(flops=4 * macs, bytes_accessed=20 * 2**20, transcendentals=0),
        name="attend",
    )(me, src, slot, valid, x, r, c, wq, wk, wv)


def combine_kernel(me_ref, listed_ref, dq_hbm, wq_hbm, *rest):
    n_slot = len(rest) - 6
    parts, (out_ref, acc, dq_ref, wq_ref, back, sem) = rest[:n_slot], rest[n_slot:]
    length = back.shape[1]
    me = me_ref[0]
    block = 256
    copies = [pltpu.make_async_copy(a, b, sem.at[i]) for i, (a, b) in enumerate(
        [(dq_hbm, dq_ref), (wq_hbm, wq_ref)] + [(p, back.at[s]) for s, p in enumerate(parts)])]
    for c in copies:
        c.start()
    for c in copies:
        c.wait()
    for n in range(0, acc.shape[2], block):
        cols = slice(n, n + block)
        acc[:, :, cols] = mm_nt(dq_ref[...], wq_ref[cols, :]).reshape(acc.shape[0], length, block)
    for s in range(n_slot):
        at = listed_ref[lax.rem(me + n_slot - s, n_slot)]
        acc[at] += back[s].astype(F32)
    out_ref[...] = acc[...].astype(BF)


def combine(me, listed, dq, wq, parts):
    length, width = parts[0].shape
    n_src = dq.shape[0] // length
    smem = pl.BlockSpec(memory_space=pltpu.SMEM)
    hbm = pl.BlockSpec(memory_space=pltpu.HBM)
    return pl.pallas_call(
        combine_kernel,
        in_specs=[smem, smem] + [hbm] * (2 + len(parts)),
        out_specs=pl.BlockSpec(memory_space=pltpu.VMEM),
        out_shape=jax.ShapeDtypeStruct((n_src, length, width), BF),
        scratch_shapes=[
            pltpu.VMEM((n_src, length, width), F32), pltpu.VMEM(dq.shape, BF), pltpu.VMEM(wq.shape, BF),
            pltpu.VMEM((len(parts), length, width), BF), pltpu.SemaphoreType.DMA((2 + len(parts),)),
        ],
        compiler_params=pltpu.CompilerParams(vmem_limit_bytes=60 * 2**20),
        cost_estimate=pl.CostEstimate(flops=2 * dq.size * width, bytes_accessed=6 * 2**20, transcendentals=0),
        name="combine",
    )(me, listed, dq, wq, *parts)


def pick_kernel(listed_ref, x_hbm, out_hbm, x_ref, sem):
    load = pltpu.make_async_copy(x_hbm, x_ref, sem.at[0])
    load.start()
    load.wait()
    n = out_hbm.shape[0]
    stores = [pltpu.make_async_copy(x_ref.at[listed_ref[i]], out_hbm.at[i], sem.at[1 + i]) for i in range(n)]
    for c in stores:
        c.start()
    for c in stores:
        c.wait()


def pick(listed, x):
    n = listed.shape[0]
    hbm = pl.BlockSpec(memory_space=pltpu.HBM)
    return pl.pallas_call(
        pick_kernel,
        in_specs=[pl.BlockSpec(memory_space=pltpu.SMEM), hbm],
        out_specs=hbm,
        out_shape=jax.ShapeDtypeStruct((n,) + x.shape[1:], x.dtype),
        scratch_shapes=[pltpu.VMEM(x.shape, x.dtype), pltpu.SemaphoreType.DMA((1 + n,))],
        compiler_params=pltpu.CompilerParams(vmem_limit_bytes=60 * 2**20),
        name="pick",
    )(listed, x)


def sum_kernel(parts_ref, out_ref):
    out_ref[...] = jnp.sum(parts_ref[...].astype(F32), axis=0).astype(BF)


def sum_parts(parts):
    count, n, each, width = parts.shape
    return pl.pallas_call(
        sum_kernel,
        grid=(n,),
        in_specs=[pl.BlockSpec((count, 1, each, width), lambda i: (0, i, 0, 0))],
        out_specs=pl.BlockSpec((1, each, width), lambda i: (i, 0, 0)),
        out_shape=jax.ShapeDtypeStruct((n, each, width), BF),
        compiler_params=pltpu.CompilerParams(vmem_limit_bytes=16 * 2**20),
        cost_estimate=pl.CostEstimate(flops=parts.size, bytes_accessed=2 * parts.size, transcendentals=0),
        name="sum_parts",
    )(parts)


def spread_kernel(a_ref, b_ref, c_ref, d_ref, out_ref, *, factor):
    a, b, c, d = (ref[...].astype(F32) for ref in (a_ref, b_ref, c_ref, d_ref))
    total = (a + c) + (b + d)
    out_ref[...] = jnp.broadcast_to((total * factor).astype(BF)[None], out_ref.shape)


def spread(parts, copies, factor):
    n, each, width = parts[0].shape
    return pl.pallas_call(
        functools.partial(spread_kernel, factor=factor),
        grid=(n,),
        in_specs=[pl.BlockSpec((1, each, width), lambda i: (i, 0, 0))] * len(parts),
        out_specs=pl.BlockSpec((copies, 1, each, width), lambda i: (0, i, 0, 0)),
        out_shape=jax.ShapeDtypeStruct((copies, n, each, width), BF),
        compiler_params=pltpu.CompilerParams(vmem_limit_bytes=60 * 2**20),
        cost_estimate=pl.CostEstimate(flops=4 * parts[0].size, bytes_accessed=2 * copies * parts[0].size, transcendentals=0),
        name="spread",
    )(*parts)


def place_kernel(half_ref, rows_ref, *rest):
    n = rows_ref.shape[1]
    for i, out in enumerate(rest[-n:]):
        out[0] = rows_ref[:, i]


def place(half, rows, into=()):
    pieces, n, each, width = rows.shape
    step = pieces // 4
    hbm = pl.BlockSpec(memory_space=pl.ANY)
    return pl.pallas_call(
        place_kernel,
        grid_spec=pltpu.PrefetchScalarGridSpec(
            num_scalar_prefetch=1,
            grid=(pieces // step,),
            in_specs=[pl.BlockSpec((step, n, each, width), lambda p, half: (p, 0, 0, 0))] + [hbm] * len(into),
            out_specs=[pl.BlockSpec((1, step, each, width), lambda p, half: (half[0], p, 0, 0))] * n,
        ),
        out_shape=[jax.ShapeDtypeStruct((2, pieces, each, width), BF)] * n,
        input_output_aliases={2 + i: i for i in range(len(into))},
        compiler_params=pltpu.CompilerParams(vmem_limit_bytes=16 * 2**20),
        cost_estimate=pl.CostEstimate(flops=0, bytes_accessed=4 * rows.size, transcendentals=0),
        name="place",
    )(half, rows, *into)


def body(sentences, cotangent, w_query, w_key, w_value, send_rows, pair_src, pair_slot, pair_valid):
    sent_dev, length, width = sentences.shape
    n_lang = lax.axis_size("lang")
    n_pair = lax.axis_size("pair")
    me = lax.axis_index("lang")
    listed = send_rows[0].reshape(-1)
    outgoing = pick(listed, sentences)
    received = lax.all_to_all(outgoing, "lang", split_axis=0, concat_axis=0, tiled=True)
    x = sentences.reshape(-1, width)
    c = cotangent.reshape(-1, width)
    where = me.reshape(1).astype(jnp.int32)
    attended, dq, keep, send, *dx = attend(
        where, pair_src, pair_slot, pair_valid, x, received, c, w_query, w_key, w_value, pieces=n_pair
    )
    other_core = [(i, i ^ 1) for i in range(n_lang)]
    other = lax.ppermute(send, "lang", other_core)
    back = [dx[0]]
    for s in range(1, n_lang):
        back.append(lax.ppermute(dx[s], "lang", [(i, (i + s) % n_lang) for i in range(n_lang)]))
    chip = (keep.astype(F32) + other.astype(F32)).astype(BF)
    pieces = lax.all_to_all(chip, "pair", split_axis=0, concat_axis=0, tiled=True)
    pieces, *back[1:4] = lax.optimization_barrier((pieces, *back[1:4]))
    plane = sum_parts(pieces)
    rings = [plane]
    for y in range(1, n_lang // 2):
        rings.append(lax.ppermute(plane, "lang", [(i, (i + 2 * y) % n_lang) for i in range(n_lang)]))
    factor = 1.0 / (sent_dev * n_lang * n_pair * length) ** 0.5
    near = lax.all_to_all(spread(rings, n_pair, factor), "pair", split_axis=0, concat_axis=0, tiled=True)
    grad_sentences = combine(where, listed, dq, w_query, back)
    near, grad_sentences = lax.optimization_barrier((near, grad_sentences))
    far = lax.ppermute(near, "lang", other_core)
    core = lax.rem(where, 2)
    grads = place(1 - core, far, place(core, near))
    grads = tuple(g.reshape(width, width) for g in grads)
    return (attended.reshape(sentences.shape), grad_sentences) + grads


def solution(mesh):
    split3, split2 = P(("lang", "pair"), None, None), P(("lang", "pair"), None)
    in_specs = (split3, split3, P(), P(), P(), split3, split2, split2, split2)
    out_specs = (split3, split3, P(), P(), P())
    return jax.shard_map(body, mesh=mesh, in_specs=in_specs, out_specs=out_specs, check_vma=False)
```

```python
import functools

import jax
import jax.numpy as jnp
from jax import lax
from jax.experimental import pallas as pl
from jax.experimental.pallas import tpu as pltpu
from jax.sharding import PartitionSpec as P

SIZE = 64
LANES = 128
BF, F32 = jnp.bfloat16, jnp.float32
NT = (((1,), (1,)), ((), ()))


def mm(a, b):
    return jnp.dot(a, b, preferred_element_type=F32)


def mm_nt(a, b):
    return lax.dot_general(a, b, NT, preferred_element_type=F32)


def attend_kernel(me_ref, src_ref, slot_ref, valid_ref, x_hbm, r_hbm, c_hbm, wq_hbm, wk_hbm, wv_hbm,
                  *rest, n_src, n_slot, length):
    outs, scratch = rest[:4 + n_slot], rest[4 + n_slot:]
    att_hbm, dq_hbm, keep_hbm, send_hbm = outs[:4]
    dx_hbm = outs[4:]
    (mult, x_ref, r_ref, c_ref, wq_ref, wk_ref, wv_ref, att_v, dq_v, gw_v, dx_v,
     xt, rt, q2, g2, k_s, v_s, kt, vt, ot, dqt, dk_acc, dv_acc, sem_in, sem_r, sem_out) = scratch
    width = x_ref.shape[1]
    heads = width // LANES
    n_pairs = src_ref.shape[-1]
    me = me_ref[0]
    block = 256

    copies = [pltpu.make_async_copy(a, b, sem_in.at[i]) for i, (a, b) in enumerate(
        ((x_hbm, x_ref), (wq_hbm, wq_ref), (c_hbm, c_ref), (wk_hbm, wk_ref), (wv_hbm, wv_ref)))]
    slots = [pltpu.make_async_copy(r_hbm.at[lax.rem(me + p, n_slot)], r_ref.at[pl.ds(p * length, length), :],
                                   sem_r.at[p]) for p in range(n_slot)]
    for c in copies[:4] + slots + copies[4:]:
        c.start()

    for i in range(n_src * n_slot):
        mult[i] = 0
    for j in range(n_pairs):
        at = lax.rem(slot_ref[0, j] + n_slot - me, n_slot) * n_src + src_ref[0, j]
        mult[at] = mult[at] + valid_ref[0, j]
    ot[...] = jnp.zeros_like(ot)
    dqt[...] = jnp.zeros_like(dqt)
    dk_acc[...] = jnp.zeros_like(dk_acc)
    dv_acc[...] = jnp.zeros_like(dv_acc)

    for c in copies[:3]:
        c.wait()
    low = lax.broadcasted_iota(jnp.int32, (n_src * length, LANES), 1) < SIZE
    zero = jnp.zeros((n_src * length, LANES), BF)
    for n in range(0, width, block):
        q = mm(x_ref[...], wq_ref[:, n:n + block]).astype(BF) * BF(0.125)
        for h in range(n // LANES, (n + block) // LANES):
            qh = q[:, h * LANES - n:(h + 1) * LANES - n]
            gh = c_ref[:, h * LANES:(h + 1) * LANES]
            for ref, rows in ((q2, qh), (g2, gh)):
                top = jnp.where(low, rows, zero)
                bot = jnp.where(low, zero, rows)
                for s in range(n_src):
                    ref[s, h, :length, :] = top[s * length:(s + 1) * length]
                    ref[s, h, length:, :] = bot[s * length:(s + 1) * length]
    for s in range(n_src):
        xt[:, s * length:(s + 1) * length] = x_ref[s * length:(s + 1) * length, :].T

    copies[3].wait()
    for c in slots:
        c.wait()
    half = n_slot // 2
    for w_ref, nat, tra in ((wk_ref, k_s, kt), (wv_ref, v_s, vt)):
        if w_ref is wv_ref:
            copies[4].wait()
        for n in range(0, width, block):
            cols = slice(n, n + block)
            for lo in range(0, n_slot, half):
                k = mm(r_ref[lo * length:(lo + half) * length, :], w_ref[:, cols]).astype(BF)
                for t in range(half):
                    rows = k[t * length:(t + 1) * length]
                    nat[lo + t, :, cols] = rows
                    tra[lo + t, cols, :] = rows.T
    for t in range(n_slot):
        rt[:, t * length:(t + 1) * length] = r_ref[t * length:(t + 1) * length, :].T

    def combo(i, _):
        count = mult[i]

        @pl.when(count > 0)
        def _():
            t = i // n_src
            s = i % n_src
            m = count.astype(F32)

            def scores(h):
                cols = slice(h * LANES, (h + 1) * LANES)
                return mm_nt(k_s[t, :, cols], q2[s, h]), mm_nt(v_s[t, :, cols], g2[s, h])

            def soft(st, dp):
                e = jnp.exp(st - jnp.max(st, axis=0, keepdims=True))
                inv = 1.0 / jnp.sum(e, axis=0, keepdims=True)
                delta = jnp.sum(e * dp, axis=0, keepdims=True) * inv
                p = e * (inv * m)
                return p.astype(BF), (p * (dp - delta)).astype(BF)

            def grads(h, pb, ds):
                cols = slice(h * LANES, (h + 1) * LANES)
                dv = mm(pb, g2[s, h])
                dk = mm(ds, q2[s, h])
                o = mm(vt[t, cols, :], pb)
                dq = mm(kt[t, cols, :], ds)
                dv_acc[t, :, cols] += dv
                dk_acc[t, :, cols] += dk
                for part in range(2):
                    rows = slice(h * LANES + part * SIZE, h * LANES + (part + 1) * SIZE)
                    own = slice(part * SIZE, (part + 1) * SIZE)
                    keys = slice(part * length, (part + 1) * length)
                    ot[s, rows, :] += o[own, keys]
                    dqt[s, rows, :] += dq[own, keys]

            ready = [scores(h) for h in range(min(2, heads))]
            waiting = []
            for h in range(heads):
                if h + 2 < heads:
                    ready.append(scores(h + 2))
                waiting.append((h,) + soft(*ready.pop(0)))
                if h > 0:
                    grads(*waiting.pop(0))
            grads(*waiting.pop(0))
        return 0

    lax.fori_loop(0, n_src * n_slot, combo, 0)

    for t in range(n_slot):
        k_s[t] = dk_acc[t].astype(BF)
        v_s[t] = dv_acc[t].astype(BF)
    for s in range(n_src):
        dq_v[s * length:(s + 1) * length, :] = (dqt[s].T * 0.125).astype(BF)
    dk = k_s[...].reshape(n_slot * length, width)
    dv = v_s[...].reshape(n_slot * length, width)

    done = []

    def out(src, dst):
        c = pltpu.make_async_copy(src, dst, sem_out.at[len(done)])
        c.start()
        done.append(c)

    _, _, _, pieces, _, each, part = gw_v.shape
    core = lax.rem(me, 2)
    for k, dst in enumerate((send_hbm, keep_hbm)):
        base = pl.multiple_of((core if k else 1 - core) * (2 * pieces * each), LANES)
        rows = pl.ds(base, 2 * pieces * each)
        for n in range(0, width, block):
            cols = slice(n, n + block)
            for i, (lhs, rhs) in enumerate(((xt, dq_v[:, cols]), (rt, dk[:, cols]), (rt, dv[:, cols]))):
                g = mm(lhs[rows, :], rhs).astype(BF).reshape(pieces, 2, each, block)
                for up in range(2):
                    gw_v[k, up, n // part, :, i, :, n % part:n % part + block] = g[:, up]
        out(gw_v.at[k], dst)
        if k == 0:
            out(dq_v, dq_hbm)
    for s in range(n_src):
        att_v[s * length:(s + 1) * length, :] = ot[s].T.astype(BF)
    out(att_v, att_hbm)
    for lo in range(0, n_slot, half):
        rows = slice(lo * length, (lo + half) * length)
        for n in range(0, width, block):
            cols = slice(n, n + block)
            dx_v[rows, cols] = (mm_nt(dk[rows], wk_ref[cols, :]) + mm_nt(dv[rows], wv_ref[cols, :])).astype(BF)
        for t in range(lo, lo + half):
            out(dx_v.at[pl.ds(t * length, length), :], dx_hbm[t])
    for c in done:
        c.wait()


def attend(me, src, slot, valid, x, r, c, wq, wk, wv, *, pieces):
    n_slot, length, width = r.shape
    rows = x.shape[0]
    n_src = rows // length
    each = width // 4 // pieces
    share = (2, 2, pieces, 3, each, width // 2)
    heads = width // LANES
    smem = pl.BlockSpec(memory_space=pltpu.SMEM)
    hbm = pl.BlockSpec(memory_space=pltpu.HBM)
    shape = jax.ShapeDtypeStruct
    vm = pltpu.VMEM
    macs = 2 * (n_src + 3 * n_slot) * length * width * width + 12 * 6 * length * length * width
    return pl.pallas_call(
        functools.partial(attend_kernel, n_src=n_src, n_slot=n_slot, length=length),
        in_specs=[smem] * 4 + [hbm] * 6,
        out_specs=[hbm] * (4 + n_slot),
        out_shape=[shape((rows, width), BF), shape((rows, width), BF),
                   shape(share, BF), shape(share, BF)]
        + [shape((length, width), BF)] * n_slot,
        scratch_shapes=[
            pltpu.SMEM((n_src * n_slot,), jnp.int32),
            vm((rows, width), BF), vm((n_slot * length, width), BF), vm((rows, width), BF),
            vm((width, width), BF), vm((width, width), BF), vm((width, width), BF),
            vm((rows, width), BF), vm((rows, width), BF),
            vm((2,) + share, BF), vm((n_slot * length, width), BF),
            vm((width, rows), BF), vm((width, n_slot * length), BF),
            vm((n_src, heads, 2 * length, LANES), BF), vm((n_src, heads, 2 * length, LANES), BF),
            vm((n_slot, length, width), BF), vm((n_slot, length, width), BF),
            vm((n_slot, width, length), BF), vm((n_slot, width, length), BF),
            vm((n_src, width, length), F32), vm((n_src, width, length), F32),
            vm((n_slot, length, width), F32), vm((n_slot, length, width), F32),
            pltpu.SemaphoreType.DMA((5,)), pltpu.SemaphoreType.DMA((n_slot,)),
            pltpu.SemaphoreType.DMA((4 + n_slot,)),
        ],
        compiler_params=pltpu.CompilerParams(vmem_limit_bytes=60 * 2**20),
        cost_estimate=pl.CostEstimate(flops=4 * macs, bytes_accessed=20 * 2**20, transcendentals=0),
        name="attend",
    )(me, src, slot, valid, x, r, c, wq, wk, wv)


def combine_kernel(me_ref, listed_ref, dq_hbm, wq_hbm, *rest):
    n_slot = len(rest) - 6
    parts, (out_ref, acc, dq_ref, wq_ref, back, sem) = rest[:n_slot], rest[n_slot:]
    length = back.shape[1]
    me = me_ref[0]
    block = 256
    copies = [pltpu.make_async_copy(a, b, sem.at[i]) for i, (a, b) in enumerate(
        [(dq_hbm, dq_ref), (wq_hbm, wq_ref)] + [(p, back.at[s]) for s, p in enumerate(parts)])]
    for c in copies:
        c.start()
    for c in copies:
        c.wait()
    for n in range(0, acc.shape[2], block):
        cols = slice(n, n + block)
        acc[:, :, cols] = mm_nt(dq_ref[...], wq_ref[cols, :]).reshape(acc.shape[0], length, block)
    for s in range(n_slot):
        at = listed_ref[lax.rem(me + n_slot - s, n_slot)]
        acc[at] += back[s].astype(F32)
    out_ref[...] = acc[...].astype(BF)


def combine(me, listed, dq, wq, parts):
    length, width = parts[0].shape
    n_src = dq.shape[0] // length
    smem = pl.BlockSpec(memory_space=pltpu.SMEM)
    hbm = pl.BlockSpec(memory_space=pltpu.HBM)
    return pl.pallas_call(
        combine_kernel,
        in_specs=[smem, smem] + [hbm] * (2 + len(parts)),
        out_specs=pl.BlockSpec(memory_space=pltpu.VMEM),
        out_shape=jax.ShapeDtypeStruct((n_src, length, width), BF),
        scratch_shapes=[
            pltpu.VMEM((n_src, length, width), F32), pltpu.VMEM(dq.shape, BF), pltpu.VMEM(wq.shape, BF),
            pltpu.VMEM((len(parts), length, width), BF), pltpu.SemaphoreType.DMA((2 + len(parts),)),
        ],
        compiler_params=pltpu.CompilerParams(vmem_limit_bytes=60 * 2**20),
        cost_estimate=pl.CostEstimate(flops=2 * dq.size * width, bytes_accessed=6 * 2**20, transcendentals=0),
        name="combine",
    )(me, listed, dq, wq, *parts)


def pick_kernel(listed_ref, x_hbm, out_hbm, x_ref, sem):
    load = pltpu.make_async_copy(x_hbm, x_ref, sem.at[0])
    load.start()
    load.wait()
    n = out_hbm.shape[0]
    stores = [pltpu.make_async_copy(x_ref.at[listed_ref[i]], out_hbm.at[i], sem.at[1 + i]) for i in range(n)]
    for c in stores:
        c.start()
    for c in stores:
        c.wait()


def pick(listed, x):
    n = listed.shape[0]
    hbm = pl.BlockSpec(memory_space=pltpu.HBM)
    return pl.pallas_call(
        pick_kernel,
        in_specs=[pl.BlockSpec(memory_space=pltpu.SMEM), hbm],
        out_specs=hbm,
        out_shape=jax.ShapeDtypeStruct((n,) + x.shape[1:], x.dtype),
        scratch_shapes=[pltpu.VMEM(x.shape, x.dtype), pltpu.SemaphoreType.DMA((1 + n,))],
        compiler_params=pltpu.CompilerParams(vmem_limit_bytes=60 * 2**20),
        name="pick",
    )(listed, x)


def add_kernel(a_ref, b_ref, out_ref):
    out_ref[...] = (a_ref[...].astype(F32) + b_ref[...].astype(F32)).astype(BF)


def add(a, b):
    count, n, each, width = a.shape
    spec = pl.BlockSpec((count // 4, n, each, width), lambda i: (i, 0, 0, 0))
    return pl.pallas_call(
        add_kernel,
        grid=(4,),
        in_specs=[spec, spec],
        out_specs=spec,
        out_shape=jax.ShapeDtypeStruct(a.shape, BF),
        compiler_params=pltpu.CompilerParams(vmem_limit_bytes=16 * 2**20),
        cost_estimate=pl.CostEstimate(flops=a.size, bytes_accessed=6 * a.size, transcendentals=0),
        name="add",
    )(a, b)


def spread_kernel(parts_ref, out_ref, *, factor):
    total = jnp.sum(parts_ref[...].astype(F32), axis=0) * factor
    out_ref[...] = jnp.broadcast_to(total.astype(BF)[None], out_ref.shape)


def spread(parts, factor):
    count, n, each, width = parts.shape
    spec = pl.BlockSpec((count, 1, each, width), lambda i: (0, i, 0, 0))
    return pl.pallas_call(
        functools.partial(spread_kernel, factor=factor),
        grid=(n,),
        in_specs=[spec],
        out_specs=spec,
        out_shape=jax.ShapeDtypeStruct(parts.shape, BF),
        compiler_params=pltpu.CompilerParams(vmem_limit_bytes=16 * 2**20),
        cost_estimate=pl.CostEstimate(flops=parts.size, bytes_accessed=4 * parts.size, transcendentals=0),
        name="spread",
    )(parts)


def place_kernel(half_ref, rows_ref, *rest):
    n = rows_ref.shape[3]
    width = rows_ref.shape[5]
    for i, out in enumerate(rest[-n:]):
        for up in range(2):
            for right in range(2):
                out[0, :, up, :, right * width:(right + 1) * width] = rows_ref[up, right, :, i]


def place(half, rows, into=()):
    _, _, pieces, n, each, width = rows.shape
    step = pieces // 4
    hbm = pl.BlockSpec(memory_space=pl.ANY)
    return pl.pallas_call(
        place_kernel,
        grid_spec=pltpu.PrefetchScalarGridSpec(
            num_scalar_prefetch=1,
            grid=(pieces // step,),
            in_specs=[pl.BlockSpec((2, 2, step, n, each, width), lambda p, half: (0, 0, p, 0, 0, 0))] + [hbm] * len(into),
            out_specs=[pl.BlockSpec((1, step, 2, each, 2 * width), lambda p, half: (half[0], p, 0, 0, 0))] * n,
        ),
        out_shape=[jax.ShapeDtypeStruct((2, pieces, 2, each, 2 * width), BF)] * n,
        input_output_aliases={2 + i: i for i in range(len(into))},
        compiler_params=pltpu.CompilerParams(vmem_limit_bytes=16 * 2**20),
        cost_estimate=pl.CostEstimate(flops=0, bytes_accessed=4 * rows.size, transcendentals=0),
        name="place",
    )(half, rows, *into)


def body(sentences, cotangent, w_query, w_key, w_value, send_rows, pair_src, pair_slot, pair_valid):
    sent_dev, length, width = sentences.shape
    n_lang = lax.axis_size("lang")
    n_pair = lax.axis_size("pair")
    me = lax.axis_index("lang")
    listed = send_rows[0].reshape(-1)
    outgoing = pick(listed, sentences)
    received = lax.all_to_all(outgoing, "lang", split_axis=0, concat_axis=0, tiled=True)
    x = sentences.reshape(-1, width)
    c = cotangent.reshape(-1, width)
    where = me.reshape(1).astype(jnp.int32)
    attended, dq, keep, send, *dx = attend(
        where, pair_src, pair_slot, pair_valid, x, received, c, w_query, w_key, w_value, pieces=n_pair
    )
    other_core = [(i, i ^ 1) for i in range(n_lang)]
    other = lax.ppermute(send, "lang", other_core)
    back = [dx[0]]
    for s in range(1, n_lang):
        back.append(lax.ppermute(dx[s], "lang", [(i, (i + s) % n_lang) for i in range(n_lang)]))
    same_core = [[lang * n_pair + p for lang in range(core, n_lang, 2) for p in range(n_pair)] for core in range(2)]

    def over_chips(a):
        return lax.all_to_all(
            a, ("lang", "pair"), split_axis=0, concat_axis=0, axis_index_groups=same_core, tiled=True
        )

    flat = (-1,) + keep.shape[3:]
    pieces = over_chips(add(keep.reshape(flat), other.reshape(flat)))
    pieces, *back[1:4] = lax.optimization_barrier((pieces, *back[1:4]))
    factor = 1.0 / (sent_dev * n_lang * n_pair * length) ** 0.5
    near = over_chips(spread(pieces, factor)).reshape(keep.shape)
    grad_sentences = combine(where, listed, dq, w_query, back)
    near, grad_sentences = lax.optimization_barrier((near, grad_sentences))
    far = lax.ppermute(near, "lang", other_core)
    core = lax.rem(where, 2)
    grads = place(1 - core, far, place(core, near))
    grads = tuple(g.reshape(width, width) for g in grads)
    return (attended.reshape(sentences.shape), grad_sentences) + grads


def solution(mesh):
    split3, split2 = P(("lang", "pair"), None, None), P(("lang", "pair"), None)
    in_specs = (split3, split3, P(), P(), P(), split3, split2, split2, split2)
    out_specs = (split3, split3, P(), P(), P())
    return jax.shard_map(body, mesh=mesh, in_specs=in_specs, out_specs=out_specs, check_vma=False)
```

```python
import functools

import jax
import jax.numpy as jnp
from jax import lax
from jax.experimental import pallas as pl
from jax.experimental.pallas import tpu as pltpu
from jax.sharding import PartitionSpec as P

SIZE = 64
LANES = 128
BF, F32 = jnp.bfloat16, jnp.float32
NT = (((1,), (1,)), ((), ()))


def mm(a, b):
    return jnp.dot(a, b, preferred_element_type=F32)


def mm_nt(a, b):
    return lax.dot_general(a, b, NT, preferred_element_type=F32)


def attend_kernel(me_ref, src_ref, slot_ref, valid_ref, x_hbm, r_hbm, c_hbm, wq_hbm, wk_hbm, wv_hbm,
                  *rest, n_src, n_slot, length):
    outs, scratch = rest[:6 + n_slot], rest[6 + n_slot:]
    att_hbm, dq_hbm = outs[:2]
    gw_hbm = (outs[4:6], outs[2:4])
    dx_hbm = outs[6:]
    (mult, x_ref, r_ref, c_ref, wq_ref, wk_ref, wv_ref, att_v, dq_v, gw_v, dx_v,
     xt, rt, q2, g2, k_s, v_s, kt, vt, ot, dqt, dk_acc, dv_acc, sem_in, sem_r, sem_out) = scratch
    width = x_ref.shape[1]
    heads = width // LANES
    n_pairs = src_ref.shape[-1]
    me = me_ref[0]
    block = 256

    copies = [pltpu.make_async_copy(a, b, sem_in.at[i]) for i, (a, b) in enumerate(
        ((x_hbm, x_ref), (wq_hbm, wq_ref), (c_hbm, c_ref), (wk_hbm, wk_ref), (wv_hbm, wv_ref)))]
    slots = [pltpu.make_async_copy(r_hbm.at[lax.rem(me + p, n_slot)], r_ref.at[pl.ds(p * length, length), :],
                                   sem_r.at[p]) for p in range(n_slot)]
    for c in copies[:4] + slots + copies[4:]:
        c.start()

    for i in range(n_src * n_slot):
        mult[i] = 0
    for j in range(n_pairs):
        at = lax.rem(slot_ref[0, j] + n_slot - me, n_slot) * n_src + src_ref[0, j]
        mult[at] = mult[at] + valid_ref[0, j]
    ot[...] = jnp.zeros_like(ot)
    dqt[...] = jnp.zeros_like(dqt)
    dk_acc[...] = jnp.zeros_like(dk_acc)
    dv_acc[...] = jnp.zeros_like(dv_acc)

    for c in copies[:3]:
        c.wait()
    low = lax.broadcasted_iota(jnp.int32, (n_src * length, LANES), 1) < SIZE
    zero = jnp.zeros((n_src * length, LANES), BF)
    for n in range(0, width, block):
        q = mm(x_ref[...], wq_ref[:, n:n + block]).astype(BF) * BF(0.125)
        for h in range(n // LANES, (n + block) // LANES):
            qh = q[:, h * LANES - n:(h + 1) * LANES - n]
            gh = c_ref[:, h * LANES:(h + 1) * LANES]
            for ref, rows in ((q2, qh), (g2, gh)):
                top = jnp.where(low, rows, zero)
                bot = jnp.where(low, zero, rows)
                for s in range(n_src):
                    ref[s, h, :length, :] = top[s * length:(s + 1) * length]
                    ref[s, h, length:, :] = bot[s * length:(s + 1) * length]
    for s in range(n_src):
        xt[:, s * length:(s + 1) * length] = x_ref[s * length:(s + 1) * length, :].T

    copies[3].wait()
    for c in slots:
        c.wait()
    half = n_slot // 2
    for w_ref, nat, tra in ((wk_ref, k_s, kt), (wv_ref, v_s, vt)):
        if w_ref is wv_ref:
            copies[4].wait()
        for n in range(0, width, block):
            cols = slice(n, n + block)
            for lo in range(0, n_slot, half):
                k = mm(r_ref[lo * length:(lo + half) * length, :], w_ref[:, cols]).astype(BF)
                for t in range(half):
                    rows = k[t * length:(t + 1) * length]
                    nat[lo + t, :, cols] = rows
                    tra[lo + t, cols, :] = rows.T
    for t in range(n_slot):
        rt[:, t * length:(t + 1) * length] = r_ref[t * length:(t + 1) * length, :].T

    def combo(i, _):
        count = mult[i]

        @pl.when(count > 0)
        def _():
            t = i // n_src
            s = i % n_src
            m = count.astype(F32)

            def scores(h):
                cols = slice(h * LANES, (h + 1) * LANES)
                return mm_nt(k_s[t, :, cols], q2[s, h]), mm_nt(v_s[t, :, cols], g2[s, h])

            def soft(st, dp):
                e = jnp.exp(st - jnp.max(st, axis=0, keepdims=True))
                inv = 1.0 / jnp.sum(e, axis=0, keepdims=True)
                delta = jnp.sum(e * dp, axis=0, keepdims=True) * inv
                p = e * (inv * m)
                return p.astype(BF), (p * (dp - delta)).astype(BF)

            def grads(h, pb, ds):
                cols = slice(h * LANES, (h + 1) * LANES)
                dv = mm(pb, g2[s, h])
                dk = mm(ds, q2[s, h])
                o = mm(vt[t, cols, :], pb)
                dq = mm(kt[t, cols, :], ds)
                dv_acc[t, :, cols] += dv
                dk_acc[t, :, cols] += dk
                for part in range(2):
                    rows = slice(h * LANES + part * SIZE, h * LANES + (part + 1) * SIZE)
                    own = slice(part * SIZE, (part + 1) * SIZE)
                    keys = slice(part * length, (part + 1) * length)
                    ot[s, rows, :] += o[own, keys]
                    dqt[s, rows, :] += dq[own, keys]

            ready = [scores(h) for h in range(min(2, heads))]
            waiting = []
            for h in range(heads):
                if h + 2 < heads:
                    ready.append(scores(h + 2))
                waiting.append((h,) + soft(*ready.pop(0)))
                if h > 0:
                    grads(*waiting.pop(0))
            grads(*waiting.pop(0))
        return 0

    lax.fori_loop(0, n_src * n_slot, combo, 0)

    for t in range(n_slot):
        k_s[t] = dk_acc[t].astype(BF)
        v_s[t] = dv_acc[t].astype(BF)
    for s in range(n_src):
        dq_v[s * length:(s + 1) * length, :] = (dqt[s].T * 0.125).astype(BF)
    dk = k_s[...].reshape(n_slot * length, width)
    dv = v_s[...].reshape(n_slot * length, width)

    done = []

    def out(src, dst):
        c = pltpu.make_async_copy(src, dst, sem_out.at[len(done)])
        c.start()
        done.append(c)

    _, _, pieces, _, each, _ = gw_v.shape
    core = lax.rem(me, 2)
    for k, halves in enumerate(gw_hbm):
        base = pl.multiple_of((core if k else 1 - core) * (2 * pieces * each), LANES)
        rows = pl.ds(base, 2 * pieces * each)
        for n in range(0, width, block):
            cols = slice(n, n + block)
            for i, (lhs, rhs) in enumerate(((xt, dq_v[:, cols]), (rt, dk[:, cols]), (rt, dv[:, cols]))):
                g = mm(lhs[rows, :], rhs).astype(BF).reshape(2, pieces, each, block)
                for part in range(2):
                    gw_v[k, part, :, i, :, cols] = g[part]
        for part, dst in enumerate(halves):
            out(gw_v.at[k, part], dst)
        if k == 0:
            out(dq_v, dq_hbm)
    for s in range(n_src):
        att_v[s * length:(s + 1) * length, :] = ot[s].T.astype(BF)
    out(att_v, att_hbm)
    for lo in range(0, n_slot, half):
        rows = slice(lo * length, (lo + half) * length)
        for n in range(0, width, block):
            cols = slice(n, n + block)
            dx_v[rows, cols] = (mm_nt(dk[rows], wk_ref[cols, :]) + mm_nt(dv[rows], wv_ref[cols, :])).astype(BF)
        for t in range(lo, lo + half):
            out(dx_v.at[pl.ds(t * length, length), :], dx_hbm[t])
    for c in done:
        c.wait()


def attend(me, src, slot, valid, x, r, c, wq, wk, wv, *, pieces):
    n_slot, length, width = r.shape
    rows = x.shape[0]
    n_src = rows // length
    each = width // 4 // pieces
    share = (pieces, 3, each, width)
    heads = width // LANES
    smem = pl.BlockSpec(memory_space=pltpu.SMEM)
    hbm = pl.BlockSpec(memory_space=pltpu.HBM)
    shape = jax.ShapeDtypeStruct
    vm = pltpu.VMEM
    macs = 2 * (n_src + 3 * n_slot) * length * width * width + 12 * 6 * length * length * width
    return pl.pallas_call(
        functools.partial(attend_kernel, n_src=n_src, n_slot=n_slot, length=length),
        in_specs=[smem] * 4 + [hbm] * 6,
        out_specs=[hbm] * (6 + n_slot),
        out_shape=[shape((rows, width), BF), shape((rows, width), BF)] + [shape(share, BF)] * 4
        + [shape((length, width), BF)] * n_slot,
        scratch_shapes=[
            pltpu.SMEM((n_src * n_slot,), jnp.int32),
            vm((rows, width), BF), vm((n_slot * length, width), BF), vm((rows, width), BF),
            vm((width, width), BF), vm((width, width), BF), vm((width, width), BF),
            vm((rows, width), BF), vm((rows, width), BF),
            vm((2, 2) + share, BF), vm((n_slot * length, width), BF),
            vm((width, rows), BF), vm((width, n_slot * length), BF),
            vm((n_src, heads, 2 * length, LANES), BF), vm((n_src, heads, 2 * length, LANES), BF),
            vm((n_slot, length, width), BF), vm((n_slot, length, width), BF),
            vm((n_slot, width, length), BF), vm((n_slot, width, length), BF),
            vm((n_src, width, length), F32), vm((n_src, width, length), F32),
            vm((n_slot, length, width), F32), vm((n_slot, length, width), F32),
            pltpu.SemaphoreType.DMA((5,)), pltpu.SemaphoreType.DMA((n_slot,)),
            pltpu.SemaphoreType.DMA((6 + n_slot,)),
        ],
        compiler_params=pltpu.CompilerParams(vmem_limit_bytes=60 * 2**20),
        cost_estimate=pl.CostEstimate(flops=4 * macs, bytes_accessed=20 * 2**20, transcendentals=0),
        name="attend",
    )(me, src, slot, valid, x, r, c, wq, wk, wv)


def combine_kernel(me_ref, listed_ref, dq_hbm, wq_hbm, *rest):
    n_slot = len(rest) - 6
    parts, (out_ref, acc, dq_ref, wq_ref, back, sem) = rest[:n_slot], rest[n_slot:]
    length = back.shape[1]
    me = me_ref[0]
    block = 256
    copies = [pltpu.make_async_copy(a, b, sem.at[i]) for i, (a, b) in enumerate(
        [(dq_hbm, dq_ref), (wq_hbm, wq_ref)] + [(p, back.at[s]) for s, p in enumerate(parts)])]
    for c in copies:
        c.start()
    for c in copies:
        c.wait()
    for n in range(0, acc.shape[2], block):
        cols = slice(n, n + block)
        acc[:, :, cols] = mm_nt(dq_ref[...], wq_ref[cols, :]).reshape(acc.shape[0], length, block)
    for s in range(n_slot):
        at = listed_ref[lax.rem(me + n_slot - s, n_slot)]
        acc[at] += back[s].astype(F32)
    out_ref[...] = acc[...].astype(BF)


def combine(me, listed, dq, wq, parts):
    length, width = parts[0].shape
    n_src = dq.shape[0] // length
    smem = pl.BlockSpec(memory_space=pltpu.SMEM)
    hbm = pl.BlockSpec(memory_space=pltpu.HBM)
    return pl.pallas_call(
        combine_kernel,
        in_specs=[smem, smem] + [hbm] * (2 + len(parts)),
        out_specs=pl.BlockSpec(memory_space=pltpu.VMEM),
        out_shape=jax.ShapeDtypeStruct((n_src, length, width), BF),
        scratch_shapes=[
            pltpu.VMEM((n_src, length, width), F32), pltpu.VMEM(dq.shape, BF), pltpu.VMEM(wq.shape, BF),
            pltpu.VMEM((len(parts), length, width), BF), pltpu.SemaphoreType.DMA((2 + len(parts),)),
        ],
        compiler_params=pltpu.CompilerParams(vmem_limit_bytes=60 * 2**20),
        cost_estimate=pl.CostEstimate(flops=2 * dq.size * width, bytes_accessed=6 * 2**20, transcendentals=0),
        name="combine",
    )(me, listed, dq, wq, *parts)


def pick_kernel(listed_ref, x_hbm, out_hbm, x_ref, sem):
    load = pltpu.make_async_copy(x_hbm, x_ref, sem.at[0])
    load.start()
    load.wait()
    n = out_hbm.shape[0]
    stores = [pltpu.make_async_copy(x_ref.at[listed_ref[i]], out_hbm.at[i], sem.at[1 + i]) for i in range(n)]
    for c in stores:
        c.start()
    for c in stores:
        c.wait()


def pick(listed, x):
    n = listed.shape[0]
    hbm = pl.BlockSpec(memory_space=pltpu.HBM)
    return pl.pallas_call(
        pick_kernel,
        in_specs=[pl.BlockSpec(memory_space=pltpu.SMEM), hbm],
        out_specs=hbm,
        out_shape=jax.ShapeDtypeStruct((n,) + x.shape[1:], x.dtype),
        scratch_shapes=[pltpu.VMEM(x.shape, x.dtype), pltpu.SemaphoreType.DMA((1 + n,))],
        compiler_params=pltpu.CompilerParams(vmem_limit_bytes=60 * 2**20),
        name="pick",
    )(listed, x)


def add_kernel(a_ref, b_ref, out_ref):
    out_ref[...] = (a_ref[...].astype(F32) + b_ref[...].astype(F32)).astype(BF)


def add(a, b):
    count, n, each, width = a.shape
    spec = pl.BlockSpec((count // 2, n, each, width), lambda i: (i, 0, 0, 0))
    return pl.pallas_call(
        add_kernel,
        grid=(2,),
        in_specs=[spec, spec],
        out_specs=spec,
        out_shape=jax.ShapeDtypeStruct(a.shape, BF),
        compiler_params=pltpu.CompilerParams(vmem_limit_bytes=60 * 2**20),
        cost_estimate=pl.CostEstimate(flops=a.size, bytes_accessed=6 * a.size, transcendentals=0),
        name="add",
    )(a, b)


def sum_kernel(*refs):
    for half, ref in enumerate(refs[:-1]):
        refs[-1][half] = jnp.sum(ref[...].astype(F32), axis=0).astype(BF)


def sum_parts(*halves):
    count, n, each, width = halves[0].shape
    size = len(halves) * halves[0].size
    return pl.pallas_call(
        sum_kernel,
        grid=(n,),
        in_specs=[pl.BlockSpec((count, 1, each, width), lambda i: (0, i, 0, 0))] * len(halves),
        out_specs=pl.BlockSpec((len(halves), 1, each, width), lambda i: (0, i, 0, 0)),
        out_shape=jax.ShapeDtypeStruct((len(halves), n, each, width), BF),
        compiler_params=pltpu.CompilerParams(vmem_limit_bytes=16 * 2**20),
        cost_estimate=pl.CostEstimate(flops=size, bytes_accessed=2 * size, transcendentals=0),
        name="sum_parts",
    )(*halves)


def spread_kernel(a_ref, b_ref, c_ref, d_ref, out_ref, *, factor):
    a, b, c, d = (ref[0].astype(F32) for ref in (a_ref, b_ref, c_ref, d_ref))
    total = (a + c) + (b + d)
    out_ref[...] = jnp.broadcast_to((total * factor).astype(BF)[None], out_ref.shape)


def spread(parts, half, copies, factor):
    _, n, each, width = parts[0].shape
    return pl.pallas_call(
        functools.partial(spread_kernel, factor=factor),
        grid=(n,),
        in_specs=[pl.BlockSpec((1, 1, each, width), lambda i: (half, i, 0, 0))] * len(parts),
        out_specs=pl.BlockSpec((copies, 1, each, width), lambda i: (0, i, 0, 0)),
        out_shape=jax.ShapeDtypeStruct((copies, n, each, width), BF),
        compiler_params=pltpu.CompilerParams(vmem_limit_bytes=60 * 2**20),
        cost_estimate=pl.CostEstimate(flops=4 * parts[0].size, bytes_accessed=copies * parts[0].size, transcendentals=0),
        name="spread",
    )(*parts)


def place_kernel(quarter_ref, rows_ref, *rest):
    n = rows_ref.shape[1]
    for i, out in enumerate(rest[-n:]):
        out[0] = rows_ref[:, i]


def place(quarter, rows, into=()):
    pieces, n, each, width = rows.shape
    step = pieces // 2
    hbm = pl.BlockSpec(memory_space=pl.ANY)
    return pl.pallas_call(
        place_kernel,
        grid_spec=pltpu.PrefetchScalarGridSpec(
            num_scalar_prefetch=1,
            grid=(pieces // step,),
            in_specs=[pl.BlockSpec((step, n, each, width), lambda p, at: (p, 0, 0, 0))] + [hbm] * len(into),
            out_specs=[pl.BlockSpec((1, step, each, width), lambda p, at: (at[0], p, 0, 0))] * n,
        ),
        out_shape=[jax.ShapeDtypeStruct((4, pieces, each, width), BF)] * n,
        input_output_aliases={2 + i: i for i in range(len(into))},
        compiler_params=pltpu.CompilerParams(vmem_limit_bytes=16 * 2**20),
        cost_estimate=pl.CostEstimate(flops=0, bytes_accessed=4 * rows.size, transcendentals=0),
        name="place",
    )(quarter, rows, *into)


def body(sentences, cotangent, w_query, w_key, w_value, send_rows, pair_src, pair_slot, pair_valid):
    sent_dev, length, width = sentences.shape
    n_lang = lax.axis_size("lang")
    n_pair = lax.axis_size("pair")
    me = lax.axis_index("lang")
    listed = send_rows[0].reshape(-1)
    outgoing = pick(listed, sentences)
    received = lax.all_to_all(outgoing, "lang", split_axis=0, concat_axis=0, tiled=True)
    x = sentences.reshape(-1, width)
    c = cotangent.reshape(-1, width)
    where = me.reshape(1).astype(jnp.int32)
    attended, dq, keep0, keep1, send0, send1, *dx = attend(
        where, pair_src, pair_slot, pair_valid, x, received, c, w_query, w_key, w_value, pieces=n_pair
    )
    other_core = [(i, i ^ 1) for i in range(n_lang)]

    def swap(a):
        return lax.ppermute(a, "lang", other_core)

    def over_pair(a):
        return lax.all_to_all(a, "pair", split_axis=0, concat_axis=0, tiled=True)

    back = [dx[0]]
    for s in range(1, n_lang):
        back.append(lax.ppermute(dx[s], "lang", [(i, (i + s) % n_lang) for i in range(n_lang)]))
    other0, other1 = swap(send0), swap(send1)
    chip0 = add(keep0, other0)
    chip0, other1 = lax.optimization_barrier((chip0, other1))
    pieces0 = over_pair(chip0)
    pieces1 = over_pair(add(keep1, other1))
    pieces0, pieces1, *back[1:4] = lax.optimization_barrier((pieces0, pieces1, *back[1:4]))
    plane = sum_parts(pieces0, pieces1)
    rings = [plane]
    for y in range(1, n_lang // 2):
        rings.append(lax.ppermute(plane, "lang", [(i, (i + 2 * y) % n_lang) for i in range(n_lang)]))
    factor = 1.0 / (sent_dev * n_lang * n_pair * length) ** 0.5
    near0 = over_pair(spread(rings, 0, n_pair, factor))
    copies1, near0 = lax.optimization_barrier((spread(rings, 1, n_pair, factor), near0))
    near1 = over_pair(copies1)
    grad_sentences = combine(where, listed, dq, w_query, back)
    far0 = swap(near0)
    core = lax.rem(where, 2)
    grads = place(2 - 2 * core, far0, place(2 * core, near0))
    near1, grad_sentences, *grads = lax.optimization_barrier((near1, grad_sentences, *grads))
    far1 = swap(near1)
    grads = place(3 - 2 * core, far1, place(2 * core + 1, near1, grads))
    grads = tuple(g.reshape(width, width) for g in grads)
    return (attended.reshape(sentences.shape), grad_sentences) + grads


def solution(mesh):
    split3, split2 = P(("lang", "pair"), None, None), P(("lang", "pair"), None)
    in_specs = (split3, split3, P(), P(), P(), split3, split2, split2, split2)
    out_specs = (split3, split3, P(), P(), P())
    return jax.shard_map(body, mesh=mesh, in_specs=in_specs, out_specs=out_specs, check_vma=False)
```

```python
import functools

import jax
import jax.numpy as jnp
from jax import lax
from jax.experimental import pallas as pl
from jax.experimental.pallas import tpu as pltpu
from jax.sharding import PartitionSpec as P

SIZE = 64
LANES = 128
BF, F32 = jnp.bfloat16, jnp.float32
NT = (((1,), (1,)), ((), ()))


def mm(a, b):
    return jnp.dot(a, b, preferred_element_type=F32)


def mm_nt(a, b):
    return lax.dot_general(a, b, NT, preferred_element_type=F32)


def attend_kernel(me_ref, src_ref, slot_ref, valid_ref, x_hbm, r_hbm, c_hbm, wq_hbm, wk_hbm, wv_hbm,
                  *rest, n_src, n_slot, length):
    outs, scratch = rest[:4 + n_slot], rest[4 + n_slot:]
    att_hbm, dq_hbm, keep_hbm, send_hbm = outs[:4]
    dx_hbm = outs[4:]
    (mult, x_ref, r_ref, c_ref, wq_ref, wk_ref, wv_ref, att_v, dq_v, gw_v, dx_v,
     xt, rt, q2, g2, k_s, v_s, kt, vt, ot, dqt, dk_acc, dv_acc, sem_in, sem_r, sem_out) = scratch
    width = x_ref.shape[1]
    heads = width // LANES
    n_pairs = src_ref.shape[-1]
    me = me_ref[0]
    block = 256

    copies = [pltpu.make_async_copy(a, b, sem_in.at[i]) for i, (a, b) in enumerate(
        ((x_hbm, x_ref), (wq_hbm, wq_ref), (c_hbm, c_ref), (wk_hbm, wk_ref), (wv_hbm, wv_ref)))]
    slots = [pltpu.make_async_copy(r_hbm.at[lax.rem(me + p, n_slot)], r_ref.at[pl.ds(p * length, length), :],
                                   sem_r.at[p]) for p in range(n_slot)]
    for c in copies[:4] + slots + copies[4:]:
        c.start()

    for i in range(n_src * n_slot):
        mult[i] = 0
    for j in range(n_pairs):
        at = lax.rem(slot_ref[0, j] + n_slot - me, n_slot) * n_src + src_ref[0, j]
        mult[at] = mult[at] + valid_ref[0, j]
    ot[...] = jnp.zeros_like(ot)
    dqt[...] = jnp.zeros_like(dqt)
    dk_acc[...] = jnp.zeros_like(dk_acc)
    dv_acc[...] = jnp.zeros_like(dv_acc)

    for c in copies[:3]:
        c.wait()
    low = lax.broadcasted_iota(jnp.int32, (n_src * length, LANES), 1) < SIZE
    zero = jnp.zeros((n_src * length, LANES), BF)
    for n in range(0, width, block):
        q = mm(x_ref[...], wq_ref[:, n:n + block]).astype(BF) * BF(0.125)
        for h in range(n // LANES, (n + block) // LANES):
            qh = q[:, h * LANES - n:(h + 1) * LANES - n]
            gh = c_ref[:, h * LANES:(h + 1) * LANES]
            for ref, rows in ((q2, qh), (g2, gh)):
                top = jnp.where(low, rows, zero)
                bot = jnp.where(low, zero, rows)
                for s in range(n_src):
                    ref[s, h, :length, :] = top[s * length:(s + 1) * length]
                    ref[s, h, length:, :] = bot[s * length:(s + 1) * length]
    for s in range(n_src):
        xt[:, s * length:(s + 1) * length] = x_ref[s * length:(s + 1) * length, :].T

    copies[3].wait()
    for c in slots:
        c.wait()
    half = n_slot // 2
    for w_ref, nat, tra in ((wk_ref, k_s, kt), (wv_ref, v_s, vt)):
        if w_ref is wv_ref:
            copies[4].wait()
        for n in range(0, width, block):
            cols = slice(n, n + block)
            for lo in range(0, n_slot, half):
                k = mm(r_ref[lo * length:(lo + half) * length, :], w_ref[:, cols]).astype(BF)
                for t in range(half):
                    rows = k[t * length:(t + 1) * length]
                    nat[lo + t, :, cols] = rows
                    tra[lo + t, cols, :] = rows.T
    for t in range(n_slot):
        rt[:, t * length:(t + 1) * length] = r_ref[t * length:(t + 1) * length, :].T

    def combo(i, _):
        count = mult[i]

        @pl.when(count > 0)
        def _():
            t = i // n_src
            s = i % n_src
            m = count.astype(F32)

            def scores(h):
                cols = slice(h * LANES, (h + 1) * LANES)
                return mm_nt(k_s[t, :, cols], q2[s, h]), mm_nt(v_s[t, :, cols], g2[s, h])

            def soft(st, dp):
                e = jnp.exp(st - jnp.max(st, axis=0, keepdims=True))
                inv = 1.0 / jnp.sum(e, axis=0, keepdims=True)
                delta = jnp.sum(e * dp, axis=0, keepdims=True) * inv
                p = e * (inv * m)
                return p.astype(BF), (p * (dp - delta)).astype(BF)

            def grads(h, pb, ds):
                cols = slice(h * LANES, (h + 1) * LANES)
                dv = mm(pb, g2[s, h])
                dk = mm(ds, q2[s, h])
                o = mm(vt[t, cols, :], pb)
                dq = mm(kt[t, cols, :], ds)
                dv_acc[t, :, cols] += dv
                dk_acc[t, :, cols] += dk
                for part in range(2):
                    rows = slice(h * LANES + part * SIZE, h * LANES + (part + 1) * SIZE)
                    own = slice(part * SIZE, (part + 1) * SIZE)
                    keys = slice(part * length, (part + 1) * length)
                    ot[s, rows, :] += o[own, keys]
                    dqt[s, rows, :] += dq[own, keys]

            ready = [scores(h) for h in range(min(2, heads))]
            waiting = []
            for h in range(heads):
                if h + 2 < heads:
                    ready.append(scores(h + 2))
                waiting.append((h,) + soft(*ready.pop(0)))
                if h > 0:
                    grads(*waiting.pop(0))
            grads(*waiting.pop(0))
        return 0

    lax.fori_loop(0, n_src * n_slot, combo, 0)

    for t in range(n_slot):
        k_s[t] = dk_acc[t].astype(BF)
        v_s[t] = dv_acc[t].astype(BF)
    for s in range(n_src):
        dq_v[s * length:(s + 1) * length, :] = (dqt[s].T * 0.125).astype(BF)
    dk = k_s[...].reshape(n_slot * length, width)
    dv = v_s[...].reshape(n_slot * length, width)

    done = []

    def out(src, dst):
        c = pltpu.make_async_copy(src, dst, sem_out.at[len(done)])
        c.start()
        done.append(c)

    _, _, _, pieces, _, each, part = gw_v.shape
    core = lax.rem(me, 2)
    for k, dst in enumerate((send_hbm, keep_hbm)):
        base = pl.multiple_of((core if k else 1 - core) * (2 * pieces * each), LANES)
        rows = pl.ds(base, 2 * pieces * each)
        for n in range(0, width, block):
            cols = slice(n, n + block)
            for i, (lhs, rhs) in enumerate(((xt, dq_v[:, cols]), (rt, dk[:, cols]), (rt, dv[:, cols]))):
                g = mm(lhs[rows, :], rhs).astype(BF).reshape(pieces, 2, each, block)
                for up in range(2):
                    gw_v[k, up, n // part, :, i, :, n % part:n % part + block] = g[:, up]
        out(gw_v.at[k], dst)
        if k == 0:
            out(dq_v, dq_hbm)
    for s in range(n_src):
        att_v[s * length:(s + 1) * length, :] = ot[s].T.astype(BF)
    out(att_v, att_hbm)
    for lo in range(0, n_slot, half):
        rows = slice(lo * length, (lo + half) * length)
        for n in range(0, width, block):
            cols = slice(n, n + block)
            dx_v[rows, cols] = (mm_nt(dk[rows], wk_ref[cols, :]) + mm_nt(dv[rows], wv_ref[cols, :])).astype(BF)
        for t in range(lo, lo + half):
            out(dx_v.at[pl.ds(t * length, length), :], dx_hbm[t])
    for c in done:
        c.wait()


def attend(me, src, slot, valid, x, r, c, wq, wk, wv, *, pieces):
    n_slot, length, width = r.shape
    rows = x.shape[0]
    n_src = rows // length
    each = width // 4 // pieces
    share = (2, 2, pieces, 3, each, width // 2)
    heads = width // LANES
    smem = pl.BlockSpec(memory_space=pltpu.SMEM)
    hbm = pl.BlockSpec(memory_space=pltpu.HBM)
    shape = jax.ShapeDtypeStruct
    vm = pltpu.VMEM
    macs = 2 * (n_src + 3 * n_slot) * length * width * width + 12 * 6 * length * length * width
    return pl.pallas_call(
        functools.partial(attend_kernel, n_src=n_src, n_slot=n_slot, length=length),
        in_specs=[smem] * 4 + [hbm] * 6,
        out_specs=[hbm] * (4 + n_slot),
        out_shape=[shape((rows, width), BF), shape((rows, width), BF),
                   shape(share, BF), shape(share, BF)]
        + [shape((length, width), BF)] * n_slot,
        scratch_shapes=[
            pltpu.SMEM((n_src * n_slot,), jnp.int32),
            vm((rows, width), BF), vm((n_slot * length, width), BF), vm((rows, width), BF),
            vm((width, width), BF), vm((width, width), BF), vm((width, width), BF),
            vm((rows, width), BF), vm((rows, width), BF),
            vm((2,) + share, BF), vm((n_slot * length, width), BF),
            vm((width, rows), BF), vm((width, n_slot * length), BF),
            vm((n_src, heads, 2 * length, LANES), BF), vm((n_src, heads, 2 * length, LANES), BF),
            vm((n_slot, length, width), BF), vm((n_slot, length, width), BF),
            vm((n_slot, width, length), BF), vm((n_slot, width, length), BF),
            vm((n_src, width, length), F32), vm((n_src, width, length), F32),
            vm((n_slot, length, width), F32), vm((n_slot, length, width), F32),
            pltpu.SemaphoreType.DMA((5,)), pltpu.SemaphoreType.DMA((n_slot,)),
            pltpu.SemaphoreType.DMA((4 + n_slot,)),
        ],
        compiler_params=pltpu.CompilerParams(vmem_limit_bytes=60 * 2**20),
        cost_estimate=pl.CostEstimate(flops=4 * macs, bytes_accessed=20 * 2**20, transcendentals=0),
        name="attend",
    )(me, src, slot, valid, x, r, c, wq, wk, wv)


def load(pairs, sem):
    copies = [pltpu.make_async_copy(a, b, sem.at[i]) for i, (a, b) in enumerate(pairs)]
    for c in copies:
        c.start()
    return copies


def add_parts(me_ref, listed_ref, acc, back, shifts, n_slot):
    for i, s in enumerate(shifts):
        at = listed_ref[lax.rem(me_ref[0] + n_slot - s, n_slot)]
        acc[at] += back[i][...].astype(F32)


def combine_kernel(me_ref, listed_ref, dq_hbm, wq_hbm, *rest, shifts, n_slot):
    parts, (out_ref, dq_ref, wq_ref, back, sem) = rest[:len(shifts)], rest[len(shifts):]
    length = back.shape[1]
    block = 256
    copies = load([(dq_hbm, dq_ref), (wq_hbm, wq_ref)] + [(p, back.at[i]) for i, p in enumerate(parts)], sem)
    for c in copies[:2]:
        c.wait()
    for n in range(0, out_ref.shape[2], block):
        cols = slice(n, n + block)
        out_ref[:, :, cols] = mm_nt(dq_ref[...], wq_ref[cols, :]).reshape(out_ref.shape[0], length, block)
    for c in copies[2:]:
        c.wait()
    add_parts(me_ref, listed_ref, out_ref, back, shifts, n_slot)


def finish_kernel(me_ref, listed_ref, acc_ref, *rest, shifts, n_slot):
    parts, (out_ref, acc) = rest[:len(shifts)], rest[len(shifts):]
    acc[...] = acc_ref[...]
    add_parts(me_ref, listed_ref, acc, parts, shifts, n_slot)
    out_ref[...] = acc[...].astype(BF)


def combine(me, listed, dq, wq, parts, shifts):
    length, width = parts[0].shape
    n_src = dq.shape[0] // length
    smem = pl.BlockSpec(memory_space=pltpu.SMEM)
    hbm = pl.BlockSpec(memory_space=pl.ANY)
    return pl.pallas_call(
        functools.partial(combine_kernel, shifts=shifts, n_slot=listed.shape[0]),
        in_specs=[smem, smem] + [hbm] * (2 + len(parts)),
        out_specs=pl.BlockSpec(memory_space=pltpu.VMEM),
        out_shape=jax.ShapeDtypeStruct((n_src, length, width), F32),
        scratch_shapes=[
            pltpu.VMEM(dq.shape, BF), pltpu.VMEM(wq.shape, BF),
            pltpu.VMEM((len(parts), length, width), BF), pltpu.SemaphoreType.DMA((2 + len(parts),)),
        ],
        compiler_params=pltpu.CompilerParams(vmem_limit_bytes=24 * 2**20),
        cost_estimate=pl.CostEstimate(flops=2 * dq.size * width, bytes_accessed=6 * 2**20, transcendentals=0),
        name="combine",
    )(me, listed, dq, wq, *parts)


def finish(me, listed, acc, parts, shifts):
    smem = pl.BlockSpec(memory_space=pltpu.SMEM)
    vmem = pl.BlockSpec(memory_space=pltpu.VMEM)
    return pl.pallas_call(
        functools.partial(finish_kernel, shifts=shifts, n_slot=listed.shape[0]),
        in_specs=[smem, smem] + [vmem] * (1 + len(parts)),
        out_specs=vmem,
        out_shape=jax.ShapeDtypeStruct(acc.shape, BF),
        scratch_shapes=[pltpu.VMEM(acc.shape, F32)],
        compiler_params=pltpu.CompilerParams(vmem_limit_bytes=16 * 2**20),
        cost_estimate=pl.CostEstimate(flops=acc.size, bytes_accessed=8 * acc.size, transcendentals=0),
        name="finish",
    )(me, listed, acc, *parts)


def pick_kernel(listed_ref, x_hbm, out_hbm, x_ref, sem):
    load = pltpu.make_async_copy(x_hbm, x_ref, sem.at[0])
    load.start()
    load.wait()
    n = out_hbm.shape[0]
    stores = [pltpu.make_async_copy(x_ref.at[listed_ref[i]], out_hbm.at[i], sem.at[1 + i]) for i in range(n)]
    for c in stores:
        c.start()
    for c in stores:
        c.wait()


def pick(listed, x):
    n = listed.shape[0]
    hbm = pl.BlockSpec(memory_space=pltpu.HBM)
    return pl.pallas_call(
        pick_kernel,
        in_specs=[pl.BlockSpec(memory_space=pltpu.SMEM), hbm],
        out_specs=hbm,
        out_shape=jax.ShapeDtypeStruct((n,) + x.shape[1:], x.dtype),
        scratch_shapes=[pltpu.VMEM(x.shape, x.dtype), pltpu.SemaphoreType.DMA((1 + n,))],
        compiler_params=pltpu.CompilerParams(vmem_limit_bytes=60 * 2**20),
        name="pick",
    )(listed, x)


def add_kernel(a_ref, b_ref, out_ref):
    out_ref[...] = (a_ref[...].astype(F32) + b_ref[...].astype(F32)).astype(BF)


def add(a, b):
    count, n, each, width = a.shape
    spec = pl.BlockSpec((count // 4, n, each, width), lambda i: (i, 0, 0, 0))
    return pl.pallas_call(
        add_kernel,
        grid=(4,),
        in_specs=[spec, spec],
        out_specs=spec,
        out_shape=jax.ShapeDtypeStruct(a.shape, BF),
        compiler_params=pltpu.CompilerParams(vmem_limit_bytes=16 * 2**20),
        cost_estimate=pl.CostEstimate(flops=a.size, bytes_accessed=6 * a.size, transcendentals=0),
        name="add",
    )(a, b)


def spread_kernel(parts_ref, out_ref, *, factor):
    total = jnp.sum(parts_ref[...].astype(F32), axis=0) * factor
    out_ref[...] = jnp.broadcast_to(total.astype(BF)[None], out_ref.shape)


def spread(parts, factor):
    count, n, each, width = parts.shape
    spec = pl.BlockSpec((count, 1, each, width), lambda i: (0, i, 0, 0))
    return pl.pallas_call(
        functools.partial(spread_kernel, factor=factor),
        grid=(n,),
        in_specs=[spec],
        out_specs=spec,
        out_shape=jax.ShapeDtypeStruct(parts.shape, BF),
        compiler_params=pltpu.CompilerParams(vmem_limit_bytes=16 * 2**20),
        cost_estimate=pl.CostEstimate(flops=parts.size, bytes_accessed=4 * parts.size, transcendentals=0),
        name="spread",
    )(parts)


def place_kernel(half_ref, rows_ref, *rest):
    n = rows_ref.shape[3]
    width = rows_ref.shape[5]
    for i, out in enumerate(rest[-n:]):
        for up in range(2):
            for right in range(2):
                out[0, :, up, :, right * width:(right + 1) * width] = rows_ref[up, right, :, i]


def place(half, rows, into=()):
    _, _, pieces, n, each, width = rows.shape
    step = pieces // 4
    hbm = pl.BlockSpec(memory_space=pl.ANY)
    return pl.pallas_call(
        place_kernel,
        grid_spec=pltpu.PrefetchScalarGridSpec(
            num_scalar_prefetch=1,
            grid=(pieces // step,),
            in_specs=[pl.BlockSpec((2, 2, step, n, each, width), lambda p, half: (0, 0, p, 0, 0, 0))] + [hbm] * len(into),
            out_specs=[pl.BlockSpec((1, step, 2, each, 2 * width), lambda p, half: (half[0], p, 0, 0, 0))] * n,
        ),
        out_shape=[jax.ShapeDtypeStruct((2, pieces, 2, each, 2 * width), BF)] * n,
        input_output_aliases={2 + i: i for i in range(len(into))},
        compiler_params=pltpu.CompilerParams(vmem_limit_bytes=16 * 2**20),
        cost_estimate=pl.CostEstimate(flops=0, bytes_accessed=4 * rows.size, transcendentals=0),
        name="place",
    )(half, rows, *into)


def body(sentences, cotangent, w_query, w_key, w_value, send_rows, pair_src, pair_slot, pair_valid):
    sent_dev, length, width = sentences.shape
    n_lang = lax.axis_size("lang")
    n_pair = lax.axis_size("pair")
    me = lax.axis_index("lang")
    listed = send_rows[0].reshape(-1)
    outgoing = pick(listed, sentences)
    received = lax.all_to_all(outgoing, "lang", split_axis=0, concat_axis=0, tiled=True)
    x = sentences.reshape(-1, width)
    c = cotangent.reshape(-1, width)
    where = me.reshape(1).astype(jnp.int32)
    attended, dq, keep, send, *dx = attend(
        where, pair_src, pair_slot, pair_valid, x, received, c, w_query, w_key, w_value, pieces=n_pair
    )
    other_core = [(i, i ^ 1) for i in range(n_lang)]
    other = lax.ppermute(send, "lang", other_core)
    back = [dx[0]]
    for s in range(1, n_lang):
        back.append(lax.ppermute(dx[s], "lang", [(i, (i + s) % n_lang) for i in range(n_lang)]))
    same_core = [[lang * n_pair + p for lang in range(core, n_lang, 2) for p in range(n_pair)] for core in range(2)]

    def over_chips(a):
        return lax.all_to_all(
            a, ("lang", "pair"), split_axis=0, concat_axis=0, axis_index_groups=same_core, tiled=True
        )

    flat = (-1,) + keep.shape[3:]
    chip = add(keep.reshape(flat), other.reshape(flat))
    chip, *back[1:4] = lax.optimization_barrier((chip, *back[1:4]))
    factor = 1.0 / (sent_dev * n_lang * n_pair * length) ** 0.5
    copies = spread(over_chips(chip), factor)
    copies, *back[4:6] = lax.optimization_barrier((copies, *back[4:6]))
    near = over_chips(copies).reshape(keep.shape)
    acc = combine(where, listed, dq, w_query, back[:6], tuple(range(6)))
    near, acc = lax.optimization_barrier((near, acc))
    far = lax.ppermute(near, "lang", other_core)
    far, *back[6:] = lax.optimization_barrier((far, *back[6:]))
    grad_sentences = finish(where, listed, acc, back[6:], tuple(range(6, n_lang)))
    core = lax.rem(where, 2)
    grads = place(1 - core, far, place(core, near))
    grads = tuple(g.reshape(width, width) for g in grads)
    return (attended.reshape(sentences.shape), grad_sentences) + grads


def solution(mesh):
    split3, split2 = P(("lang", "pair"), None, None), P(("lang", "pair"), None)
    in_specs = (split3, split3, P(), P(), P(), split3, split2, split2, split2)
    out_specs = (split3, split3, P(), P(), P())
    return jax.shard_map(body, mesh=mesh, in_specs=in_specs, out_specs=out_specs, check_vma=False)
```

```python
import functools

import jax
import jax.numpy as jnp
from jax import lax
from jax.experimental import pallas as pl
from jax.experimental.pallas import tpu as pltpu
from jax.sharding import PartitionSpec as P

SIZE = 64
LANES = 128
BF, F32 = jnp.bfloat16, jnp.float32
NT = (((1,), (1,)), ((), ()))


def mm(a, b):
    return jnp.dot(a, b, preferred_element_type=F32)


def mm_nt(a, b):
    return lax.dot_general(a, b, NT, preferred_element_type=F32)


def attend_kernel(me_ref, src_ref, slot_ref, valid_ref, x_hbm, r_hbm, c_hbm, wq_hbm, wk_hbm, wv_hbm,
                  *rest, n_src, n_slot, length):
    outs, scratch = rest[:6], rest[6:]
    att_hbm, dq_hbm, keep_hbm, send_hbm, dk_hbm, dv_hbm = outs
    (mult, x_ref, r_ref, c_ref, wq_ref, wk_ref, wv_ref, att_v, dq_v, gw_v,
     xt, rt, q2, g2, k_s, v_s, kt, vt, ot, dqt, dk_acc, dv_acc, sem_in, sem_r, sem_out) = scratch
    width = x_ref.shape[1]
    heads = width // LANES
    n_pairs = src_ref.shape[-1]
    me = me_ref[0]
    block = 256

    copies = [pltpu.make_async_copy(a, b, sem_in.at[i]) for i, (a, b) in enumerate(
        ((x_hbm, x_ref), (wq_hbm, wq_ref), (c_hbm, c_ref), (wk_hbm, wk_ref), (wv_hbm, wv_ref)))]
    slots = [pltpu.make_async_copy(r_hbm.at[lax.rem(me + p, n_slot)], r_ref.at[pl.ds(p * length, length), :],
                                   sem_r.at[p]) for p in range(n_slot)]
    for c in copies[:4] + slots + copies[4:]:
        c.start()

    for i in range(n_src * n_slot):
        mult[i] = 0
    for j in range(n_pairs):
        at = lax.rem(slot_ref[0, j] + n_slot - me, n_slot) * n_src + src_ref[0, j]
        mult[at] = mult[at] + valid_ref[0, j]
    ot[...] = jnp.zeros_like(ot)
    dqt[...] = jnp.zeros_like(dqt)
    dk_acc[...] = jnp.zeros_like(dk_acc)
    dv_acc[...] = jnp.zeros_like(dv_acc)

    for c in copies[:3]:
        c.wait()
    low = lax.broadcasted_iota(jnp.int32, (n_src * length, LANES), 1) < SIZE
    zero = jnp.zeros((n_src * length, LANES), BF)
    for n in range(0, width, block):
        q = mm(x_ref[...], wq_ref[:, n:n + block]).astype(BF) * BF(0.125)
        for h in range(n // LANES, (n + block) // LANES):
            qh = q[:, h * LANES - n:(h + 1) * LANES - n]
            gh = c_ref[:, h * LANES:(h + 1) * LANES]
            for ref, rows in ((q2, qh), (g2, gh)):
                top = jnp.where(low, rows, zero)
                bot = jnp.where(low, zero, rows)
                for s in range(n_src):
                    ref[s, h, :length, :] = top[s * length:(s + 1) * length]
                    ref[s, h, length:, :] = bot[s * length:(s + 1) * length]
    for s in range(n_src):
        xt[:, s * length:(s + 1) * length] = x_ref[s * length:(s + 1) * length, :].T

    copies[3].wait()
    for c in slots:
        c.wait()
    half = n_slot // 2
    for w_ref, nat, tra in ((wk_ref, k_s, kt), (wv_ref, v_s, vt)):
        if w_ref is wv_ref:
            copies[4].wait()
        for n in range(0, width, block):
            cols = slice(n, n + block)
            for lo in range(0, n_slot, half):
                k = mm(r_ref[lo * length:(lo + half) * length, :], w_ref[:, cols]).astype(BF)
                for t in range(half):
                    rows = k[t * length:(t + 1) * length]
                    nat[lo + t, :, cols] = rows
                    tra[lo + t, cols, :] = rows.T
    for t in range(n_slot):
        rt[:, t * length:(t + 1) * length] = r_ref[t * length:(t + 1) * length, :].T

    def combo(i, _):
        count = mult[i]

        @pl.when(count > 0)
        def _():
            t = i // n_src
            s = i % n_src
            m = count.astype(F32)

            def scores(h):
                cols = slice(h * LANES, (h + 1) * LANES)
                return mm_nt(k_s[t, :, cols], q2[s, h]), mm_nt(v_s[t, :, cols], g2[s, h])

            def soft(st, dp):
                e = jnp.exp(st - jnp.max(st, axis=0, keepdims=True))
                inv = 1.0 / jnp.sum(e, axis=0, keepdims=True)
                delta = jnp.sum(e * dp, axis=0, keepdims=True) * inv
                p = e * (inv * m)
                return p.astype(BF), (p * (dp - delta)).astype(BF)

            def grads(h, pb, ds):
                cols = slice(h * LANES, (h + 1) * LANES)
                dv = mm(pb, g2[s, h])
                dk = mm(ds, q2[s, h])
                o = mm(vt[t, cols, :], pb)
                dq = mm(kt[t, cols, :], ds)
                dv_acc[t, :, cols] += dv
                dk_acc[t, :, cols] += dk
                for part in range(2):
                    rows = slice(h * LANES + part * SIZE, h * LANES + (part + 1) * SIZE)
                    own = slice(part * SIZE, (part + 1) * SIZE)
                    keys = slice(part * length, (part + 1) * length)
                    ot[s, rows, :] += o[own, keys]
                    dqt[s, rows, :] += dq[own, keys]

            ready = [scores(h) for h in range(min(2, heads))]
            waiting = []
            for h in range(heads):
                if h + 2 < heads:
                    ready.append(scores(h + 2))
                waiting.append((h,) + soft(*ready.pop(0)))
                if h > 0:
                    grads(*waiting.pop(0))
            grads(*waiting.pop(0))
        return 0

    lax.fori_loop(0, n_src * n_slot, combo, 0)

    for t in range(n_slot):
        k_s[t] = dk_acc[t].astype(BF)
        v_s[t] = dv_acc[t].astype(BF)
    for s in range(n_src):
        dq_v[s * length:(s + 1) * length, :] = (dqt[s].T * 0.125).astype(BF)
    dk = k_s[...].reshape(n_slot * length, width)
    dv = v_s[...].reshape(n_slot * length, width)

    done = []

    def out(src, dst):
        c = pltpu.make_async_copy(src, dst, sem_out.at[len(done)])
        c.start()
        done.append(c)

    _, pieces, _, each, _ = gw_v.shape
    core = lax.rem(me, 2)
    for k, dst in enumerate((send_hbm, keep_hbm)):
        base = pl.multiple_of((core if k else 1 - core) * (pieces * each), LANES)
        rows = pl.ds(base, pieces * each)
        for n in range(0, width, block):
            cols = slice(n, n + block)
            for i, (lhs, rhs) in enumerate(((xt, dq_v[:, cols]), (rt, dk[:, cols]), (rt, dv[:, cols]))):
                gw_v[k, :, i, :, cols] = mm(lhs[rows, :], rhs).astype(BF).reshape(pieces, each, block)
        out(gw_v.at[k], dst)
        if k == 0:
            out(dq_v, dq_hbm)
            out(k_s, dk_hbm)
            out(v_s, dv_hbm)
    for s in range(n_src):
        att_v[s * length:(s + 1) * length, :] = ot[s].T.astype(BF)
    out(att_v, att_hbm)
    for c in done:
        c.wait()


def attend(me, src, slot, valid, x, r, c, wq, wk, wv, *, pieces):
    n_slot, length, width = r.shape
    rows = x.shape[0]
    n_src = rows // length
    each = width // 2 // pieces
    heads = width // LANES
    smem = pl.BlockSpec(memory_space=pltpu.SMEM)
    hbm = pl.BlockSpec(memory_space=pltpu.HBM)
    shape = jax.ShapeDtypeStruct
    vm = pltpu.VMEM
    macs = 2 * (n_src + 2 * n_slot) * length * width * width + 12 * 6 * length * length * width
    return pl.pallas_call(
        functools.partial(attend_kernel, n_src=n_src, n_slot=n_slot, length=length),
        in_specs=[smem] * 4 + [hbm] * 6,
        out_specs=[hbm] * 6,
        out_shape=[shape((rows, width), BF), shape((rows, width), BF),
                   shape((pieces, 3, each, width), BF), shape((pieces, 3, each, width), BF)]
        + [shape((n_slot, length, width), BF)] * 2,
        scratch_shapes=[
            pltpu.SMEM((n_src * n_slot,), jnp.int32),
            vm((rows, width), BF), vm((n_slot * length, width), BF), vm((rows, width), BF),
            vm((width, width), BF), vm((width, width), BF), vm((width, width), BF),
            vm((rows, width), BF), vm((rows, width), BF),
            vm((2, pieces, 3, each, width), BF),
            vm((width, rows), BF), vm((width, n_slot * length), BF),
            vm((n_src, heads, 2 * length, LANES), BF), vm((n_src, heads, 2 * length, LANES), BF),
            vm((n_slot, length, width), BF), vm((n_slot, length, width), BF),
            vm((n_slot, width, length), BF), vm((n_slot, width, length), BF),
            vm((n_src, width, length), F32), vm((n_src, width, length), F32),
            vm((n_slot, length, width), F32), vm((n_slot, length, width), F32),
            pltpu.SemaphoreType.DMA((5,)), pltpu.SemaphoreType.DMA((n_slot,)),
            pltpu.SemaphoreType.DMA((6,)),
        ],
        compiler_params=pltpu.CompilerParams(vmem_limit_bytes=60 * 2**20),
        cost_estimate=pl.CostEstimate(flops=4 * macs, bytes_accessed=20 * 2**20, transcendentals=0),
        name="attend",
    )(me, src, slot, valid, x, r, c, wq, wk, wv)


def input_kernel(dk_hbm, dv_hbm, wk_hbm, wv_hbm, *rest):
    n_slot = dk_hbm.shape[0]
    outs, (dk, dv, wk, wv, acc, dx, sem_in, sem_out) = rest[:n_slot], rest[n_slot:]
    length, width = dk.shape[1:]
    block, half = 256, n_slot // 2
    loads = [pltpu.make_async_copy(a, b, sem_in.at[i]) for i, (a, b) in enumerate(
        ((dk_hbm, dk), (wk_hbm, wk), (dv_hbm, dv), (wv_hbm, wv)))]
    for c in loads:
        c.start()
    stores = [pltpu.make_async_copy(dx.at[t], outs[t], sem_out.at[t]) for t in range(n_slot)]
    for d, w, final in ((dk, wk, False), (dv, wv, True)):
        for c in loads[2 * final:2 * final + 2]:
            c.wait()
        for lo in range(0, n_slot, half):
            rows = d[lo:lo + half].reshape(half * length, width)
            for n in range(0, width, block):
                cols = slice(n, n + block)
                part = mm_nt(rows, w[cols, :]).reshape(half, length, block)
                if final:
                    dx[lo:lo + half, :, cols] = (acc[lo:lo + half, :, cols] + part).astype(BF)
                else:
                    acc[lo:lo + half, :, cols] = part
            if final:
                for c in stores[lo:lo + half]:
                    c.start()
    for c in stores:
        c.wait()


def input_grads(dk, dv, wk, wv):
    n_slot, length, width = dk.shape
    hbm = pl.BlockSpec(memory_space=pltpu.HBM)
    vm = pltpu.VMEM
    return pl.pallas_call(
        input_kernel,
        in_specs=[hbm] * 4,
        out_specs=[hbm] * n_slot,
        out_shape=[jax.ShapeDtypeStruct((length, width), BF)] * n_slot,
        scratch_shapes=[
            vm(dk.shape, BF), vm(dv.shape, BF), vm(wk.shape, BF), vm(wv.shape, BF), vm(dk.shape, F32), vm(dk.shape, BF),
            pltpu.SemaphoreType.DMA((4,)), pltpu.SemaphoreType.DMA((n_slot,)),
        ],
        compiler_params=pltpu.CompilerParams(vmem_limit_bytes=60 * 2**20),
        cost_estimate=pl.CostEstimate(flops=4 * dk.size * width, bytes_accessed=10 * 2**20, transcendentals=0),
        name="input_grads",
    )(dk, dv, wk, wv)


def add_kernel(a_ref, b_ref, out_ref):
    out_ref[...] = (a_ref[...].astype(F32) + b_ref[...].astype(F32)).astype(BF)


def add(a, b):
    count, n, each, width = a.shape
    spec = pl.BlockSpec((count // 4, n, each, width), lambda i: (i, 0, 0, 0))
    return pl.pallas_call(
        add_kernel,
        grid=(4,),
        in_specs=[spec, spec],
        out_specs=spec,
        out_shape=jax.ShapeDtypeStruct(a.shape, BF),
        compiler_params=pltpu.CompilerParams(vmem_limit_bytes=16 * 2**20),
        cost_estimate=pl.CostEstimate(flops=a.size, bytes_accessed=6 * a.size, transcendentals=0),
        name="add",
    )(a, b)


def combine_kernel(me_ref, listed_ref, dq_hbm, wq_hbm, *rest):
    n_slot = len(rest) - 6
    parts, (out_ref, acc, dq_ref, wq_ref, back, sem) = rest[:n_slot], rest[n_slot:]
    length = back.shape[1]
    me = me_ref[0]
    block = 256
    copies = [pltpu.make_async_copy(a, b, sem.at[i]) for i, (a, b) in enumerate(
        [(dq_hbm, dq_ref), (wq_hbm, wq_ref)] + [(p, back.at[s]) for s, p in enumerate(parts)])]
    for c in copies:
        c.start()
    for c in copies:
        c.wait()
    for n in range(0, acc.shape[2], block):
        cols = slice(n, n + block)
        acc[:, :, cols] = mm_nt(dq_ref[...], wq_ref[cols, :]).reshape(acc.shape[0], length, block)
    for s in range(n_slot):
        at = listed_ref[lax.rem(me + n_slot - s, n_slot)]
        acc[at] += back[s].astype(F32)
    out_ref[...] = acc[...].astype(BF)


def combine(me, listed, dq, wq, parts):
    length, width = parts[0].shape
    n_src = dq.shape[0] // length
    smem = pl.BlockSpec(memory_space=pltpu.SMEM)
    hbm = pl.BlockSpec(memory_space=pltpu.HBM)
    return pl.pallas_call(
        combine_kernel,
        in_specs=[smem, smem] + [hbm] * (2 + len(parts)),
        out_specs=pl.BlockSpec(memory_space=pltpu.VMEM),
        out_shape=jax.ShapeDtypeStruct((n_src, length, width), BF),
        scratch_shapes=[
            pltpu.VMEM((n_src, length, width), F32), pltpu.VMEM(dq.shape, BF), pltpu.VMEM(wq.shape, BF),
            pltpu.VMEM((len(parts), length, width), BF), pltpu.SemaphoreType.DMA((2 + len(parts),)),
        ],
        compiler_params=pltpu.CompilerParams(vmem_limit_bytes=60 * 2**20),
        cost_estimate=pl.CostEstimate(flops=2 * dq.size * width, bytes_accessed=6 * 2**20, transcendentals=0),
        name="combine",
    )(me, listed, dq, wq, *parts)


def pick_kernel(listed_ref, x_hbm, out_hbm, x_ref, sem):
    load = pltpu.make_async_copy(x_hbm, x_ref, sem.at[0])
    load.start()
    load.wait()
    n = out_hbm.shape[0]
    stores = [pltpu.make_async_copy(x_ref.at[listed_ref[i]], out_hbm.at[i], sem.at[1 + i]) for i in range(n)]
    for c in stores:
        c.start()
    for c in stores:
        c.wait()


def pick(listed, x):
    n = listed.shape[0]
    hbm = pl.BlockSpec(memory_space=pltpu.HBM)
    return pl.pallas_call(
        pick_kernel,
        in_specs=[pl.BlockSpec(memory_space=pltpu.SMEM), hbm],
        out_specs=hbm,
        out_shape=jax.ShapeDtypeStruct((n,) + x.shape[1:], x.dtype),
        scratch_shapes=[pltpu.VMEM(x.shape, x.dtype), pltpu.SemaphoreType.DMA((1 + n,))],
        compiler_params=pltpu.CompilerParams(vmem_limit_bytes=60 * 2**20),
        name="pick",
    )(listed, x)


def sum_kernel(parts_ref, out_ref):
    out_ref[...] = jnp.sum(parts_ref[...].astype(F32), axis=0).astype(BF)


def sum_parts(parts):
    count, n, each, width = parts.shape
    return pl.pallas_call(
        sum_kernel,
        grid=(n,),
        in_specs=[pl.BlockSpec((count, 1, each, width), lambda i: (0, i, 0, 0))],
        out_specs=pl.BlockSpec((1, each, width), lambda i: (i, 0, 0)),
        out_shape=jax.ShapeDtypeStruct((n, each, width), BF),
        compiler_params=pltpu.CompilerParams(vmem_limit_bytes=16 * 2**20),
        cost_estimate=pl.CostEstimate(flops=parts.size, bytes_accessed=2 * parts.size, transcendentals=0),
        name="sum_parts",
    )(parts)


def spread_kernel(a_ref, b_ref, c_ref, d_ref, out_ref, *, factor):
    a, b, c, d = (ref[...].astype(F32) for ref in (a_ref, b_ref, c_ref, d_ref))
    total = (a + c) + (b + d)
    out_ref[...] = jnp.broadcast_to((total * factor).astype(BF)[None], out_ref.shape)


def spread(parts, copies, factor):
    n, each, width = parts[0].shape
    return pl.pallas_call(
        functools.partial(spread_kernel, factor=factor),
        grid=(n,),
        in_specs=[pl.BlockSpec((1, each, width), lambda i: (i, 0, 0))] * len(parts),
        out_specs=pl.BlockSpec((copies, 1, each, width), lambda i: (0, i, 0, 0)),
        out_shape=jax.ShapeDtypeStruct((copies, n, each, width), BF),
        compiler_params=pltpu.CompilerParams(vmem_limit_bytes=16 * 2**20),
        cost_estimate=pl.CostEstimate(flops=4 * parts[0].size, bytes_accessed=2 * copies * parts[0].size, transcendentals=0),
        name="spread",
    )(*parts)


def place_kernel(half_ref, rows_ref, *rest):
    n = rows_ref.shape[1]
    for i, out in enumerate(rest[-n:]):
        out[0] = rows_ref[:, i]


def place(half, rows, into=()):
    pieces, n, each, width = rows.shape
    step = pieces // 4
    hbm = pl.BlockSpec(memory_space=pl.ANY)
    return pl.pallas_call(
        place_kernel,
        grid_spec=pltpu.PrefetchScalarGridSpec(
            num_scalar_prefetch=1,
            grid=(pieces // step,),
            in_specs=[pl.BlockSpec((step, n, each, width), lambda p, half: (p, 0, 0, 0))] + [hbm] * len(into),
            out_specs=[pl.BlockSpec((1, step, each, width), lambda p, half: (half[0], p, 0, 0))] * n,
        ),
        out_shape=[jax.ShapeDtypeStruct((2, pieces, each, width), BF)] * n,
        input_output_aliases={2 + i: i for i in range(len(into))},
        compiler_params=pltpu.CompilerParams(vmem_limit_bytes=16 * 2**20),
        cost_estimate=pl.CostEstimate(flops=0, bytes_accessed=4 * rows.size, transcendentals=0),
        name="place",
    )(half, rows, *into)


def body(sentences, cotangent, w_query, w_key, w_value, send_rows, pair_src, pair_slot, pair_valid):
    sent_dev, length, width = sentences.shape
    n_lang = lax.axis_size("lang")
    n_pair = lax.axis_size("pair")
    me = lax.axis_index("lang")
    listed = send_rows[0].reshape(-1)
    outgoing = pick(listed, sentences)
    received = lax.all_to_all(outgoing, "lang", split_axis=0, concat_axis=0, tiled=True)
    x = sentences.reshape(-1, width)
    c = cotangent.reshape(-1, width)
    where = me.reshape(1).astype(jnp.int32)
    attended, dq, keep, send, dk, dv = attend(
        where, pair_src, pair_slot, pair_valid, x, received, c, w_query, w_key, w_value, pieces=n_pair
    )
    other_core = [(i, i ^ 1) for i in range(n_lang)]
    other = lax.ppermute(send, "lang", other_core)
    dx = input_grads(dk, dv, w_key, w_value)
    other, *dx = lax.optimization_barrier((other, *dx))
    chip = add(keep, other)
    back = [dx[0]]
    for s in range(1, n_lang):
        back.append(lax.ppermute(dx[s], "lang", [(i, (i + s) % n_lang) for i in range(n_lang)]))
    pieces = lax.all_to_all(chip, "pair", split_axis=0, concat_axis=0, tiled=True)
    pieces, *back[1:4] = lax.optimization_barrier((pieces, *back[1:4]))
    plane = sum_parts(pieces)
    rings = [plane]
    for y in range(1, n_lang // 2):
        rings.append(lax.ppermute(plane, "lang", [(i, (i + 2 * y) % n_lang) for i in range(n_lang)]))
    factor = 1.0 / (sent_dev * n_lang * n_pair * length) ** 0.5
    near = lax.all_to_all(spread(rings, n_pair, factor), "pair", split_axis=0, concat_axis=0, tiled=True)
    grad_sentences = combine(where, listed, dq, w_query, back)
    near, grad_sentences = lax.optimization_barrier((near, grad_sentences))
    far = lax.ppermute(near, "lang", other_core)
    core = lax.rem(where, 2)
    grads = place(1 - core, far, place(core, near))
    grads = tuple(g.reshape(width, width) for g in grads)
    return (attended.reshape(sentences.shape), grad_sentences) + grads


def solution(mesh):
    split3, split2 = P(("lang", "pair"), None, None), P(("lang", "pair"), None)
    in_specs = (split3, split3, P(), P(), P(), split3, split2, split2, split2)
    out_specs = (split3, split3, P(), P(), P())
    return jax.shard_map(body, mesh=mesh, in_specs=in_specs, out_specs=out_specs, check_vma=False)
```

```python
import functools

import jax
import jax.numpy as jnp
from jax import lax
from jax.experimental import pallas as pl
from jax.experimental.pallas import tpu as pltpu
from jax.sharding import PartitionSpec as P

SIZE = 64
LANES = 128
BF, F32 = jnp.bfloat16, jnp.float32
NT = (((1,), (1,)), ((), ()))


def mm(a, b):
    return jnp.dot(a, b, preferred_element_type=F32)


def mm_nt(a, b):
    return lax.dot_general(a, b, NT, preferred_element_type=F32)


def attend_kernel(me_ref, src_ref, slot_ref, valid_ref, x_hbm, r_hbm, c_hbm, wq_hbm, wk_hbm, wv_hbm,
                  *rest, n_src, n_slot, length):
    outs, scratch = rest[:7], rest[7:]
    att_hbm, dq_hbm, xk_hbm, rk_hbm, send_hbm, dk_hbm, dv_hbm = outs
    (mult, x_ref, r_ref, c_ref, wq_ref, wk_ref, wv_ref, att_v, dq_v, gw_v,
     xt, rt, q2, g2, k_s, v_s, kt, vt, ot, dqt, dk_acc, dv_acc, sem_in, sem_r, sem_out) = scratch
    width = x_ref.shape[1]
    heads = width // LANES
    n_pairs = src_ref.shape[-1]
    me = me_ref[0]
    block = 256

    copies = [pltpu.make_async_copy(a, b, sem_in.at[i]) for i, (a, b) in enumerate(
        ((x_hbm, x_ref), (wq_hbm, wq_ref), (c_hbm, c_ref), (wk_hbm, wk_ref), (wv_hbm, wv_ref)))]
    slots = [pltpu.make_async_copy(r_hbm.at[lax.rem(me + p, n_slot)], r_ref.at[pl.ds(p * length, length), :],
                                   sem_r.at[p]) for p in range(n_slot)]
    for c in copies[:4] + slots + copies[4:]:
        c.start()

    for i in range(n_src * n_slot):
        mult[i] = 0
    for j in range(n_pairs):
        at = lax.rem(slot_ref[0, j] + n_slot - me, n_slot) * n_src + src_ref[0, j]
        mult[at] = mult[at] + valid_ref[0, j]
    ot[...] = jnp.zeros_like(ot)
    dqt[...] = jnp.zeros_like(dqt)
    dk_acc[...] = jnp.zeros_like(dk_acc)
    dv_acc[...] = jnp.zeros_like(dv_acc)

    for c in copies[:3]:
        c.wait()
    low = lax.broadcasted_iota(jnp.int32, (n_src * length, LANES), 1) < SIZE
    zero = jnp.zeros((n_src * length, LANES), BF)
    for n in range(0, width, block):
        q = mm(x_ref[...], wq_ref[:, n:n + block]).astype(BF) * BF(0.125)
        for h in range(n // LANES, (n + block) // LANES):
            qh = q[:, h * LANES - n:(h + 1) * LANES - n]
            gh = c_ref[:, h * LANES:(h + 1) * LANES]
            for ref, rows in ((q2, qh), (g2, gh)):
                top = jnp.where(low, rows, zero)
                bot = jnp.where(low, zero, rows)
                for s in range(n_src):
                    ref[s, h, :length, :] = top[s * length:(s + 1) * length]
                    ref[s, h, length:, :] = bot[s * length:(s + 1) * length]
    for s in range(n_src):
        xt[:, s * length:(s + 1) * length] = x_ref[s * length:(s + 1) * length, :].T

    copies[3].wait()
    for c in slots:
        c.wait()
    half = n_slot // 2
    for w_ref, nat, tra in ((wk_ref, k_s, kt), (wv_ref, v_s, vt)):
        if w_ref is wv_ref:
            copies[4].wait()
        for n in range(0, width, block):
            cols = slice(n, n + block)
            for lo in range(0, n_slot, half):
                k = mm(r_ref[lo * length:(lo + half) * length, :], w_ref[:, cols]).astype(BF)
                for t in range(half):
                    rows = k[t * length:(t + 1) * length]
                    nat[lo + t, :, cols] = rows
                    tra[lo + t, cols, :] = rows.T
    for t in range(n_slot):
        rt[:, t * length:(t + 1) * length] = r_ref[t * length:(t + 1) * length, :].T

    def combo(i, _):
        count = mult[i]

        @pl.when(count > 0)
        def _():
            t = i // n_src
            s = i % n_src
            m = count.astype(F32)

            def scores(h):
                cols = slice(h * LANES, (h + 1) * LANES)
                return mm_nt(k_s[t, :, cols], q2[s, h]), mm_nt(v_s[t, :, cols], g2[s, h])

            def soft(st, dp):
                e = jnp.exp(st - jnp.max(st, axis=0, keepdims=True))
                inv = 1.0 / jnp.sum(e, axis=0, keepdims=True)
                delta = jnp.sum(e * dp, axis=0, keepdims=True) * inv
                p = e * (inv * m)
                return p.astype(BF), (p * (dp - delta)).astype(BF)

            def grads(h, pb, ds):
                cols = slice(h * LANES, (h + 1) * LANES)
                dv = mm(pb, g2[s, h])
                dk = mm(ds, q2[s, h])
                o = mm(vt[t, cols, :], pb)
                dq = mm(kt[t, cols, :], ds)
                dv_acc[t, :, cols] += dv
                dk_acc[t, :, cols] += dk
                for part in range(2):
                    rows = slice(h * LANES + part * SIZE, h * LANES + (part + 1) * SIZE)
                    own = slice(part * SIZE, (part + 1) * SIZE)
                    keys = slice(part * length, (part + 1) * length)
                    ot[s, rows, :] += o[own, keys]
                    dqt[s, rows, :] += dq[own, keys]

            ready = [scores(h) for h in range(min(2, heads))]
            waiting = []
            for h in range(heads):
                if h + 2 < heads:
                    ready.append(scores(h + 2))
                waiting.append((h,) + soft(*ready.pop(0)))
                if h > 0:
                    grads(*waiting.pop(0))
            grads(*waiting.pop(0))
        return 0

    lax.fori_loop(0, n_src * n_slot, combo, 0)

    for t in range(n_slot):
        k_s[t] = dk_acc[t].astype(BF)
        v_s[t] = dv_acc[t].astype(BF)
    for s in range(n_src):
        dq_v[s * length:(s + 1) * length, :] = (dqt[s].T * 0.125).astype(BF)
    dk = k_s[...].reshape(n_slot * length, width)
    dv = v_s[...].reshape(n_slot * length, width)

    done = []

    def out(src, dst):
        c = pltpu.make_async_copy(src, dst, sem_out.at[len(done)])
        c.start()
        done.append(c)

    pieces, _, each, _ = gw_v.shape
    core = lax.rem(me, 2)
    count = pieces * each
    own = pl.ds(pl.multiple_of(core * count, LANES), count)
    rows = pl.ds(pl.multiple_of((1 - core) * count, LANES), count)
    out(dq_v, dq_hbm)
    out(k_s, dk_hbm)
    out(v_s, dv_hbm)
    out(xt.at[own, :], xk_hbm)
    out(rt.at[own, :], rk_hbm)
    for n in range(0, width, block):
        cols = slice(n, n + block)
        for i, (lhs, rhs) in enumerate(((xt, dq_v[:, cols]), (rt, dk[:, cols]), (rt, dv[:, cols]))):
            gw_v[:, i, :, cols] = mm(lhs[rows, :], rhs).astype(BF).reshape(pieces, each, block)
    out(gw_v, send_hbm)
    for s in range(n_src):
        att_v[s * length:(s + 1) * length, :] = ot[s].T.astype(BF)
    out(att_v, att_hbm)
    for c in done:
        c.wait()


def attend(me, src, slot, valid, x, r, c, wq, wk, wv, *, pieces):
    n_slot, length, width = r.shape
    rows = x.shape[0]
    n_src = rows // length
    each = width // 2 // pieces
    heads = width // LANES
    smem = pl.BlockSpec(memory_space=pltpu.SMEM)
    hbm = pl.BlockSpec(memory_space=pltpu.HBM)
    shape = jax.ShapeDtypeStruct
    vm = pltpu.VMEM
    macs = 2 * (n_src + 2 * n_slot) * length * width * width + 12 * 6 * length * length * width
    return pl.pallas_call(
        functools.partial(attend_kernel, n_src=n_src, n_slot=n_slot, length=length),
        in_specs=[smem] * 4 + [hbm] * 6,
        out_specs=[hbm] * 7,
        out_shape=[shape((rows, width), BF), shape((rows, width), BF),
                   shape((width // 2, rows), BF), shape((width // 2, n_slot * length), BF),
                   shape((pieces, 3, each, width), BF)]
        + [shape((n_slot, length, width), BF)] * 2,
        scratch_shapes=[
            pltpu.SMEM((n_src * n_slot,), jnp.int32),
            vm((rows, width), BF), vm((n_slot * length, width), BF), vm((rows, width), BF),
            vm((width, width), BF), vm((width, width), BF), vm((width, width), BF),
            vm((rows, width), BF), vm((rows, width), BF),
            vm((pieces, 3, each, width), BF),
            vm((width, rows), BF), vm((width, n_slot * length), BF),
            vm((n_src, heads, 2 * length, LANES), BF), vm((n_src, heads, 2 * length, LANES), BF),
            vm((n_slot, length, width), BF), vm((n_slot, length, width), BF),
            vm((n_slot, width, length), BF), vm((n_slot, width, length), BF),
            vm((n_src, width, length), F32), vm((n_src, width, length), F32),
            vm((n_slot, length, width), F32), vm((n_slot, length, width), F32),
            pltpu.SemaphoreType.DMA((5,)), pltpu.SemaphoreType.DMA((n_slot,)),
            pltpu.SemaphoreType.DMA((7,)),
        ],
        compiler_params=pltpu.CompilerParams(vmem_limit_bytes=60 * 2**20),
        cost_estimate=pl.CostEstimate(flops=4 * macs, bytes_accessed=20 * 2**20, transcendentals=0),
        name="attend",
    )(me, src, slot, valid, x, r, c, wq, wk, wv)


def keep_kernel(x_hbm, r_hbm, dq_hbm, dk_hbm, dv_hbm, out_hbm, x, r, dq, dk, dv, gw, sem_in, sem_out):
    n_slot, length, width = dk.shape
    pieces, _, each, _ = gw.shape
    block = 256
    loads = [pltpu.make_async_copy(a, b, sem_in.at[i]) for i, (a, b) in enumerate(
        ((x_hbm, x), (dq_hbm, dq), (r_hbm, r), (dk_hbm, dk), (dv_hbm, dv)))]
    for c in loads:
        c.start()
    stores = [pltpu.make_async_copy(gw.at[:, i], out_hbm.at[:, i], sem_out.at[i]) for i in range(3)]
    for i, (lhs, rhs, needs) in enumerate(((x, dq, loads[:2]), (r, dk, loads[2:4]), (r, dv, loads[4:]))):
        for c in needs:
            c.wait()
        for n in range(0, width, block):
            cols = slice(n, n + block)
            d = rhs[:, cols] if i == 0 else rhs[:, :, cols].reshape(n_slot * length, block)
            gw[:, i, :, cols] = mm(lhs[...], d).astype(BF).reshape(pieces, each, block)
        stores[i].start()
    for c in stores:
        c.wait()


def keep_grads(x, r, dq, dk, dv, pieces):
    half, width = x.shape[0], dq.shape[1]
    hbm = pl.BlockSpec(memory_space=pltpu.HBM)
    vm = pltpu.VMEM
    share = (pieces, 3, half // pieces, width)
    return pl.pallas_call(
        keep_kernel,
        in_specs=[hbm] * 5,
        out_specs=hbm,
        out_shape=jax.ShapeDtypeStruct(share, BF),
        scratch_shapes=[vm(a.shape, BF) for a in (x, r, dq, dk, dv)] + [
            vm(share, BF), pltpu.SemaphoreType.DMA((5,)), pltpu.SemaphoreType.DMA((3,))],
        compiler_params=pltpu.CompilerParams(vmem_limit_bytes=60 * 2**20),
        cost_estimate=pl.CostEstimate(flops=2 * (x.size + 2 * r.size) * width, bytes_accessed=10 * 2**20, transcendentals=0),
        name="keep_grads",
    )(x, r, dq, dk, dv)


def input_kernel(dk_hbm, dv_hbm, wk_hbm, wv_hbm, *rest):
    n_slot = dk_hbm.shape[0]
    outs, (dk, dv, wk, wv, acc, dx, sem_in, sem_out) = rest[:n_slot], rest[n_slot:]
    length, width = dk.shape[1:]
    block, half = 256, n_slot // 2
    loads = [pltpu.make_async_copy(a, b, sem_in.at[i]) for i, (a, b) in enumerate(
        ((dk_hbm, dk), (wk_hbm, wk), (dv_hbm, dv), (wv_hbm, wv)))]
    for c in loads:
        c.start()
    stores = [pltpu.make_async_copy(dx.at[t], outs[t], sem_out.at[t]) for t in range(n_slot)]
    for d, w, final in ((dk, wk, False), (dv, wv, True)):
        for c in loads[2 * final:2 * final + 2]:
            c.wait()
        for lo in range(0, n_slot, half):
            rows = d[lo:lo + half].reshape(half * length, width)
            for n in range(0, width, block):
                cols = slice(n, n + block)
                part = mm_nt(rows, w[cols, :]).reshape(half, length, block)
                if final:
                    dx[lo:lo + half, :, cols] = (acc[lo:lo + half, :, cols] + part).astype(BF)
                else:
                    acc[lo:lo + half, :, cols] = part
            if final:
                for c in stores[lo:lo + half]:
                    c.start()
    for c in stores:
        c.wait()


def input_grads(dk, dv, wk, wv):
    n_slot, length, width = dk.shape
    hbm = pl.BlockSpec(memory_space=pltpu.HBM)
    vm = pltpu.VMEM
    return pl.pallas_call(
        input_kernel,
        in_specs=[hbm] * 4,
        out_specs=[hbm] * n_slot,
        out_shape=[jax.ShapeDtypeStruct((length, width), BF)] * n_slot,
        scratch_shapes=[
            vm(dk.shape, BF), vm(dv.shape, BF), vm(wk.shape, BF), vm(wv.shape, BF), vm(dk.shape, F32), vm(dk.shape, BF),
            pltpu.SemaphoreType.DMA((4,)), pltpu.SemaphoreType.DMA((n_slot,)),
        ],
        compiler_params=pltpu.CompilerParams(vmem_limit_bytes=60 * 2**20),
        cost_estimate=pl.CostEstimate(flops=4 * dk.size * width, bytes_accessed=10 * 2**20, transcendentals=0),
        name="input_grads",
    )(dk, dv, wk, wv)


def add_kernel(a_ref, b_ref, out_ref):
    out_ref[...] = (a_ref[...].astype(F32) + b_ref[...].astype(F32)).astype(BF)


def add(a, b):
    count, n, each, width = a.shape
    spec = pl.BlockSpec((count // 4, n, each, width), lambda i: (i, 0, 0, 0))
    return pl.pallas_call(
        add_kernel,
        grid=(4,),
        in_specs=[spec, spec],
        out_specs=spec,
        out_shape=jax.ShapeDtypeStruct(a.shape, BF),
        compiler_params=pltpu.CompilerParams(vmem_limit_bytes=16 * 2**20),
        cost_estimate=pl.CostEstimate(flops=a.size, bytes_accessed=6 * a.size, transcendentals=0),
        name="add",
    )(a, b)


def combine_kernel(me_ref, listed_ref, dq_hbm, wq_hbm, *rest):
    n_slot = len(rest) - 6
    parts, (out_ref, acc, dq_ref, wq_ref, back, sem) = rest[:n_slot], rest[n_slot:]
    length = back.shape[1]
    me = me_ref[0]
    block = 256
    copies = [pltpu.make_async_copy(a, b, sem.at[i]) for i, (a, b) in enumerate(
        [(dq_hbm, dq_ref), (wq_hbm, wq_ref)] + [(p, back.at[s]) for s, p in enumerate(parts)])]
    for c in copies:
        c.start()
    for c in copies:
        c.wait()
    for n in range(0, acc.shape[2], block):
        cols = slice(n, n + block)
        acc[:, :, cols] = mm_nt(dq_ref[...], wq_ref[cols, :]).reshape(acc.shape[0], length, block)
    for s in range(n_slot):
        at = listed_ref[lax.rem(me + n_slot - s, n_slot)]
        acc[at] += back[s].astype(F32)
    out_ref[...] = acc[...].astype(BF)


def combine(me, listed, dq, wq, parts):
    length, width = parts[0].shape
    n_src = dq.shape[0] // length
    smem = pl.BlockSpec(memory_space=pltpu.SMEM)
    hbm = pl.BlockSpec(memory_space=pltpu.HBM)
    return pl.pallas_call(
        combine_kernel,
        in_specs=[smem, smem] + [hbm] * (2 + len(parts)),
        out_specs=pl.BlockSpec(memory_space=pltpu.VMEM),
        out_shape=jax.ShapeDtypeStruct((n_src, length, width), BF),
        scratch_shapes=[
            pltpu.VMEM((n_src, length, width), F32), pltpu.VMEM(dq.shape, BF), pltpu.VMEM(wq.shape, BF),
            pltpu.VMEM((len(parts), length, width), BF), pltpu.SemaphoreType.DMA((2 + len(parts),)),
        ],
        compiler_params=pltpu.CompilerParams(vmem_limit_bytes=60 * 2**20),
        cost_estimate=pl.CostEstimate(flops=2 * dq.size * width, bytes_accessed=6 * 2**20, transcendentals=0),
        name="combine",
    )(me, listed, dq, wq, *parts)


def pick_kernel(listed_ref, x_hbm, out_hbm, x_ref, sem):
    load = pltpu.make_async_copy(x_hbm, x_ref, sem.at[0])
    load.start()
    load.wait()
    n = out_hbm.shape[0]
    stores = [pltpu.make_async_copy(x_ref.at[listed_ref[i]], out_hbm.at[i], sem.at[1 + i]) for i in range(n)]
    for c in stores:
        c.start()
    for c in stores:
        c.wait()


def pick(listed, x):
    n = listed.shape[0]
    hbm = pl.BlockSpec(memory_space=pltpu.HBM)
    return pl.pallas_call(
        pick_kernel,
        in_specs=[pl.BlockSpec(memory_space=pltpu.SMEM), hbm],
        out_specs=hbm,
        out_shape=jax.ShapeDtypeStruct((n,) + x.shape[1:], x.dtype),
        scratch_shapes=[pltpu.VMEM(x.shape, x.dtype), pltpu.SemaphoreType.DMA((1 + n,))],
        compiler_params=pltpu.CompilerParams(vmem_limit_bytes=60 * 2**20),
        name="pick",
    )(listed, x)


def sum_kernel(parts_ref, out_ref):
    out_ref[...] = jnp.sum(parts_ref[...].astype(F32), axis=0).astype(BF)


def sum_parts(parts):
    count, n, each, width = parts.shape
    return pl.pallas_call(
        sum_kernel,
        grid=(n,),
        in_specs=[pl.BlockSpec((count, 1, each, width), lambda i: (0, i, 0, 0))],
        out_specs=pl.BlockSpec((1, each, width), lambda i: (i, 0, 0)),
        out_shape=jax.ShapeDtypeStruct((n, each, width), BF),
        compiler_params=pltpu.CompilerParams(vmem_limit_bytes=16 * 2**20),
        cost_estimate=pl.CostEstimate(flops=parts.size, bytes_accessed=2 * parts.size, transcendentals=0),
        name="sum_parts",
    )(parts)


def spread_kernel(a_ref, b_ref, c_ref, d_ref, out_ref, *, factor):
    a, b, c, d = (ref[...].astype(F32) for ref in (a_ref, b_ref, c_ref, d_ref))
    total = (a + c) + (b + d)
    out_ref[...] = jnp.broadcast_to((total * factor).astype(BF)[None], out_ref.shape)


def spread(parts, copies, factor):
    n, each, width = parts[0].shape
    return pl.pallas_call(
        functools.partial(spread_kernel, factor=factor),
        grid=(n,),
        in_specs=[pl.BlockSpec((1, each, width), lambda i: (i, 0, 0))] * len(parts),
        out_specs=pl.BlockSpec((copies, 1, each, width), lambda i: (0, i, 0, 0)),
        out_shape=jax.ShapeDtypeStruct((copies, n, each, width), BF),
        compiler_params=pltpu.CompilerParams(vmem_limit_bytes=16 * 2**20),
        cost_estimate=pl.CostEstimate(flops=4 * parts[0].size, bytes_accessed=2 * copies * parts[0].size, transcendentals=0),
        name="spread",
    )(*parts)


def place_kernel(half_ref, rows_ref, *rest):
    n = rows_ref.shape[1]
    for i, out in enumerate(rest[-n:]):
        out[0] = rows_ref[:, i]


def place(half, rows, into=()):
    pieces, n, each, width = rows.shape
    step = pieces // 4
    hbm = pl.BlockSpec(memory_space=pl.ANY)
    return pl.pallas_call(
        place_kernel,
        grid_spec=pltpu.PrefetchScalarGridSpec(
            num_scalar_prefetch=1,
            grid=(pieces // step,),
            in_specs=[pl.BlockSpec((step, n, each, width), lambda p, half: (p, 0, 0, 0))] + [hbm] * len(into),
            out_specs=[pl.BlockSpec((1, step, each, width), lambda p, half: (half[0], p, 0, 0))] * n,
        ),
        out_shape=[jax.ShapeDtypeStruct((2, pieces, each, width), BF)] * n,
        input_output_aliases={2 + i: i for i in range(len(into))},
        compiler_params=pltpu.CompilerParams(vmem_limit_bytes=16 * 2**20),
        cost_estimate=pl.CostEstimate(flops=0, bytes_accessed=4 * rows.size, transcendentals=0),
        name="place",
    )(half, rows, *into)


def body(sentences, cotangent, w_query, w_key, w_value, send_rows, pair_src, pair_slot, pair_valid):
    sent_dev, length, width = sentences.shape
    n_lang = lax.axis_size("lang")
    n_pair = lax.axis_size("pair")
    me = lax.axis_index("lang")
    listed = send_rows[0].reshape(-1)
    outgoing = pick(listed, sentences)
    received = lax.all_to_all(outgoing, "lang", split_axis=0, concat_axis=0, tiled=True)
    x = sentences.reshape(-1, width)
    c = cotangent.reshape(-1, width)
    where = me.reshape(1).astype(jnp.int32)
    attended, dq, xk, rk, send, dk, dv = attend(
        where, pair_src, pair_slot, pair_valid, x, received, c, w_query, w_key, w_value, pieces=n_pair
    )
    other_core = [(i, i ^ 1) for i in range(n_lang)]
    other = lax.ppermute(send, "lang", other_core)
    keep = keep_grads(xk, rk, dq, dk, dv, n_pair)
    other, keep = lax.optimization_barrier((other, keep))
    chip, dk, dv = lax.optimization_barrier((add(keep, other), dk, dv))
    dx = input_grads(dk, dv, w_key, w_value)
    back = [dx[0]]
    for s in range(1, n_lang):
        back.append(lax.ppermute(dx[s], "lang", [(i, (i + s) % n_lang) for i in range(n_lang)]))
    pieces = lax.all_to_all(chip, "pair", split_axis=0, concat_axis=0, tiled=True)
    pieces, *back[1:4] = lax.optimization_barrier((pieces, *back[1:4]))
    plane = sum_parts(pieces)
    rings = [plane]
    for y in range(1, n_lang // 2):
        rings.append(lax.ppermute(plane, "lang", [(i, (i + 2 * y) % n_lang) for i in range(n_lang)]))
    factor = 1.0 / (sent_dev * n_lang * n_pair * length) ** 0.5
    near = lax.all_to_all(spread(rings, n_pair, factor), "pair", split_axis=0, concat_axis=0, tiled=True)
    grad_sentences = combine(where, listed, dq, w_query, back)
    near, grad_sentences = lax.optimization_barrier((near, grad_sentences))
    far = lax.ppermute(near, "lang", other_core)
    core = lax.rem(where, 2)
    grads = place(1 - core, far, place(core, near))
    grads = tuple(g.reshape(width, width) for g in grads)
    return (attended.reshape(sentences.shape), grad_sentences) + grads


def solution(mesh):
    split3, split2 = P(("lang", "pair"), None, None), P(("lang", "pair"), None)
    in_specs = (split3, split3, P(), P(), P(), split3, split2, split2, split2)
    out_specs = (split3, split3, P(), P(), P())
    return jax.shard_map(body, mesh=mesh, in_specs=in_specs, out_specs=out_specs, check_vma=False)
```

```python
import functools

import jax
import jax.numpy as jnp
from jax import lax
from jax.experimental import pallas as pl
from jax.experimental.pallas import tpu as pltpu
from jax.sharding import PartitionSpec as P

SIZE = 64
LANES = 128
BF, F32 = jnp.bfloat16, jnp.float32
NT = (((1,), (1,)), ((), ()))


def mm(a, b):
    return jnp.dot(a, b, preferred_element_type=F32)


def mm_nt(a, b):
    return lax.dot_general(a, b, NT, preferred_element_type=F32)


def attend_kernel(me_ref, src_ref, slot_ref, valid_ref, x_hbm, r_hbm, c_hbm, wq_hbm, wk_hbm, wv_hbm,
                  *rest, n_src, n_slot, length):
    outs, scratch = rest[:7], rest[7:]
    att_hbm, dq_hbm, xk_hbm, rk_hbm, send_hbm, dk_hbm, dv_hbm = outs
    (mult, x_ref, r_ref, c_ref, wq_ref, wk_ref, wv_ref, att_v, dq_v, gw_v,
     xt, rt, q2, g2, k_s, v_s, kt, vt, ot, dqt, dk_acc, dv_acc, sem_in, sem_r, sem_out) = scratch
    width = x_ref.shape[1]
    heads = width // LANES
    n_pairs = src_ref.shape[-1]
    me = me_ref[0]
    block = 256

    copies = [pltpu.make_async_copy(a, b, sem_in.at[i]) for i, (a, b) in enumerate(
        ((x_hbm, x_ref), (wq_hbm, wq_ref), (c_hbm, c_ref), (wk_hbm, wk_ref), (wv_hbm, wv_ref)))]
    slots = [pltpu.make_async_copy(r_hbm.at[lax.rem(me + p, n_slot)], r_ref.at[pl.ds(p * length, length), :],
                                   sem_r.at[p]) for p in range(n_slot)]
    for c in copies[:4] + slots + copies[4:]:
        c.start()

    for i in range(n_src * n_slot):
        mult[i] = 0
    for j in range(n_pairs):
        at = lax.rem(slot_ref[0, j] + n_slot - me, n_slot) * n_src + src_ref[0, j]
        mult[at] = mult[at] + valid_ref[0, j]
    ot[...] = jnp.zeros_like(ot)
    dqt[...] = jnp.zeros_like(dqt)
    dk_acc[...] = jnp.zeros_like(dk_acc)
    dv_acc[...] = jnp.zeros_like(dv_acc)

    for c in copies[:3]:
        c.wait()
    low = lax.broadcasted_iota(jnp.int32, (n_src * length, LANES), 1) < SIZE
    zero = jnp.zeros((n_src * length, LANES), BF)
    for n in range(0, width, block):
        q = mm(x_ref[...], wq_ref[:, n:n + block]).astype(BF) * BF(0.125)
        for h in range(n // LANES, (n + block) // LANES):
            qh = q[:, h * LANES - n:(h + 1) * LANES - n]
            gh = c_ref[:, h * LANES:(h + 1) * LANES]
            for ref, rows in ((q2, qh), (g2, gh)):
                top = jnp.where(low, rows, zero)
                bot = jnp.where(low, zero, rows)
                for s in range(n_src):
                    ref[s, h, :length, :] = top[s * length:(s + 1) * length]
                    ref[s, h, length:, :] = bot[s * length:(s + 1) * length]
    for s in range(n_src):
        xt[:, s * length:(s + 1) * length] = x_ref[s * length:(s + 1) * length, :].T

    copies[3].wait()
    for c in slots:
        c.wait()
    half = n_slot // 2
    for w_ref, nat, tra in ((wk_ref, k_s, kt), (wv_ref, v_s, vt)):
        if w_ref is wv_ref:
            copies[4].wait()
        for n in range(0, width, block):
            cols = slice(n, n + block)
            for lo in range(0, n_slot, half):
                k = mm(r_ref[lo * length:(lo + half) * length, :], w_ref[:, cols]).astype(BF)
                for t in range(half):
                    rows = k[t * length:(t + 1) * length]
                    nat[lo + t, :, cols] = rows
                    tra[lo + t, cols, :] = rows.T
    for t in range(n_slot):
        rt[:, t * length:(t + 1) * length] = r_ref[t * length:(t + 1) * length, :].T

    def combo(i, _):
        count = mult[i]

        @pl.when(count > 0)
        def _():
            t = i // n_src
            s = i % n_src
            m = count.astype(F32)

            def scores(h):
                cols = slice(h * LANES, (h + 1) * LANES)
                return mm_nt(k_s[t, :, cols], q2[s, h]), mm_nt(v_s[t, :, cols], g2[s, h])

            def soft(st, dp):
                e = jnp.exp(st - jnp.max(st, axis=0, keepdims=True))
                inv = 1.0 / jnp.sum(e, axis=0, keepdims=True)
                delta = jnp.sum(e * dp, axis=0, keepdims=True) * inv
                p = e * (inv * m)
                return p.astype(BF), (p * (dp - delta)).astype(BF)

            def grads(h, pb, ds):
                cols = slice(h * LANES, (h + 1) * LANES)
                dv = mm(pb, g2[s, h])
                dk = mm(ds, q2[s, h])
                o = mm(vt[t, cols, :], pb)
                dq = mm(kt[t, cols, :], ds)
                dv_acc[t, :, cols] += dv
                dk_acc[t, :, cols] += dk
                for part in range(2):
                    rows = slice(h * LANES + part * SIZE, h * LANES + (part + 1) * SIZE)
                    own = slice(part * SIZE, (part + 1) * SIZE)
                    keys = slice(part * length, (part + 1) * length)
                    ot[s, rows, :] += o[own, keys]
                    dqt[s, rows, :] += dq[own, keys]

            ready = [scores(h) for h in range(min(2, heads))]
            waiting = []
            for h in range(heads):
                if h + 2 < heads:
                    ready.append(scores(h + 2))
                waiting.append((h,) + soft(*ready.pop(0)))
                if h > 0:
                    grads(*waiting.pop(0))
            grads(*waiting.pop(0))
        return 0

    lax.fori_loop(0, n_src * n_slot, combo, 0)

    for t in range(n_slot):
        k_s[t] = dk_acc[t].astype(BF)
        v_s[t] = dv_acc[t].astype(BF)
    for s in range(n_src):
        dq_v[s * length:(s + 1) * length, :] = (dqt[s].T * 0.125).astype(BF)
    dk = k_s[...].reshape(n_slot * length, width)
    dv = v_s[...].reshape(n_slot * length, width)

    done = []

    def out(src, dst):
        c = pltpu.make_async_copy(src, dst, sem_out.at[len(done)])
        c.start()
        done.append(c)

    pieces, _, each, _ = gw_v.shape
    core = lax.rem(me, 2)
    count = pieces * each
    own = pl.ds(pl.multiple_of(core * count, LANES), count)
    rows = pl.ds(pl.multiple_of((1 - core) * count, LANES), count)
    out(dq_v, dq_hbm)
    out(k_s, dk_hbm)
    out(v_s, dv_hbm)
    out(xt.at[own, :], xk_hbm)
    out(rt.at[own, :], rk_hbm)
    for i, (lhs, rhs) in enumerate(((xt, dq_v), (rt, dk), (rt, dv))):
        for n in range(0, width, block):
            cols = slice(n, n + block)
            gw_v[:, i, :, cols] = mm(lhs[rows, :], rhs[:, cols]).astype(BF).reshape(pieces, each, block)
        out(gw_v.at[:, i], send_hbm.at[:, i])
    for s in range(n_src):
        att_v[s * length:(s + 1) * length, :] = ot[s].T.astype(BF)
    out(att_v, att_hbm)
    for c in done:
        c.wait()


def attend(me, src, slot, valid, x, r, c, wq, wk, wv, *, pieces):
    n_slot, length, width = r.shape
    rows = x.shape[0]
    n_src = rows // length
    each = width // 2 // pieces
    heads = width // LANES
    smem = pl.BlockSpec(memory_space=pltpu.SMEM)
    hbm = pl.BlockSpec(memory_space=pltpu.HBM)
    shape = jax.ShapeDtypeStruct
    vm = pltpu.VMEM
    macs = 2 * (n_src + 2 * n_slot) * length * width * width + 12 * 6 * length * length * width
    return pl.pallas_call(
        functools.partial(attend_kernel, n_src=n_src, n_slot=n_slot, length=length),
        in_specs=[smem] * 4 + [hbm] * 6,
        out_specs=[hbm] * 7,
        out_shape=[shape((rows, width), BF), shape((rows, width), BF),
                   shape((width // 2, rows), BF), shape((width // 2, n_slot * length), BF),
                   shape((pieces, 3, each, width), BF)]
        + [shape((n_slot, length, width), BF)] * 2,
        scratch_shapes=[
            pltpu.SMEM((n_src * n_slot,), jnp.int32),
            vm((rows, width), BF), vm((n_slot * length, width), BF), vm((rows, width), BF),
            vm((width, width), BF), vm((width, width), BF), vm((width, width), BF),
            vm((rows, width), BF), vm((rows, width), BF),
            vm((pieces, 3, each, width), BF),
            vm((width, rows), BF), vm((width, n_slot * length), BF),
            vm((n_src, heads, 2 * length, LANES), BF), vm((n_src, heads, 2 * length, LANES), BF),
            vm((n_slot, length, width), BF), vm((n_slot, length, width), BF),
            vm((n_slot, width, length), BF), vm((n_slot, width, length), BF),
            vm((n_src, width, length), F32), vm((n_src, width, length), F32),
            vm((n_slot, length, width), F32), vm((n_slot, length, width), F32),
            pltpu.SemaphoreType.DMA((5,)), pltpu.SemaphoreType.DMA((n_slot,)),
            pltpu.SemaphoreType.DMA((9,)),
        ],
        compiler_params=pltpu.CompilerParams(vmem_limit_bytes=60 * 2**20),
        cost_estimate=pl.CostEstimate(flops=4 * macs, bytes_accessed=20 * 2**20, transcendentals=0),
        name="attend",
    )(me, src, slot, valid, x, r, c, wq, wk, wv)


def keep_kernel(x_hbm, r_hbm, dq_hbm, dk_hbm, dv_hbm, out_hbm, x, r, dq, dk, dv, gw, sem_in, sem_out):
    n_slot, length, width = dk.shape
    pieces, _, each, _ = gw.shape
    block = 256
    loads = [pltpu.make_async_copy(a, b, sem_in.at[i]) for i, (a, b) in enumerate(
        ((x_hbm, x), (dq_hbm, dq), (r_hbm, r), (dk_hbm, dk), (dv_hbm, dv)))]
    for c in loads:
        c.start()
    stores = [pltpu.make_async_copy(gw.at[:, i], out_hbm.at[:, i], sem_out.at[i]) for i in range(3)]
    for i, (lhs, rhs, needs) in enumerate(((x, dq, loads[:2]), (r, dk, loads[2:4]), (r, dv, loads[4:]))):
        for c in needs:
            c.wait()
        for n in range(0, width, block):
            cols = slice(n, n + block)
            d = rhs[:, cols] if i == 0 else rhs[:, :, cols].reshape(n_slot * length, block)
            gw[:, i, :, cols] = mm(lhs[...], d).astype(BF).reshape(pieces, each, block)
        stores[i].start()
    for c in stores:
        c.wait()


def keep_grads(x, r, dq, dk, dv, pieces):
    half, width = x.shape[0], dq.shape[1]
    hbm = pl.BlockSpec(memory_space=pltpu.HBM)
    vm = pltpu.VMEM
    share = (pieces, 3, half // pieces, width)
    return pl.pallas_call(
        keep_kernel,
        in_specs=[hbm] * 5,
        out_specs=hbm,
        out_shape=jax.ShapeDtypeStruct(share, BF),
        scratch_shapes=[vm(a.shape, BF) for a in (x, r, dq, dk, dv)] + [
            vm(share, BF), pltpu.SemaphoreType.DMA((5,)), pltpu.SemaphoreType.DMA((3,))],
        compiler_params=pltpu.CompilerParams(vmem_limit_bytes=60 * 2**20),
        cost_estimate=pl.CostEstimate(flops=2 * (x.size + 2 * r.size) * width, bytes_accessed=10 * 2**20, transcendentals=0),
        name="keep_grads",
    )(x, r, dq, dk, dv)


def input_kernel(dk_hbm, dv_hbm, wk_hbm, wv_hbm, *rest):
    n_slot = dk_hbm.shape[0]
    outs, (dk, dv, wk, wv, acc, dx, sem_in, sem_out) = rest[:n_slot], rest[n_slot:]
    length, width = dk.shape[1:]
    block, half = 256, n_slot // 2
    loads = [pltpu.make_async_copy(a, b, sem_in.at[i]) for i, (a, b) in enumerate(
        ((dk_hbm, dk), (wk_hbm, wk), (dv_hbm, dv), (wv_hbm, wv)))]
    for c in loads:
        c.start()
    stores = [pltpu.make_async_copy(dx.at[t], outs[t], sem_out.at[t]) for t in range(n_slot)]
    for d, w, final in ((dk, wk, False), (dv, wv, True)):
        for c in loads[2 * final:2 * final + 2]:
            c.wait()
        for lo in range(0, n_slot, half):
            rows = d[lo:lo + half].reshape(half * length, width)
            for n in range(0, width, block):
                cols = slice(n, n + block)
                part = mm_nt(rows, w[cols, :]).reshape(half, length, block)
                if final:
                    dx[lo:lo + half, :, cols] = (acc[lo:lo + half, :, cols] + part).astype(BF)
                else:
                    acc[lo:lo + half, :, cols] = part
            if final:
                for c in stores[lo:lo + half]:
                    c.start()
    for c in stores:
        c.wait()


def input_grads(dk, dv, wk, wv):
    n_slot, length, width = dk.shape
    hbm = pl.BlockSpec(memory_space=pltpu.HBM)
    vm = pltpu.VMEM
    return pl.pallas_call(
        input_kernel,
        in_specs=[hbm] * 4,
        out_specs=[hbm] * n_slot,
        out_shape=[jax.ShapeDtypeStruct((length, width), BF)] * n_slot,
        scratch_shapes=[
            vm(dk.shape, BF), vm(dv.shape, BF), vm(wk.shape, BF), vm(wv.shape, BF), vm(dk.shape, F32), vm(dk.shape, BF),
            pltpu.SemaphoreType.DMA((4,)), pltpu.SemaphoreType.DMA((n_slot,)),
        ],
        compiler_params=pltpu.CompilerParams(vmem_limit_bytes=60 * 2**20),
        cost_estimate=pl.CostEstimate(flops=4 * dk.size * width, bytes_accessed=10 * 2**20, transcendentals=0),
        name="input_grads",
    )(dk, dv, wk, wv)


def add_kernel(a_ref, b_ref, out_ref):
    out_ref[...] = (a_ref[...].astype(F32) + b_ref[...].astype(F32)).astype(BF)


def add(a, b):
    count, n, each, width = a.shape
    spec = pl.BlockSpec((count // 4, n, each, width), lambda i: (i, 0, 0, 0))
    return pl.pallas_call(
        add_kernel,
        grid=(4,),
        in_specs=[spec, spec],
        out_specs=spec,
        out_shape=jax.ShapeDtypeStruct(a.shape, BF),
        compiler_params=pltpu.CompilerParams(vmem_limit_bytes=16 * 2**20),
        cost_estimate=pl.CostEstimate(flops=a.size, bytes_accessed=6 * a.size, transcendentals=0),
        name="add",
    )(a, b)


def combine_kernel(me_ref, listed_ref, dq_hbm, wq_hbm, *rest):
    n_slot = len(rest) - 6
    parts, (out_ref, acc, dq_ref, wq_ref, back, sem) = rest[:n_slot], rest[n_slot:]
    length = back.shape[1]
    me = me_ref[0]
    block = 256
    copies = [pltpu.make_async_copy(a, b, sem.at[i]) for i, (a, b) in enumerate(
        [(dq_hbm, dq_ref), (wq_hbm, wq_ref)] + [(p, back.at[s]) for s, p in enumerate(parts)])]
    for c in copies:
        c.start()
    for c in copies:
        c.wait()
    for n in range(0, acc.shape[2], block):
        cols = slice(n, n + block)
        acc[:, :, cols] = mm_nt(dq_ref[...], wq_ref[cols, :]).reshape(acc.shape[0], length, block)
    for s in range(n_slot):
        at = listed_ref[lax.rem(me + n_slot - s, n_slot)]
        acc[at] += back[s].astype(F32)
    out_ref[...] = acc[...].astype(BF)


def combine(me, listed, dq, wq, parts):
    length, width = parts[0].shape
    n_src = dq.shape[0] // length
    smem = pl.BlockSpec(memory_space=pltpu.SMEM)
    hbm = pl.BlockSpec(memory_space=pltpu.HBM)
    return pl.pallas_call(
        combine_kernel,
        in_specs=[smem, smem] + [hbm] * (2 + len(parts)),
        out_specs=pl.BlockSpec(memory_space=pltpu.VMEM),
        out_shape=jax.ShapeDtypeStruct((n_src, length, width), BF),
        scratch_shapes=[
            pltpu.VMEM((n_src, length, width), F32), pltpu.VMEM(dq.shape, BF), pltpu.VMEM(wq.shape, BF),
            pltpu.VMEM((len(parts), length, width), BF), pltpu.SemaphoreType.DMA((2 + len(parts),)),
        ],
        compiler_params=pltpu.CompilerParams(vmem_limit_bytes=60 * 2**20),
        cost_estimate=pl.CostEstimate(flops=2 * dq.size * width, bytes_accessed=6 * 2**20, transcendentals=0),
        name="combine",
    )(me, listed, dq, wq, *parts)


def pick_kernel(listed_ref, x_hbm, out_hbm, x_ref, sem):
    load = pltpu.make_async_copy(x_hbm, x_ref, sem.at[0])
    load.start()
    load.wait()
    n = out_hbm.shape[0]
    stores = [pltpu.make_async_copy(x_ref.at[listed_ref[i]], out_hbm.at[i], sem.at[1 + i]) for i in range(n)]
    for c in stores:
        c.start()
    for c in stores:
        c.wait()


def pick(listed, x):
    n = listed.shape[0]
    hbm = pl.BlockSpec(memory_space=pltpu.HBM)
    return pl.pallas_call(
        pick_kernel,
        in_specs=[pl.BlockSpec(memory_space=pltpu.SMEM), hbm],
        out_specs=hbm,
        out_shape=jax.ShapeDtypeStruct((n,) + x.shape[1:], x.dtype),
        scratch_shapes=[pltpu.VMEM(x.shape, x.dtype), pltpu.SemaphoreType.DMA((1 + n,))],
        compiler_params=pltpu.CompilerParams(vmem_limit_bytes=60 * 2**20),
        name="pick",
    )(listed, x)


def sum_kernel(parts_ref, out_ref):
    out_ref[...] = jnp.sum(parts_ref[...].astype(F32), axis=0).astype(BF)


def sum_parts(parts):
    count, n, each, width = parts.shape
    return pl.pallas_call(
        sum_kernel,
        grid=(n,),
        in_specs=[pl.BlockSpec((count, 1, each, width), lambda i: (0, i, 0, 0))],
        out_specs=pl.BlockSpec((1, each, width), lambda i: (i, 0, 0)),
        out_shape=jax.ShapeDtypeStruct((n, each, width), BF),
        compiler_params=pltpu.CompilerParams(vmem_limit_bytes=16 * 2**20),
        cost_estimate=pl.CostEstimate(flops=parts.size, bytes_accessed=2 * parts.size, transcendentals=0),
        name="sum_parts",
    )(parts)


def spread_kernel(a_ref, b_ref, c_ref, d_ref, out_ref, *, factor):
    a, b, c, d = (ref[...].astype(F32) for ref in (a_ref, b_ref, c_ref, d_ref))
    total = (a + c) + (b + d)
    out_ref[...] = jnp.broadcast_to((total * factor).astype(BF)[None], out_ref.shape)


def spread(parts, copies, factor):
    n, each, width = parts[0].shape
    return pl.pallas_call(
        functools.partial(spread_kernel, factor=factor),
        grid=(n,),
        in_specs=[pl.BlockSpec((1, each, width), lambda i: (i, 0, 0))] * len(parts),
        out_specs=pl.BlockSpec((copies, 1, each, width), lambda i: (0, i, 0, 0)),
        out_shape=jax.ShapeDtypeStruct((copies, n, each, width), BF),
        compiler_params=pltpu.CompilerParams(vmem_limit_bytes=16 * 2**20),
        cost_estimate=pl.CostEstimate(flops=4 * parts[0].size, bytes_accessed=2 * copies * parts[0].size, transcendentals=0),
        name="spread",
    )(*parts)


def place_kernel(half_ref, rows_ref, *rest):
    n = rows_ref.shape[1]
    for i, out in enumerate(rest[-n:]):
        out[0] = rows_ref[:, i]


def place(half, rows, into=()):
    pieces, n, each, width = rows.shape
    step = pieces // 4
    hbm = pl.BlockSpec(memory_space=pl.ANY)
    return pl.pallas_call(
        place_kernel,
        grid_spec=pltpu.PrefetchScalarGridSpec(
            num_scalar_prefetch=1,
            grid=(pieces // step,),
            in_specs=[pl.BlockSpec((step, n, each, width), lambda p, half: (p, 0, 0, 0))] + [hbm] * len(into),
            out_specs=[pl.BlockSpec((1, step, each, width), lambda p, half: (half[0], p, 0, 0))] * n,
        ),
        out_shape=[jax.ShapeDtypeStruct((2, pieces, each, width), BF)] * n,
        input_output_aliases={2 + i: i for i in range(len(into))},
        compiler_params=pltpu.CompilerParams(vmem_limit_bytes=16 * 2**20),
        cost_estimate=pl.CostEstimate(flops=0, bytes_accessed=4 * rows.size, transcendentals=0),
        name="place",
    )(half, rows, *into)


def body(sentences, cotangent, w_query, w_key, w_value, send_rows, pair_src, pair_slot, pair_valid):
    sent_dev, length, width = sentences.shape
    n_lang = lax.axis_size("lang")
    n_pair = lax.axis_size("pair")
    me = lax.axis_index("lang")
    listed = send_rows[0].reshape(-1)
    outgoing = pick(listed, sentences)
    received = lax.all_to_all(outgoing, "lang", split_axis=0, concat_axis=0, tiled=True)
    x = sentences.reshape(-1, width)
    c = cotangent.reshape(-1, width)
    where = me.reshape(1).astype(jnp.int32)
    attended, dq, xk, rk, send, dk, dv = attend(
        where, pair_src, pair_slot, pair_valid, x, received, c, w_query, w_key, w_value, pieces=n_pair
    )
    other_core = [(i, i ^ 1) for i in range(n_lang)]
    other = lax.ppermute(send, "lang", other_core)
    keep = keep_grads(xk, rk, dq, dk, dv, n_pair)
    other, keep = lax.optimization_barrier((other, keep))
    chip, dk, dv = lax.optimization_barrier((add(keep, other), dk, dv))
    dx = input_grads(dk, dv, w_key, w_value)
    back = [dx[0]]
    for s in range(1, n_lang):
        back.append(lax.ppermute(dx[s], "lang", [(i, (i + s) % n_lang) for i in range(n_lang)]))
    pieces = lax.all_to_all(chip, "pair", split_axis=0, concat_axis=0, tiled=True)
    pieces, *back[1:4] = lax.optimization_barrier((pieces, *back[1:4]))
    plane = sum_parts(pieces)
    rings = [plane]
    for y in range(1, n_lang // 2):
        rings.append(lax.ppermute(plane, "lang", [(i, (i + 2 * y) % n_lang) for i in range(n_lang)]))
    factor = 1.0 / (sent_dev * n_lang * n_pair * length) ** 0.5
    near = lax.all_to_all(spread(rings, n_pair, factor), "pair", split_axis=0, concat_axis=0, tiled=True)
    grad_sentences = combine(where, listed, dq, w_query, back)
    near, grad_sentences = lax.optimization_barrier((near, grad_sentences))
    far = lax.ppermute(near, "lang", other_core)
    core = lax.rem(where, 2)
    grads = place(1 - core, far, place(core, near))
    grads = tuple(g.reshape(width, width) for g in grads)
    return (attended.reshape(sentences.shape), grad_sentences) + grads


def solution(mesh):
    split3, split2 = P(("lang", "pair"), None, None), P(("lang", "pair"), None)
    in_specs = (split3, split3, P(), P(), P(), split3, split2, split2, split2)
    out_specs = (split3, split3, P(), P(), P())
    return jax.shard_map(body, mesh=mesh, in_specs=in_specs, out_specs=out_specs, check_vma=False)
```
